128 devices in a mesh: mem: 4 (over x_lo, core), lat: 32 (over x_hi, z, y).
Axes of the slice: x: 4 (x_hi: 2, x_lo: 2; x = x_hi * 2 + x_lo), y: 4, z: 4, core: 2. Of those that a mesh axis runs over, the one named last changes fastest.
Arguments:
- latent: bfloat16 [8, 16384, 1024], P('mem', 'lat'), may hold values from -8 to 8
- member_noise: bfloat16 [8, 1024], P('mem'), may hold values from -3 to 3
- w_qkv: bfloat16 [1024, 3072], replicated, may hold values from -0.28125 to 0.28125
- w_out: bfloat16 [1024, 1024], replicated, may hold values from -0.1875 to 0.1875
- dec_weight: bfloat16 [100, 1024], replicated, may hold values from -0.1875 to 0.1875
- targets: float32 [100, 16384], P(None, 'lat'), may hold values from -6 to 6
- area_weight: float32 [16384], P('lat'), may hold values from 0.1 to 1
- field_weight: float32 [100], replicated, may hold values from 0.2 to 2
- band_count: int32 [32], replicated, may hold values from 192 to 512, as said below
- band_window: int32 [32, 2], P('lat'), may hold values from 128 to 256
Outputs:
- grad_hidden: bfloat16 [8, 16384, 1024], P('mem', 'lat')
- grad_dec_weight: float32 [100, 1024], replicated
- mean_loss: float32 [], replicated
The draws below stay inside these ranges and needn't reach their ends.
Inputs may be any that keep to these rules, and one draw needn't show every extreme that they name: 512 at the first band and at the middle band; the other bands vary and tend to hold fewer the farther they lie from the middle, without falling in order; rows at band_count[b] and above of band b are unused slots.
All inputs are finite; a program needn't handle non-finite values.
Results may differ from the reference program's by a relative error of at most 0.015.
Values may be sent and summed in bfloat16 or wider, within the bound.
No kernel may reach another device: no remote copies, remote signals or barrier semaphores. Data moves between devices by JAX's collectives and lax.ppermute only.
A program may use at most 192 MiB of HBM per device.

```python
import math
import jax
import jax.numpy as jnp
from jax import lax

D = 1024
HEADS = 16
HEAD_DIM = 64
FIELDS = 100
P_DEV = 512
HALO = 256
MEMBERS = 8
BANDS = 32
TOKENS = 16384


def draw_latent(key, part):
    own_key = jax.random.fold_in(key, 31)
    values = jnp.clip(jax.random.normal(own_key, (MEMBERS, TOKENS, D), jnp.float32), -6.0, 6.0)
    return values.astype(jnp.bfloat16)


def draw_w_qkv(key, part):
    own_key = jax.random.fold_in(key, 37)
    weight_part = jnp.clip(jax.random.normal(own_key, (D, 3 * D), jnp.float32), -6.0, 6.0) * D ** (-0.5)
    return weight_part.astype(jnp.bfloat16)


def draw_band_count(key, part):
    key = jax.random.fold_in(key, 11)
    band_index = jnp.arange(BANDS, dtype=jnp.int32)
    distance = jnp.abs(2 * band_index - (BANDS - 1))
    base_count = P_DEV - P_DEV // 2 * distance // (BANDS - 1)
    trimmed = jax.random.randint(key, (BANDS,), 0, P_DEV // 8 + 1, dtype=jnp.int32)
    counts = base_count - trimmed
    counts = jnp.where(band_index == BANDS - 1, P_DEV - P_DEV // 2 - P_DEV // 8, counts)
    counts = jnp.where(band_index == 0, P_DEV, counts)
    counts = jnp.where(band_index == BANDS // 2, P_DEV, counts)
    return counts.astype(jnp.int32)


def draw_band_window(key, part):
    key = jax.random.fold_in(key, 23)
    window_rows = jax.random.randint(key, (BANDS, 2), HALO // 2, HALO + 1, dtype=jnp.int32)
    band_index = jnp.arange(BANDS, dtype=jnp.int32)[:, None]
    window_rows = jnp.where(band_index == 1, HALO, window_rows)
    window_rows = jnp.where(band_index == 2, HALO // 2, window_rows)
    return window_rows.astype(jnp.int32)


def block_levels(stream_key, dims, pieces, smallest, high):
    loudness, own = 1.0, jax.random.fold_in(stream_key, 6)
    for axis_at, parts in pieces:
        draws = jnp.exp(jax.random.uniform(jax.random.fold_in(own, axis_at), (parts,), jnp.float32, smallest / len(pieces), high / len(pieces)))
        loudness = loudness * jnp.repeat(draws, dims[axis_at] // parts).reshape([-1 if axis == axis_at else 1 for axis in range(len(dims))])
    return loudness


def noise(key, extent, spread, most, split=(), kind=jnp.bfloat16):
    factor_of = block_levels(key, extent, split, -0.22, 0.18) if split else 1.0
    array = jax.random.normal(key, extent, jnp.float32) * spread * factor_of
    return jnp.minimum(jnp.maximum(array, -most), most).astype(kind)


def setup_inputs(seed: int = 0) -> dict:
    seeds = jax.random.split(jax.random.key(seed), 11)
    latent = draw_latent(jax.random.fold_in(seeds[10], 71), 0)
    member_noise = noise(seeds[1], (MEMBERS, D), 0.5, 3.0, ((0, 4),))
    w_qkv = draw_w_qkv(jax.random.fold_in(seeds[10], 71), 0)
    w_out = noise(seeds[3], (D, D), D ** -0.5, 0.1875)
    dec_weight = noise(seeds[4], (FIELDS, D), D ** -0.5, 0.1875)
    targets = noise(seeds[5], (FIELDS, TOKENS), 1.0, 6.0, ((1, 32),), jnp.float32)
    area_weight = jnp.clip(jnp.exp(math.log(1.0) - 2.3025851 * jax.random.uniform(seeds[6], (TOKENS,), jnp.float32) ** block_levels(seeds[6], (TOKENS,), ((0, 32),), -0.2, 0.2)), 0.1, 1.0)
    field_weight = jnp.clip(jnp.exp(jax.random.uniform(seeds[7], (FIELDS,), jnp.float32, math.log(0.2), math.log(2.0))), 0.2, 2.0)
    band_count = draw_band_count(jax.random.fold_in(seeds[10], 71), 0)
    band_window = draw_band_window(jax.random.fold_in(seeds[10], 71), 0)
    return dict(latent=latent, member_noise=member_noise, w_qkv=w_qkv, w_out=w_out, dec_weight=dec_weight, targets=targets, area_weight=area_weight, field_weight=field_weight, band_count=band_count, band_window=band_window)


norm_eps = 1e-05
smooth_width = 0.25

def layer_norm(inputs):
    row_mean = lax.optimization_barrier(jnp.mean(inputs, axis=-1, keepdims=True))
    centred = inputs - row_mean
    row_var = lax.optimization_barrier(jnp.mean(centred * centred, axis=-1, keepdims=True))
    inverse = lax.rsqrt(row_var + norm_eps)
    return (centred * inverse, inverse)

def smooth_slope(gap_value):
    return gap_value * lax.rsqrt(gap_value * gap_value + smooth_width * smooth_width)

def smooth_abs(gap_value):
    return jnp.sqrt(gap_value * gap_value + smooth_width * smooth_width)

def crps_part(own_preds, all_preds, target, point_scale):
    ensemble = all_preds.shape[0]
    observed = own_preds - target[None]
    pair_slope = jnp.zeros_like(own_preds)
    pair_abs = jnp.zeros_like(own_preds)
    for k in range(ensemble):
        gap_value = own_preds - all_preds[k][None]
        pair_slope = pair_slope + smooth_slope(gap_value)
        pair_abs = pair_abs + smooth_abs(gap_value)
    gradient = point_scale[None] * (smooth_slope(observed) - pair_slope / (ensemble - 1))
    loss_part = jnp.sum(point_scale[None] * (smooth_abs(observed) - pair_abs / (2 * (ensemble - 1))))
    return (gradient, loss_part)

def reference(latent, member_noise, w_qkv, w_out, dec_weight, targets, area_weight, field_weight, band_count, band_window):
    place = jnp.arange(TOKENS, dtype=jnp.int32)
    band_of = place // P_DEV
    row_of = place - band_of * P_DEV
    valid = row_of < band_count[band_of]
    valid_pad = jnp.pad(valid, (HALO, HALO))
    span_rows = P_DEV + 2 * HALO
    offset = jnp.arange(span_rows, dtype=jnp.int32)[None, :] - HALO - jnp.arange(P_DEV, dtype=jnp.int32)[:, None]

    def member_forward(member_pair):
        member_rows, noise_row = member_pair
        normed_in = layer_norm(member_rows.astype(jnp.float32))[0].astype(jnp.bfloat16)
        projected = jnp.dot(normed_in, w_qkv, preferred_element_type=jnp.float32).astype(jnp.bfloat16)
        queries = projected[:, :D]
        key_pad = jnp.pad(projected[:, D:], ((HALO, HALO), (0, 0)))

        def band_attention(band_index):
            row_start = band_index * P_DEV
            band_queries = lax.dynamic_slice_in_dim(queries, row_start, P_DEV, 0).astype(jnp.float32).reshape(P_DEV, HEADS, HEAD_DIM)
            band_keys = lax.dynamic_slice_in_dim(key_pad, row_start, span_rows, 0).astype(jnp.float32)
            key_part = band_keys[:, :D].reshape(span_rows, HEADS, HEAD_DIM)
            value_part = band_keys[:, D:].reshape(span_rows, HEADS, HEAD_DIM)
            usable = lax.dynamic_slice_in_dim(valid_pad, row_start, span_rows, 0)
            window_row = band_window[band_index]
            allowed = (offset >= -window_row[0]) & (offset <= window_row[1]) & usable[None, :] | (offset == 0)
            scores = jnp.einsum('qhc,khc->hqk', band_queries, key_part) * HEAD_DIM ** (-0.5)
            scores = jnp.where(allowed[None], scores, -1e+30)
            row_max = lax.optimization_barrier(jnp.max(scores, axis=-1, keepdims=True))
            expo = jnp.exp(scores - row_max)
            row_total = lax.optimization_barrier(jnp.sum(expo, axis=-1, keepdims=True))
            attn_weight = (expo / row_total).astype(jnp.bfloat16)
            attended = jnp.einsum('hqk,khc->qhc', attn_weight.astype(jnp.float32), value_part)
            return attended.reshape(P_DEV, D).astype(jnp.bfloat16)
        attended = lax.map(band_attention, jnp.arange(BANDS, dtype=jnp.int32)).reshape(TOKENS, D)
        hidden = member_rows.astype(jnp.float32) + jnp.dot(attended, w_out, preferred_element_type=jnp.float32)
        normalized, inverse = layer_norm(hidden)
        normed_out = (normalized + noise_row.astype(jnp.float32)[None, :]).astype(jnp.bfloat16)
        return (normed_out, normalized, inverse)
    normed_out, normalized, inverse = lax.map(member_forward, (latent, member_noise))
    predicted = jnp.einsum('fd,mtd->mft', dec_weight.astype(jnp.float32), normed_out.astype(jnp.float32))
    point_weight = jnp.where(valid, area_weight, 0.0)
    point_scale = field_weight[:, None] * point_weight[None, :]
    gradient, loss_part = crps_part(predicted, predicted, targets, point_scale)
    grad_pred = gradient.astype(jnp.bfloat16)
    grad_norm = jnp.einsum('mft,fd->mtd', grad_pred.astype(jnp.float32), dec_weight.astype(jnp.float32))
    grad_hidden = inverse * (grad_norm - lax.optimization_barrier(jnp.mean(grad_norm, axis=-1, keepdims=True)) - normalized * lax.optimization_barrier(jnp.mean(grad_norm * normalized, axis=-1, keepdims=True)))
    weight_sum = jnp.einsum('mft,mtd->fd', grad_pred.astype(jnp.float32), normed_out.astype(jnp.float32))
    return (grad_hidden.astype(jnp.bfloat16), weight_sum / TOKENS, loss_part / TOKENS)
```

```python
import functools

import jax
import jax.numpy as jnp
from jax import lax
from jax.experimental import pallas as pl
from jax.experimental.pallas import tpu as pltpu
from jax.sharding import PartitionSpec as P

HEAD_DIM = 64
HALO = 256
LOG2E = 1.4426950408889634

norm_eps = 1e-05
smooth_width = 0.25
F32 = jnp.float32
BF16 = jnp.bfloat16
MIB = 1024 * 1024


def normalize(x):
    mean = jnp.mean(x, axis=-1, keepdims=True)
    centred = x - mean
    var = jnp.mean(centred * centred, axis=-1, keepdims=True)
    inverse = lax.rsqrt(var + norm_eps)
    return centred * inverse, inverse


def nt_dot(a, b):
    return lax.dot_general(a, b, (((1,), (1,)), ((), ())), preferred_element_type=F32)


def tn_dot(a, b):
    return lax.dot_general(a, b, (((0,), (0,)), ((), ())), preferred_element_type=F32)


def nn_dot(a, b):
    return jnp.dot(a, b, preferred_element_type=F32)


def project_body(latent_ref, w_ref, out_ref, normed_ref):
    step = pl.program_id(0)

    @pl.when(step == 0)
    def _():
        normed_ref[...] = normalize(latent_ref[...].astype(F32))[0].astype(BF16)

    scale = jnp.where(step == 0, HEAD_DIM ** (-0.5) * LOG2E, 1.0)
    out_ref[...] = (nn_dot(normed_ref[...], w_ref[...]) * scale).astype(BF16)


def project(latent, w_qkv):
    rows, width = latent.shape
    return pl.pallas_call(
        project_body,
        grid=(3,),
        in_specs=[
            pl.BlockSpec((rows, width), lambda s: (0, 0)),
            pl.BlockSpec((width, width), lambda s: (0, s)),
        ],
        out_specs=pl.BlockSpec((rows, width), lambda s: (0, s)),
        out_shape=jax.ShapeDtypeStruct((rows, 3 * width), BF16),
        scratch_shapes=[pltpu.VMEM((rows, width), BF16)],
        compiler_params=pltpu.CompilerParams(vmem_limit_bytes=48 * MIB),
        cost_estimate=pl.CostEstimate(
            flops=2 * rows * width * 3 * width, bytes_accessed=14 * MIB, transcendentals=0
        ),
        name="project",
    )(latent, w_qkv)


QB = 128
STEP_COLS = 256
PAIR = 2 * HEAD_DIM


def attend_body(
    info_ref,
    q_ref,
    k_ref,
    v_ref,
    before_ref,
    after_ref,
    wk_ref,
    wv_ref,
    latent_ref,
    wout_ref,
    noise_ref,
    dec_ref,
    normalized_ref,
    inverse_ref,
    normed_out_ref,
    predicted_ref,
    halo_ref,
    kx_ref,
    vx_ref,
    bias_ref,
    att_ref,
):
    step = pl.program_id(0)
    steps = pl.num_programs(0)
    rows = q_ref.shape[0]
    span = QB + 2 * HALO

    @pl.when(step == 0)
    def _():
        halo_ref[:HALO] = normalize(before_ref[...].astype(F32))[0].astype(BF16)
        halo_ref[HALO:] = normalize(after_ref[...].astype(F32))[0].astype(BF16)
        reach_low, reach_high = info_ref[0], info_ref[1]
        low_end, mid_end, high_end = info_ref[2], info_ref[3], info_ref[4]
        for block in range(rows // QB):
            q_row = lax.broadcasted_iota(jnp.int32, (QB, span), 0) + block * QB
            k_row = lax.broadcasted_iota(jnp.int32, (QB, span), 1) + block * QB - HALO
            offset = k_row - q_row
            in_window = (offset >= -reach_low) & (offset <= reach_high)
            end = jnp.where(
                k_row < 0, low_end - rows, jnp.where(k_row < rows, mid_end, high_end + rows)
            )
            allowed = (in_window & (k_row < end)) | (offset == 0)
            bias_ref[block] = jnp.where(allowed, 0.0, -1e30)

    halo = halo_ref[...]
    k_halo = nn_dot(halo, wk_ref[...]).astype(BF16)
    v_halo = nn_dot(halo, wv_ref[...]).astype(BF16)
    kx_ref[:HALO] = k_halo[:HALO]
    kx_ref[HALO : HALO + rows] = k_ref[...]
    kx_ref[HALO + rows :] = k_halo[HALO:]
    low = lax.broadcasted_iota(jnp.int32, (1, PAIR), 1) < HEAD_DIM
    ext = rows + 2 * HALO
    for pair in range(STEP_COLS // PAIR):
        cols = slice(pair * PAIR, (pair + 1) * PAIR)
        v_all = jnp.concatenate([v_halo[:HALO, cols], v_ref[:, cols], v_halo[HALO:, cols]], axis=0)
        zero = jnp.zeros_like(v_all)
        one = jnp.ones_like(v_all)
        vx_ref[2 * pair, :, :PAIR] = jnp.where(low, v_all, zero)
        vx_ref[2 * pair, :, PAIR:] = jnp.where(low, one, zero)
        vx_ref[2 * pair + 1, :, :PAIR] = jnp.where(low, zero, v_all)
        vx_ref[2 * pair + 1, :, PAIR:] = jnp.where(low, zero, one)
    for pair in range(STEP_COLS // PAIR):
        cols = slice(pair * PAIR, (pair + 1) * PAIR)
        for block in range(rows // QB):
            q = q_ref[block * QB : (block + 1) * QB, cols]
            keys = kx_ref[block * QB : block * QB + span, cols]
            bias = bias_ref[block]
            total = None
            for half in range(2):
                q_half = jnp.where(low if half == 0 else ~low, q, jnp.zeros_like(q))
                scores = nt_dot(q_half, keys) + bias
                top = jnp.max(scores, axis=-1, keepdims=True)
                weight = jnp.exp2(scores - top).astype(BF16)
                values = vx_ref[2 * pair + half, block * QB : block * QB + span, :]
                part = nn_dot(weight, values)
                total = part if total is None else total + part
            att_ref[step, block * QB : (block + 1) * QB, cols] = (
                total[:, :PAIR] / total[:, PAIR:]
            ).astype(BF16)

    @pl.when(step == steps - 1)
    def _():
        hidden = latent_ref[...].astype(F32)
        for s in range(att_ref.shape[0]):
            hidden = hidden + nn_dot(
                att_ref[s], wout_ref[s * STEP_COLS : (s + 1) * STEP_COLS, :]
            )
        normalized, inverse = normalize(hidden)
        normalized_ref[...] = normalized.astype(BF16)
        inverse_ref[...] = jnp.broadcast_to(inverse, inverse_ref.shape)
        normed_out = (normalized + noise_ref[...].astype(F32)).astype(BF16)
        normed_out_ref[...] = normed_out
        predicted_ref[...] = nt_dot(dec_ref[...], normed_out).astype(BF16)


def attend(info, member, projected, before, after, w_qkv, latent, w_out, noise, dec):
    rows, width = latent.shape[1:]
    fields = dec.shape[0]
    steps = width // STEP_COLS
    whole = lambda s: (0, 0)
    return pl.pallas_call(
        attend_body,
        grid=(steps,),
        in_specs=[
            pl.BlockSpec(memory_space=pltpu.SMEM),
            pl.BlockSpec((rows, STEP_COLS), lambda s: (member, s)),
            pl.BlockSpec((rows, STEP_COLS), lambda s: (member, steps + s)),
            pl.BlockSpec((rows, STEP_COLS), lambda s: (member, 2 * steps + s)),
            pl.BlockSpec((HALO, width), whole),
            pl.BlockSpec((HALO, width), whole),
            pl.BlockSpec((width, STEP_COLS), lambda s: (0, steps + s)),
            pl.BlockSpec((width, STEP_COLS), lambda s: (0, 2 * steps + s)),
            pl.BlockSpec((None, rows, width), lambda s: (member, 0, 0)),
            pl.BlockSpec((width, width), whole),
            pl.BlockSpec((None, 1, width), lambda s: (member, 0, 0)),
            pl.BlockSpec((fields, width), whole),
        ],
        out_specs=[
            pl.BlockSpec((rows, width), whole),
            pl.BlockSpec((rows, 128), whole),
            pl.BlockSpec((rows, width), whole),
            pl.BlockSpec((fields, rows), whole),
        ],
        out_shape=[
            jax.ShapeDtypeStruct((rows, width), BF16),
            jax.ShapeDtypeStruct((rows, 128), F32),
            jax.ShapeDtypeStruct((rows, width), BF16),
            jax.ShapeDtypeStruct((fields, rows), BF16),
        ],
        scratch_shapes=[
            pltpu.VMEM((2 * HALO, width), BF16),
            pltpu.VMEM((rows + 2 * HALO, STEP_COLS), BF16),
            pltpu.VMEM((2 * STEP_COLS // PAIR, rows + 2 * HALO, 2 * PAIR), BF16),
            pltpu.VMEM((rows // QB, QB, QB + 2 * HALO), F32),
            pltpu.VMEM((steps, rows, STEP_COLS), BF16),
        ],
        compiler_params=pltpu.CompilerParams(vmem_limit_bytes=56 * MIB),
        cost_estimate=pl.CostEstimate(
            flops=8 * 10**9, bytes_accessed=14 * MIB, transcendentals=10**7
        ),
        name="attend",
    )(info, projected, projected, projected, before, after, w_qkv, w_qkv, latent, w_out, noise, dec)


def crps_body(member_ref, pred_ref, target_ref, fw_ref, aw_ref, normed_ref, grad_ref, weight_ref, loss_ref):
    first = member_ref[0]
    count = member_ref[1]
    ensemble = pred_ref.shape[0] * pred_ref.shape[1]
    own_count = pred_ref.shape[1]
    lead = 1.0 / (ensemble - 1)
    fields, rows = target_ref.shape
    target = target_ref[...]
    used = lax.broadcasted_iota(jnp.int32, (1, rows), 1) < count
    scale = fw_ref[...] * jnp.where(used, aw_ref[...], 0.0)

    def slope(gap):
        square = gap * gap + smooth_width * smooth_width
        root = lax.rsqrt(square)
        return gap * root, square * root

    loss = jnp.zeros((fields, rows), F32)
    weight = None
    for own in range(own_count):
        mine = pred_ref[first, own].astype(F32)
        pair_slope = jnp.zeros((fields, rows), F32)
        pair_abs = jnp.zeros((fields, rows), F32)
        for other in range(ensemble):
            s, a = slope(mine - pred_ref[other // own_count, other % own_count].astype(F32))
            pair_slope = pair_slope + s
            pair_abs = pair_abs + a
        s, a = slope(mine - target)
        grad = (scale * (s - pair_slope * lead)).astype(BF16)
        grad_ref[own] = grad
        loss = loss + scale * (a - pair_abs * (0.5 * lead))
        part = nn_dot(grad, normed_ref[own])
        weight = part if weight is None else weight + part
    weight_ref[...] = weight
    loss_ref[...] = jnp.broadcast_to(
        jnp.sum(jnp.sum(loss, axis=0, keepdims=True), axis=1, keepdims=True), loss_ref.shape
    )


def crps(info, preds, targets, field_weight, area_weight, normed_out):
    _, own_count, fields, rows = preds.shape
    width = normed_out.shape[-1]
    vmem = pl.BlockSpec(memory_space=pltpu.VMEM)
    return pl.pallas_call(
        crps_body,
        in_specs=[pl.BlockSpec(memory_space=pltpu.SMEM)] + [vmem] * 5,
        out_specs=[vmem] * 3,
        out_shape=[
            jax.ShapeDtypeStruct((own_count, fields, rows), BF16),
            jax.ShapeDtypeStruct((fields, width), F32),
            jax.ShapeDtypeStruct((8, 128), F32),
        ],
        compiler_params=pltpu.CompilerParams(vmem_limit_bytes=48 * MIB),
        cost_estimate=pl.CostEstimate(
            flops=4 * 10**8, bytes_accessed=4 * MIB, transcendentals=10**6
        ),
        name="crps",
    )(info, preds, targets, field_weight, area_weight, normed_out)


def backward_body(grad_ref, dec_ref, normalized_ref, inverse_ref, out_ref):
    grad_norm = tn_dot(grad_ref[...], dec_ref[...])
    normalized = normalized_ref[...].astype(F32)
    inverse = inverse_ref[...][:, :1]
    mean = jnp.mean(grad_norm, axis=-1, keepdims=True)
    dotted = jnp.mean(grad_norm * normalized, axis=-1, keepdims=True)
    out_ref[...] = (inverse * (grad_norm - mean - normalized * dotted)).astype(BF16)


def backward(grad, dec, normalized, inverse):
    members, fields, rows = grad.shape
    width = dec.shape[1]
    return pl.pallas_call(
        backward_body,
        grid=(members,),
        in_specs=[
            pl.BlockSpec((None, fields, rows), lambda m: (m, 0, 0)),
            pl.BlockSpec((fields, width), lambda m: (0, 0)),
            pl.BlockSpec((None, rows, width), lambda m: (m, 0, 0)),
            pl.BlockSpec((None, rows, 128), lambda m: (m, 0, 0)),
        ],
        out_specs=pl.BlockSpec((None, rows, width), lambda m: (m, 0, 0)),
        out_shape=jax.ShapeDtypeStruct((members, rows, width), BF16),
        compiler_params=pltpu.CompilerParams(vmem_limit_bytes=48 * MIB),
        cost_estimate=pl.CostEstimate(
            flops=5 * 10**8, bytes_accessed=5 * MIB, transcendentals=0
        ),
        name="backward",
    )(grad, dec, normalized, inverse)


def summed(part):
    axes = ("mem", "lat")
    peers = lax.axis_size("mem") * lax.axis_size("lat")
    pieces = part.reshape(peers, -1, 128)
    mine = lax.all_to_all(pieces, axes, split_axis=0, concat_axis=0, tiled=True)
    mine = jnp.sum(mine, axis=0, keepdims=True)
    spread = jnp.broadcast_to(mine, pieces.shape)
    whole = lax.all_to_all(spread, axes, split_axis=0, concat_axis=0, tiled=True)
    return whole.reshape(part.shape)


def local(
    latent,
    member_noise,
    w_qkv,
    w_out,
    dec_weight,
    targets,
    area_weight,
    field_weight,
    band_count,
    band_window,
):
    members, rows, width = latent.shape
    band = lax.axis_index("lat")
    bands = lax.axis_size("lat")
    fields = dec_weight.shape[0]
    padded = -(-fields // 16) * 16
    up = [(i, i + 1) for i in range(bands - 1)]
    down = [(j, i) for i, j in up]
    halos = []
    for member in range(members):
        before = lax.ppermute(latent[member, rows - HALO :], "lat", up)
        after = lax.ppermute(latent[member, :HALO], "lat", down)
        halos.append((before, after))
    projected = project(latent.reshape(members * rows, width), w_qkv)
    counts = jnp.pad(band_count, (1, 1))
    around = lax.dynamic_slice_in_dim(counts, band, 3)
    info = jnp.concatenate([band_window[0], around])
    dec = jnp.pad(dec_weight, ((0, padded - fields), (0, 0)))
    noise = member_noise[:, None, :]
    outs = [
        attend(info, m, projected, *halos[m], w_qkv, latent, w_out, noise, dec)
        for m in range(members)
    ]
    normalized, inverse, normed_out, predicted = (jnp.stack(x) for x in zip(*outs, strict=True))
    preds = lax.all_gather(predicted, "mem", axis=0)
    crps_info = jnp.stack([lax.axis_index("mem"), around[1]])
    grad, weight_part, loss_part = crps(
        crps_info,
        preds,
        jnp.pad(targets, ((0, padded - fields), (0, 0))),
        jnp.pad(field_weight, (0, padded - fields))[:, None],
        area_weight[None, :],
        normed_out,
    )
    packed = jnp.concatenate([weight_part[:fields].reshape(-1, 128), loss_part], axis=0)
    peers = lax.axis_size("mem") * bands
    total = summed(jnp.pad(packed, ((0, -packed.shape[0] % peers), (0, 0))))
    grad_hidden = backward(grad, dec, normalized, inverse)
    tokens = rows * bands
    weight_sum = total[: fields * width // 128].reshape(fields, width)
    return (
        grad_hidden,
        weight_sum / tokens,
        total[fields * width // 128, 0] / tokens,
    )


def solution(mesh):
    return jax.shard_map(
        local,
        mesh=mesh,
        in_specs=(
            P("mem", "lat", None),
            P("mem", None),
            P(),
            P(),
            P(),
            P(None, "lat"),
            P("lat"),
            P(),
            P(),
            P("lat", None),
        ),
        out_specs=(P("mem", "lat", None), P(), P()),
        check_vma=False,
    )
```

```python
import jax
import jax.numpy as jnp
from jax import lax
from jax.experimental import pallas as pl
from jax.experimental.pallas import tpu as pltpu
from jax.sharding import PartitionSpec as P

HEAD_DIM = 64
HALO = 256
LOG2E = 1.4426950408889634

norm_eps = 1e-05
smooth_width = 0.25
F32 = jnp.float32
BF16 = jnp.bfloat16
MIB = 1024 * 1024


def normalize(x):
    mean = jnp.mean(x, axis=-1, keepdims=True)
    centred = x - mean
    var = jnp.mean(centred * centred, axis=-1, keepdims=True)
    inverse = lax.rsqrt(var + norm_eps)
    return centred * inverse, inverse


def nt_dot(a, b):
    return lax.dot_general(a, b, (((1,), (1,)), ((), ())), preferred_element_type=F32)


def tn_dot(a, b):
    return lax.dot_general(a, b, (((0,), (0,)), ((), ())), preferred_element_type=F32)


def nn_dot(a, b):
    return jnp.dot(a, b, preferred_element_type=F32)


QB = 256
STEP_COLS = 256
PAIR = 2 * HEAD_DIM
NEVER = -1e30


def bias_of(q_row, k_row, info_ref, rows):
    offset = k_row - q_row
    in_window = (offset >= -info_ref[0]) & (offset <= info_ref[1])
    end = jnp.where(
        k_row < 0, info_ref[2] - rows, jnp.where(k_row < rows, info_ref[3], info_ref[4] + rows)
    )
    return jnp.where((in_window & (k_row < end)) | (offset == 0), 0.0, NEVER)


def iota(shape, axis):
    return lax.broadcasted_iota(jnp.int32, shape, axis)


def with_ones(values, low):
    zero, one = jnp.zeros_like(values), jnp.ones_like(values)
    first = jnp.concatenate([jnp.where(low, values, zero), jnp.where(low, one, zero)], axis=1)
    second = jnp.concatenate([jnp.where(low, zero, values), jnp.where(low, zero, one)], axis=1)
    return first, second


def near_body(
    info_ref, latent_ref, wq_ref, wk_ref, wv_ref, q_ref, o_ref, lse_ref, normed_ref, bias_ref, k_ref, vx_ref
):
    step = pl.program_id(0)
    rows = bias_ref.shape[0]
    members = latent_ref.shape[0] // rows

    @pl.when(step == 0)
    def _():
        normed_ref[...] = normalize(latent_ref[...].astype(F32))[0].astype(BF16)
        shape = bias_ref.shape
        bias_ref[...] = bias_of(iota(shape, 0), iota(shape, 1), info_ref, rows)

    low = iota((1, PAIR), 1) < HEAD_DIM
    for member in range(members):
        span = slice(member * rows, (member + 1) * rows)
        normed = normed_ref[span]
        q_ref[span] = (nn_dot(normed, wq_ref[...]) * (HEAD_DIM ** (-0.5) * LOG2E)).astype(BF16)
        k_ref[span] = nn_dot(normed, wk_ref[...]).astype(BF16)
        values = nn_dot(normed, wv_ref[...]).astype(BF16)
        for pair in range(STEP_COLS // PAIR):
            cols = slice(pair * PAIR, (pair + 1) * PAIR)
            vx_ref[2 * pair, span], vx_ref[2 * pair + 1, span] = with_ones(values[:, cols], low)
        for pair in range(STEP_COLS // PAIR):
            cols = slice(pair * PAIR, (pair + 1) * PAIR)
            for block in range(rows // QB):
                here = slice(block * QB, (block + 1) * QB)
                mine = slice(member * rows + block * QB, member * rows + (block + 1) * QB)
                first = max(block * QB - HALO, 0)
                last = min((block + 1) * QB + HALO, rows)
                reach = slice(member * rows + first, member * rows + last)
                q = q_ref[mine, cols]
                tops = []
                total = None
                for half in range(2):
                    q_half = jnp.where(low if half == 0 else ~low, q, jnp.zeros_like(q))
                    scores = nt_dot(q_half, k_ref[reach, cols]) + bias_ref[here, first:last]
                    top = jnp.max(scores, axis=-1, keepdims=True)
                    weight = jnp.exp2(scores - top).astype(BF16)
                    part = nn_dot(weight, vx_ref[2 * pair + half, reach])
                    total = part if total is None else total + part
                    tops.append(top)
                summed_weight = total[:, PAIR:]
                o_ref[mine, cols] = (total[:, :PAIR] / summed_weight).astype(BF16)
                lse_ref[mine, cols] = jnp.where(low, tops[0], tops[1]) + jnp.log2(summed_weight)


def near(info, latent, w_qkv):
    members, rows, width = latent.shape
    tall = members * rows
    steps = width // STEP_COLS
    block = pl.BlockSpec((tall, STEP_COLS), lambda s: (0, s))
    return pl.pallas_call(
        near_body,
        grid=(steps,),
        in_specs=[
            pl.BlockSpec(memory_space=pltpu.SMEM),
            pl.BlockSpec((tall, width), lambda s: (0, 0), pipeline_mode=pl.Buffered(1)),
            pl.BlockSpec((width, STEP_COLS), lambda s: (0, s)),
            pl.BlockSpec((width, STEP_COLS), lambda s: (0, steps + s)),
            pl.BlockSpec((width, STEP_COLS), lambda s: (0, 2 * steps + s)),
        ],
        out_specs=[block, block, block],
        out_shape=[
            jax.ShapeDtypeStruct((tall, width), BF16),
            jax.ShapeDtypeStruct((tall, width), BF16),
            jax.ShapeDtypeStruct((tall, width), F32),
        ],
        scratch_shapes=[
            pltpu.VMEM((tall, width), BF16),
            pltpu.VMEM((rows, rows), F32),
            pltpu.VMEM((tall, STEP_COLS), BF16),
            pltpu.VMEM((STEP_COLS // HEAD_DIM, tall, 2 * PAIR), BF16),
        ],
        compiler_params=pltpu.CompilerParams(vmem_limit_bytes=40 * MIB),
        cost_estimate=pl.CostEstimate(
            flops=20 * 10**9, bytes_accessed=16 * MIB, transcendentals=10**7
        ),
        name="near",
    )(info, latent.reshape(tall, width), w_qkv, w_qkv, w_qkv)


def far_body(
    info_ref,
    q_ref,
    o_ref,
    lse_ref,
    before_ref,
    after_ref,
    wk_ref,
    wv_ref,
    noise_ref,
    dec_ref,
    latent_hbm,
    wout_hbm,
    normalized_ref,
    inverse_ref,
    normed_out_ref,
    predicted_ref,
    halo_ref,
    bias_ref,
    k_ref,
    vx_ref,
    att_ref,
    latent_ref,
    wout_ref,
    sem,
):
    step = pl.program_id(0)
    members, _, width = before_ref.shape
    tall = q_ref.shape[0]
    rows = tall // members
    late = [
        pltpu.make_async_copy(latent_hbm, latent_ref, sem.at[0]),
        pltpu.make_async_copy(wout_hbm, wout_ref, sem.at[1]),
    ]

    @pl.when(step == 0)
    def _():
        for copy in late:
            copy.start()
        for member in range(members):
            for side, source in enumerate((before_ref, after_ref)):
                at = (2 * member + side) * HALO
                halo_ref[at : at + HALO] = normalize(source[member].astype(F32))[0].astype(BF16)
        shape = (HALO, HALO)
        bias_ref[0] = bias_of(iota(shape, 0), iota(shape, 1) - HALO, info_ref, rows)
        bias_ref[1] = bias_of(iota(shape, 0) + rows - HALO, iota(shape, 1) + rows, info_ref, rows)

    low = iota((1, PAIR), 1) < HEAD_DIM
    k_ref[...] = nn_dot(halo_ref[...], wk_ref[...]).astype(BF16)
    values = nn_dot(halo_ref[...], wv_ref[...]).astype(BF16)
    for pair in range(STEP_COLS // PAIR):
        cols = slice(pair * PAIR, (pair + 1) * PAIR)
        vx_ref[2 * pair], vx_ref[2 * pair + 1] = with_ones(values[:, cols], low)
    for member in range(members):
        for pair in range(STEP_COLS // PAIR):
            cols = slice(pair * PAIR, (pair + 1) * PAIR)
            out_cols = pl.ds(pl.multiple_of(step * STEP_COLS + pair * PAIR, PAIR), PAIR)
            for side in range(2):
                at = member * rows + side * (rows - HALO)
                mine = slice(at, at + HALO)
                reach = slice((2 * member + side) * HALO, (2 * member + side + 1) * HALO)
                q = q_ref[mine, cols]
                lse = lse_ref[mine, cols]
                tops = []
                total = None
                for half in range(2):
                    q_half = jnp.where(low if half == 0 else ~low, q, jnp.zeros_like(q))
                    scores = nt_dot(q_half, k_ref[reach, cols]) + bias_ref[side]
                    top = jnp.max(scores, axis=-1, keepdims=True)
                    weight = jnp.exp2(scores - top).astype(BF16)
                    part = nn_dot(weight, vx_ref[2 * pair + half, reach])
                    total = part if total is None else total + part
                    tops.append(top)
                far_top = jnp.where(low, tops[0], tops[1])
                top = jnp.maximum(lse, far_top)
                near_share, far_share = jnp.exp2(lse - top), jnp.exp2(far_top - top)
                att_ref[mine, out_cols] = (
                    (near_share * o_ref[mine, cols].astype(F32) + far_share * total[:, :PAIR])
                    / (near_share + far_share * total[:, PAIR:])
                ).astype(BF16)

    @pl.when(step == pl.num_programs(0) - 1)
    def _():
        for copy in late:
            copy.wait()
        for member in range(members):
            span = slice(member * rows, (member + 1) * rows)
            hidden = latent_ref[member].astype(F32) + nn_dot(att_ref[span], wout_ref[...])
            normalized, inverse = normalize(hidden)
            normalized_ref[member] = normalized.astype(BF16)
            inverse_ref[member] = jnp.broadcast_to(inverse, inverse_ref.shape[1:])
            normed_out = (normalized + noise_ref[member].astype(F32)).astype(BF16)
            normed_out_ref[member] = normed_out
            predicted_ref[member] = nt_dot(dec_ref[...], normed_out).astype(BF16)


def far(info, q, o, lse, before, after, w_qkv, noise, dec, latent, w_out):
    members, rows, width = latent.shape
    tall = members * rows
    fields = dec.shape[0]
    steps = width // STEP_COLS
    block = pl.BlockSpec((tall, STEP_COLS), lambda s: (0, s))
    whole2 = lambda s: (0, 0)
    whole3 = lambda s: (0, 0, 0)
    once = pl.Buffered(1)
    anywhere = pl.BlockSpec(memory_space=pl.ANY)
    return pl.pallas_call(
        far_body,
        grid=(steps,),
        in_specs=[
            pl.BlockSpec(memory_space=pltpu.SMEM),
            block,
            block,
            block,
            pl.BlockSpec((members, HALO, width), whole3, pipeline_mode=once),
            pl.BlockSpec((members, HALO, width), whole3, pipeline_mode=once),
            pl.BlockSpec((width, STEP_COLS), lambda s: (0, steps + s)),
            pl.BlockSpec((width, STEP_COLS), lambda s: (0, 2 * steps + s)),
            pl.BlockSpec((members, 1, width), whole3),
            pl.BlockSpec((fields, width), whole2),
            anywhere,
            anywhere,
        ],
        out_specs=[
            pl.BlockSpec((members, rows, width), whole3),
            pl.BlockSpec((members, rows, 128), whole3),
            pl.BlockSpec((members, rows, width), whole3),
            pl.BlockSpec((members, fields, rows), whole3),
        ],
        out_shape=[
            jax.ShapeDtypeStruct((members, rows, width), BF16),
            jax.ShapeDtypeStruct((members, rows, 128), F32),
            jax.ShapeDtypeStruct((members, rows, width), BF16),
            jax.ShapeDtypeStruct((members, fields, rows), BF16),
        ],
        scratch_shapes=[
            pltpu.VMEM((members * 2 * HALO, width), BF16),
            pltpu.VMEM((2, HALO, HALO), F32),
            pltpu.VMEM((members * 2 * HALO, STEP_COLS), BF16),
            pltpu.VMEM((STEP_COLS // HEAD_DIM, members * 2 * HALO, 2 * PAIR), BF16),
            pltpu.VMEM((tall, width), BF16),
            pltpu.VMEM((members, rows, width), BF16),
            pltpu.VMEM((width, width), BF16),
            pltpu.SemaphoreType.DMA((2,)),
        ],
        compiler_params=pltpu.CompilerParams(vmem_limit_bytes=48 * MIB),
        cost_estimate=pl.CostEstimate(
            flops=15 * 10**9, bytes_accessed=22 * MIB, transcendentals=10**7
        ),
        name="far",
    )(info, q, o, lse, before, after, w_qkv, w_qkv, noise, dec, latent, w_out)


def crps_body(member_ref, pred_ref, target_ref, fw_ref, aw_ref, normed_ref, grad_ref, pieces_ref):
    first = member_ref[0]
    count = member_ref[1]
    ensemble = pred_ref.shape[0] * pred_ref.shape[1]
    own_count = pred_ref.shape[1]
    lead = 1.0 / (ensemble - 1)
    fields, rows = target_ref.shape
    width = normed_ref.shape[-1]
    target = target_ref[...]
    used = lax.broadcasted_iota(jnp.int32, (1, rows), 1) < count
    scale = fw_ref[...] * jnp.where(used, aw_ref[...], 0.0)

    def slope(gap):
        square = gap * gap + smooth_width * smooth_width
        root = lax.rsqrt(square)
        return gap * root, square * root

    loss = jnp.zeros((fields, rows), F32)
    weight = None
    for own in range(own_count):
        mine = pred_ref[first, own].astype(F32)
        pair_slope = jnp.zeros((fields, rows), F32)
        pair_abs = jnp.zeros((fields, rows), F32)
        for other in range(ensemble):
            s, a = slope(mine - pred_ref[other // own_count, other % own_count].astype(F32))
            pair_slope = pair_slope + s
            pair_abs = pair_abs + a
        s, a = slope(mine - target)
        grad = (scale * (s - pair_slope * lead)).astype(BF16)
        grad_ref[own] = grad
        loss = loss + scale * (a - pair_abs * (0.5 * lead))
        part = nn_dot(grad, normed_ref[own])
        weight = part if weight is None else weight + part
    tiles = width // 128
    for r in range(fields // 8):
        for c in range(tiles):
            pieces_ref[r * tiles + c] = weight[r * 8 : r * 8 + 8, c * 128 : c * 128 + 128].astype(BF16)
    used_pieces = fields // 8 * tiles
    whole = jnp.sum(jnp.sum(loss, axis=0, keepdims=True), axis=1, keepdims=True)
    high = whole.astype(BF16)
    rest = (whole - high.astype(F32)).astype(BF16)
    row = lax.broadcasted_iota(jnp.int32, (8, 128), 0)
    both = jnp.where(row == 0, high.astype(F32), jnp.where(row == 1, rest.astype(F32), 0.0))
    pieces_ref[used_pieces] = both.astype(BF16)
    pieces_ref[used_pieces + 1 :] = jnp.zeros_like(pieces_ref[used_pieces + 1 :])


def crps(info, preds, targets, field_weight, area_weight, normed_out, peers):
    _, own_count, fields, rows = preds.shape
    vmem = pl.BlockSpec(memory_space=pltpu.VMEM)
    return pl.pallas_call(
        crps_body,
        in_specs=[pl.BlockSpec(memory_space=pltpu.SMEM)] + [vmem] * 5,
        out_specs=[vmem] * 2,
        out_shape=[
            jax.ShapeDtypeStruct((own_count, fields, rows), BF16),
            jax.ShapeDtypeStruct((peers, 8, 128), BF16),
        ],
        compiler_params=pltpu.CompilerParams(vmem_limit_bytes=48 * MIB),
        cost_estimate=pl.CostEstimate(
            flops=4 * 10**8, bytes_accessed=4 * MIB, transcendentals=10**6
        ),
        name="crps",
    )(info, preds, targets, field_weight, area_weight, normed_out)


def backward_body(grad_ref, dec_ref, normalized_ref, inverse_ref, out_ref):
    grad_norm = tn_dot(grad_ref[...], dec_ref[...])
    normalized = normalized_ref[...].astype(F32)
    inverse = inverse_ref[...][:, :1]
    mean = jnp.mean(grad_norm, axis=-1, keepdims=True)
    dotted = jnp.mean(grad_norm * normalized, axis=-1, keepdims=True)
    out_ref[...] = (inverse * (grad_norm - mean - normalized * dotted)).astype(BF16)


def backward(grad, dec, normalized, inverse):
    members, fields, rows = grad.shape
    width = dec.shape[1]
    return pl.pallas_call(
        backward_body,
        grid=(members,),
        in_specs=[
            pl.BlockSpec((None, fields, rows), lambda m: (m, 0, 0)),
            pl.BlockSpec((fields, width), lambda m: (0, 0)),
            pl.BlockSpec((None, rows, width), lambda m: (m, 0, 0)),
            pl.BlockSpec((None, rows, 128), lambda m: (m, 0, 0)),
        ],
        out_specs=pl.BlockSpec((None, rows, width), lambda m: (m, 0, 0)),
        out_shape=jax.ShapeDtypeStruct((members, rows, width), BF16),
        compiler_params=pltpu.CompilerParams(vmem_limit_bytes=48 * MIB),
        cost_estimate=pl.CostEstimate(
            flops=5 * 10**8, bytes_accessed=5 * MIB, transcendentals=0
        ),
        name="backward",
    )(grad, dec, normalized, inverse)


def summed(pieces, loss_piece):
    axes = ("mem", "lat")
    parts = lax.all_to_all(pieces, axes, split_axis=0, concat_axis=0, tiled=True)
    mine = jnp.sum(parts.astype(F32), axis=0)
    loss = mine[0] + mine[1]
    rounded = lax.reduce_precision(loss, 8, 7)
    row = lax.broadcasted_iota(jnp.int32, mine.shape, 0)
    as_loss = jnp.where(row == 0, rounded, jnp.where(row == 1, loss - rounded, 0.0))
    mine = jnp.where(lax.axis_index(axes) == loss_piece, as_loss, mine).astype(BF16)
    spread = jnp.broadcast_to(mine[None], pieces.shape)
    return lax.all_to_all(spread, axes, split_axis=0, concat_axis=0, tiled=True)


def local(
    latent,
    member_noise,
    w_qkv,
    w_out,
    dec_weight,
    targets,
    area_weight,
    field_weight,
    band_count,
    band_window,
):
    members, rows, width = latent.shape
    band = lax.axis_index("lat")
    bands = lax.axis_size("lat")
    fields = dec_weight.shape[0]
    padded = -(-fields // 16) * 16
    up = [(i, i + 1) for i in range(bands - 1)]
    down = [(j, i) for i, j in up]
    before = lax.ppermute(latent[:, rows - HALO :], "lat", up)
    after = lax.ppermute(latent[:, :HALO], "lat", down)
    counts = jnp.pad(band_count, (1, 1))
    around = lax.dynamic_slice_in_dim(counts, band, 3)
    info = jnp.concatenate([band_window[0], around])
    dec = jnp.pad(dec_weight, ((0, padded - fields), (0, 0)))
    noise = member_noise[:, None, :]
    q, o, lse = near(info, latent, w_qkv)
    normalized, inverse, normed_out, predicted = far(
        info, q, o, lse, before, after, w_qkv, noise, dec, latent, w_out
    )
    preds = lax.all_gather(predicted, "mem", axis=0)
    crps_info = jnp.stack([lax.axis_index("mem"), around[1]])
    peers = lax.axis_size("mem") * bands
    grad, pieces = crps(
        crps_info,
        preds,
        jnp.pad(targets, ((0, padded - fields), (0, 0))),
        jnp.pad(field_weight, (0, padded - fields))[:, None],
        area_weight[None, :],
        normed_out,
        peers,
    )
    tiles = width // 128
    used = padded // 8 * tiles
    total = summed(pieces, used).astype(F32) / (rows * bands)
    grad_hidden = backward(grad, dec, normalized, inverse)
    weight_sum = total[:used].reshape(padded // 8, tiles, 8, 128).transpose(0, 2, 1, 3)
    return (
        grad_hidden,
        weight_sum.reshape(padded, width)[:fields],
        total[used, 0, 0] + total[used, 1, 0],
    )


def solution(mesh):
    return jax.shard_map(
        local,
        mesh=mesh,
        in_specs=(
            P("mem", "lat", None),
            P("mem", None),
            P(),
            P(),
            P(),
            P(None, "lat"),
            P("lat"),
            P(),
            P(),
            P("lat", None),
        ),
        out_specs=(P("mem", "lat", None), P(), P()),
        check_vma=False,
    )
```

```python
import jax
import jax.numpy as jnp
from jax import lax
from jax.experimental import pallas as pl
from jax.experimental.pallas import tpu as pltpu
from jax.sharding import PartitionSpec as P

HEAD_DIM = 64
HALO = 256
LOG2E = 1.4426950408889634

norm_eps = 1e-05
smooth_width = 0.25
F32 = jnp.float32
BF16 = jnp.bfloat16
MIB = 1024 * 1024


def normalize(x):
    mean = jnp.mean(x, axis=-1, keepdims=True)
    centred = x - mean
    var = jnp.mean(centred * centred, axis=-1, keepdims=True)
    inverse = lax.rsqrt(var + norm_eps)
    return centred * inverse, inverse


def nt_dot(a, b):
    return lax.dot_general(a, b, (((1,), (1,)), ((), ())), preferred_element_type=F32)


def tn_dot(a, b):
    return lax.dot_general(a, b, (((0,), (0,)), ((), ())), preferred_element_type=F32)


def nn_dot(a, b):
    return jnp.dot(a, b, preferred_element_type=F32)


QB = 256
STEP_COLS = 256
PAIR = 2 * HEAD_DIM
FIELD_TILE = 16
NEVER = -1e30


def bias_of(q_row, k_row, place_ref, count_ref, window_ref, rows):
    bands = count_ref.shape[0]
    band = lax.rem(place_ref[0], bands)
    offset = k_row - q_row
    in_window = (offset >= -window_ref[0, 0]) & (offset <= window_ref[0, 1])
    before = jnp.where(band > 0, count_ref[jnp.maximum(band - 1, 0)], 0)
    after = jnp.where(band < bands - 1, count_ref[jnp.minimum(band + 1, bands - 1)], 0)
    end = jnp.where(
        k_row < 0, before - rows, jnp.where(k_row < rows, count_ref[band], after + rows)
    )
    return jnp.where((in_window & (k_row < end)) | (offset == 0), 0.0, NEVER)


def iota(shape, axis):
    return lax.broadcasted_iota(jnp.int32, shape, axis)


def pair_scores(q, keys, bias, low):
    zero = jnp.zeros_like(q)
    both = jnp.concatenate([jnp.where(low, q, zero), jnp.where(low, zero, q)], axis=0)
    scores = nt_dot(both, keys)
    weights, tops = [], []
    for half in range(2):
        part = scores[half * q.shape[0] : (half + 1) * q.shape[0]] + bias
        top = jnp.max(part, axis=-1, keepdims=True)
        weights.append(jnp.exp2(part - top).astype(BF16))
        tops.append(top)
    return jnp.concatenate(weights, axis=1), jnp.where(low, tops[0], tops[1])


def set_ones(ref, low):
    half = ref.shape[-2] // 2
    one = jnp.ones((half, PAIR), BF16)
    for pair in range(ref.shape[0]):
        for group in range(ref.shape[1]):
            ref[pair, group, :half, PAIR:] = jnp.where(low, one, 0.0).astype(BF16)
            ref[pair, group, half:, PAIR:] = jnp.where(low, 0.0, one).astype(BF16)


def set_values(ref, group, at, value, low):
    half, count = ref.shape[-2] // 2, value.shape[0]
    for pair in range(ref.shape[0]):
        own = value[:, pair * PAIR : (pair + 1) * PAIR]
        zero = jnp.zeros_like(own)
        ref[pair, group, at : at + count, :PAIR] = jnp.where(low, own, zero)
        ref[pair, group, half + at : half + at + count, :PAIR] = jnp.where(low, zero, own)


def near_body(
    place_ref, count_ref, window_ref, latent_ref, wq_ref, wk_ref, wv_ref, q_ref, o_ref, lse_ref, normed_ref, bias_ref, k_ref, vx_ref
):
    step = pl.program_id(0)
    rows = bias_ref.shape[0]
    members = latent_ref.shape[0] // rows
    low = iota((1, PAIR), 1) < HEAD_DIM

    @pl.when(step == 0)
    def _():
        normed_ref[...] = normalize(latent_ref[...].astype(F32))[0].astype(BF16)
        shape = bias_ref.shape
        bias_ref[...] = bias_of(iota(shape, 0), iota(shape, 1), place_ref, count_ref, window_ref, rows)
        set_ones(vx_ref, low)


    def queries(at):
        span = slice(at, at + QB)
        q_ref[span] = (
            nn_dot(normed_ref[span], wq_ref[...]) * (HEAD_DIM ** (-0.5) * LOG2E)
        ).astype(BF16)

    def keys(at):
        span = slice(at, at + QB)
        k_ref[span] = nn_dot(normed_ref[span], wk_ref[...]).astype(BF16)

    def values(at):
        span = slice(at, at + QB)
        value = nn_dot(normed_ref[span], wv_ref[...]).astype(BF16)
        set_values(vx_ref, at // rows, at % rows, value, low)

    def attend(member, pair, block):
        cols = slice(pair * PAIR, (pair + 1) * PAIR)
        here = slice(block * QB, (block + 1) * QB)
        mine = slice(member * rows + block * QB, member * rows + (block + 1) * QB)
        reach = slice(member * rows, (member + 1) * rows)
        weight, top = pair_scores(q_ref[mine, cols], k_ref[reach, cols], bias_ref[here], low)
        total = nn_dot(weight, vx_ref[pair, member])
        summed_weight = total[:, PAIR:]
        o_ref[mine, cols] = (total[:, :PAIR] / summed_weight).astype(BF16)
        lse_ref[mine, cols] = top + jnp.log2(summed_weight)

    pairs, blocks = STEP_COLS // PAIR, rows // QB
    project = [
        [(f, member * rows + at) for f in (keys, values, queries) for at in range(0, rows, QB)]
        for member in range(members)
    ]
    for f, at in project[0]:
        f(at)
    for member in range(members):
        later = project[member + 1] if member + 1 < members else []
        tiles = [(pair, block) for pair in range(pairs) for block in range(blocks)]
        share = -(-len(later) // len(tiles))
        for i, (pair, block) in enumerate(tiles):
            for f, at in later[i * share : (i + 1) * share]:
                f(at)
            attend(member, pair, block)


def near(place, latent, w_qkv):
    members, rows, width = latent.shape
    tall = members * rows
    steps = width // STEP_COLS
    block = pl.BlockSpec((tall, STEP_COLS), lambda s: (0, s))
    return pl.pallas_call(
        near_body,
        grid=(steps,),
        in_specs=[
            *[pl.BlockSpec(memory_space=pltpu.SMEM)] * 3,
            pl.BlockSpec((tall, width), lambda s: (0, 0), pipeline_mode=pl.Buffered(1)),
            pl.BlockSpec((width, STEP_COLS), lambda s: (0, s)),
            pl.BlockSpec((width, STEP_COLS), lambda s: (0, steps + s)),
            pl.BlockSpec((width, STEP_COLS), lambda s: (0, 2 * steps + s)),
        ],
        out_specs=[block, block, block],
        out_shape=[
            jax.ShapeDtypeStruct((tall, width), BF16),
            jax.ShapeDtypeStruct((tall, width), BF16),
            jax.ShapeDtypeStruct((tall, width), F32),
        ],
        scratch_shapes=[
            pltpu.VMEM((tall, width), BF16),
            pltpu.VMEM((rows, rows), F32),
            pltpu.VMEM((tall, STEP_COLS), BF16),
            pltpu.VMEM((STEP_COLS // PAIR, members, 2 * rows, 2 * PAIR), BF16),
        ],
        compiler_params=pltpu.CompilerParams(vmem_limit_bytes=60 * MIB),
        cost_estimate=pl.CostEstimate(
            flops=20 * 10**9, bytes_accessed=16 * MIB, transcendentals=10**7
        ),
        name="near",
    )(*place, latent.reshape(tall, width), w_qkv, w_qkv, w_qkv)


def far_body(
    place_ref,
    count_ref,
    window_ref,
    q_ref,
    o_ref,
    lse_ref,
    before_ref,
    after_ref,
    wk_ref,
    wv_ref,
    noise_ref,
    dec_ref,
    latent_hbm,
    wout_hbm,
    normalized_hbm,
    inverse_ref,
    normed_out_hbm,
    predicted_ref,
    padded_ref,
    halo_ref,
    bias_ref,
    k_ref,
    vx_ref,
    att_ref,
    latent_ref,
    wout_ref,
    normalized_ref,
    normed_out_ref,
    sem,
    out_sem,
):
    step = pl.program_id(0)
    members, _, width = before_ref.shape
    tall = q_ref.shape[0]
    rows = tall // members
    low = iota((1, PAIR), 1) < HEAD_DIM
    late = [
        pltpu.make_async_copy(latent_hbm, latent_ref, sem.at[0]),
        pltpu.make_async_copy(wout_hbm, wout_ref, sem.at[1]),
    ]

    @pl.when(step == 0)
    def _():
        for copy in late:
            copy.start()
        padded_ref[...] = jnp.zeros_like(padded_ref)
        padded_ref[: dec_ref.shape[0]] = dec_ref[...]
        for member in range(members):
            for side, source in enumerate((before_ref, after_ref)):
                at = (2 * member + side) * HALO
                halo_ref[at : at + HALO] = normalize(source[member].astype(F32))[0].astype(BF16)
        shape = (HALO, HALO)
        bias_ref[0] = bias_of(iota(shape, 0), iota(shape, 1) - HALO, place_ref, count_ref, window_ref, rows)
        bias_ref[1] = bias_of(iota(shape, 0) + rows - HALO, iota(shape, 1) + rows, place_ref, count_ref, window_ref, rows)
        set_ones(vx_ref, low)

    def keys(at):
        span = slice(at, at + HALO)
        k_ref[span] = nn_dot(halo_ref[span], wk_ref[...]).astype(BF16)

    def values(at):
        span = slice(at, at + HALO)
        value = nn_dot(halo_ref[span], wv_ref[...]).astype(BF16)
        set_values(vx_ref, at // HALO, 0, value, low)

    def attend(member, pair, side):
        cols = slice(pair * PAIR, (pair + 1) * PAIR)
        out_cols = pl.ds(pl.multiple_of(step * STEP_COLS + pair * PAIR, PAIR), PAIR)
        at = member * rows + side * (rows - HALO)
        mine = slice(at, at + HALO)
        reach = slice((2 * member + side) * HALO, (2 * member + side + 1) * HALO)
        lse = lse_ref[mine, cols]
        weight, far_top = pair_scores(q_ref[mine, cols], k_ref[reach, cols], bias_ref[side], low)
        total = nn_dot(weight, vx_ref[pair, 2 * member + side])
        top = jnp.maximum(lse, far_top)
        near_share, far_share = jnp.exp2(lse - top), jnp.exp2(far_top - top)
        att_ref[mine, out_cols] = (
            (near_share * o_ref[mine, cols].astype(F32) + far_share * total[:, :PAIR])
            / (near_share + far_share * total[:, PAIR:])
        ).astype(BF16)

    groups = [(member, side) for member in range(members) for side in range(2)]

    def project(group):
        keys(group * HALO)
        values(group * HALO)

    project(0)
    for group, (member, side) in enumerate(groups):
        if group + 1 < len(groups):
            project(group + 1)
        for pair in range(STEP_COLS // PAIR):
            attend(member, pair, side)

    @pl.when(step == pl.num_programs(0) - 1)
    def _():
        for copy in late:
            copy.wait()
        copies = []
        for member in range(members):
            for at in range(0, rows, HALO):
                span = slice(at, at + HALO)
                attended = att_ref[member * rows + at : member * rows + at + HALO]
                hidden = latent_ref[member, span].astype(F32) + nn_dot(attended, wout_ref[...])
                normalized, inverse = normalize(hidden)
                normalized_ref[member, span] = normalized.astype(BF16)
                inverse_ref[member, span] = jnp.broadcast_to(inverse, (HALO, inverse_ref.shape[2]))
                normed_out = (normalized + noise_ref[member : member + 1].astype(F32)).astype(BF16)
                normed_out_ref[member, span] = normed_out
                predicted_ref[member, :, span] = nt_dot(padded_ref[...], normed_out).astype(BF16)
                for i, (source, target) in enumerate(
                    ((normalized_ref, normalized_hbm), (normed_out_ref, normed_out_hbm))
                ):
                    copy = pltpu.make_async_copy(
                        source.at[member, span], target.at[member, span], out_sem.at[len(copies)]
                    )
                    copy.start()
                    copies.append(copy)
        for copy in copies:
            copy.wait()


def far(place, q, o, lse, before, after, w_qkv, noise, dec, latent, w_out):
    members, rows, width = latent.shape
    tall = members * rows
    fields = dec.shape[0]
    padded = -(-fields // FIELD_TILE) * FIELD_TILE
    steps = width // STEP_COLS
    block = pl.BlockSpec((tall, STEP_COLS), lambda s: (0, s))
    whole2 = lambda s: (0, 0)
    whole3 = lambda s: (0, 0, 0)
    once = pl.Buffered(1)
    anywhere = pl.BlockSpec(memory_space=pl.ANY)
    return pl.pallas_call(
        far_body,
        grid=(steps,),
        in_specs=[
            *[pl.BlockSpec(memory_space=pltpu.SMEM)] * 3,
            block,
            block,
            block,
            pl.BlockSpec((members, HALO, width), whole3, pipeline_mode=once),
            pl.BlockSpec((members, HALO, width), whole3, pipeline_mode=once),
            pl.BlockSpec((width, STEP_COLS), lambda s: (0, steps + s)),
            pl.BlockSpec((width, STEP_COLS), lambda s: (0, 2 * steps + s)),
            pl.BlockSpec((members, width), whole2),
            pl.BlockSpec((fields, width), whole2),
            anywhere,
            anywhere,
        ],
        out_specs=[
            anywhere,
            pl.BlockSpec((members, rows, 128), whole3),
            anywhere,
            pl.BlockSpec((members, padded, rows), whole3),
            pl.BlockSpec((padded, width), whole2),
        ],
        out_shape=[
            jax.ShapeDtypeStruct((members, rows, width), BF16),
            jax.ShapeDtypeStruct((members, rows, 128), F32),
            jax.ShapeDtypeStruct((members, rows, width), BF16),
            jax.ShapeDtypeStruct((members, padded, rows), BF16),
            jax.ShapeDtypeStruct((padded, width), BF16),
        ],
        scratch_shapes=[
            pltpu.VMEM((members * 2 * HALO, width), BF16),
            pltpu.VMEM((2, HALO, HALO), F32),
            pltpu.VMEM((members * 2 * HALO, STEP_COLS), BF16),
            pltpu.VMEM((STEP_COLS // PAIR, members * 2, 2 * HALO, 2 * PAIR), BF16),
            pltpu.VMEM((tall, width), BF16),
            pltpu.VMEM((members, rows, width), BF16),
            pltpu.VMEM((width, width), BF16),
            pltpu.VMEM((members, rows, width), BF16),
            pltpu.VMEM((members, rows, width), BF16),
            pltpu.SemaphoreType.DMA((2,)),
            pltpu.SemaphoreType.DMA((2 * members * rows // HALO,)),
        ],
        compiler_params=pltpu.CompilerParams(vmem_limit_bytes=60 * MIB),
        cost_estimate=pl.CostEstimate(
            flops=15 * 10**9, bytes_accessed=22 * MIB, transcendentals=10**7
        ),
        name="far",
    )(*place, q, o, lse, before, after, w_qkv, w_qkv, noise, dec, latent, w_out)


def crps_body(
    place_ref, count_ref, pred_ref, target_ref, fw_ref, aw_ref, normed_hbm, grad_ref, pieces_ref, normed_ref, padded_ref, sem
):
    fetch = pltpu.make_async_copy(normed_hbm, normed_ref, sem)
    fetch.start()
    bands = count_ref.shape[0]
    first = lax.div(place_ref[0], bands)
    count = count_ref[lax.rem(place_ref[0], bands)]
    ensemble = pred_ref.shape[0] * pred_ref.shape[1]
    own_count = pred_ref.shape[1]
    lead = 1.0 / (ensemble - 1)
    fields, rows = padded_ref.shape
    real = target_ref.shape[0]
    padded_ref[...] = jnp.zeros_like(padded_ref)
    padded_ref[:real] = target_ref[...]
    width = normed_ref.shape[-1]
    target = padded_ref[...]
    used = lax.broadcasted_iota(jnp.int32, (1, rows), 1) < count
    shape = (fields, real)
    diagonal = iota(shape, 0) == iota(shape, 1)
    field_weight = jnp.sum(jnp.where(diagonal, fw_ref[...], 0.0), axis=1, keepdims=True)
    scale = field_weight * jnp.where(used, aw_ref[...], 0.0)

    def slope(gap):
        square = gap * gap + smooth_width * smooth_width
        root = lax.rsqrt(square)
        return gap * root, square * root

    loss = jnp.zeros((fields, rows), F32)
    grads = []
    for own in range(own_count):
        mine = pred_ref[first, own].astype(F32)
        pair_slope = jnp.zeros((fields, rows), F32)
        pair_abs = jnp.zeros((fields, rows), F32)
        for other in range(ensemble):
            s, a = slope(mine - pred_ref[other // own_count, other % own_count].astype(F32))
            pair_slope = pair_slope + s
            pair_abs = pair_abs + a
        s, a = slope(mine - target)
        grad = (scale * (s - pair_slope * lead)).astype(BF16)
        grad_ref[own] = grad
        loss = loss + scale * (a - pair_abs * (0.5 * lead))
        grads.append(grad)
    fetch.wait()
    weight = nn_dot(grads[0], normed_ref[0])
    for own in range(1, own_count):
        weight = weight + nn_dot(grads[own], normed_ref[own])
    tiles = width // 128
    for r in range(0, fields, 8):
        for c in range(tiles):
            piece = weight[r : r + 8, c * 128 : c * 128 + 128]
            pieces_ref[r // 8 * tiles + c] = piece.astype(BF16)
    used_pieces = fields // 8 * tiles
    whole = jnp.sum(jnp.sum(loss, axis=0, keepdims=True), axis=1, keepdims=True)
    high = whole.astype(BF16)
    rest = (whole - high.astype(F32)).astype(BF16)
    row = lax.broadcasted_iota(jnp.int32, (8, 128), 0)
    both = jnp.where(row == 0, high.astype(F32), jnp.where(row == 1, rest.astype(F32), 0.0))
    pieces_ref[used_pieces] = both.astype(BF16)
    pieces_ref[used_pieces + 1 :] = jnp.zeros_like(pieces_ref[used_pieces + 1 :])


def crps(place, preds, targets, field_weight, area_weight, normed_out, peers):
    _, own_count, fields, rows = preds.shape
    vmem = pl.BlockSpec(memory_space=pltpu.VMEM)
    return pl.pallas_call(
        crps_body,
        in_specs=[pl.BlockSpec(memory_space=pltpu.SMEM)] * 2
        + [vmem] * 4
        + [pl.BlockSpec(memory_space=pl.ANY)],
        out_specs=[vmem] * 2,
        out_shape=[
            jax.ShapeDtypeStruct((own_count, fields, rows), BF16),
            jax.ShapeDtypeStruct((peers, 8, 128), BF16),
        ],
        scratch_shapes=[
            pltpu.VMEM(normed_out.shape, BF16),
            pltpu.VMEM((fields, rows), F32),
            pltpu.SemaphoreType.DMA(()),
        ],
        compiler_params=pltpu.CompilerParams(vmem_limit_bytes=60 * MIB),
        cost_estimate=pl.CostEstimate(
            flops=4 * 10**8, bytes_accessed=4 * MIB, transcendentals=10**6
        ),
        name="crps",
    )(*place[:2], preds, targets, field_weight, area_weight, normed_out)


def backward_body(grad_ref, dec_ref, normalized_ref, inverse_ref, out_ref):
    grad_norm = tn_dot(grad_ref[...], dec_ref[...])
    normalized = normalized_ref[...].astype(F32)
    inverse = inverse_ref[...][:, :1]
    mean = jnp.mean(grad_norm, axis=-1, keepdims=True)
    dotted = jnp.mean(grad_norm * normalized, axis=-1, keepdims=True)
    out_ref[...] = (inverse * (grad_norm - mean - normalized * dotted)).astype(BF16)


def backward(grad, dec, normalized, inverse):
    members, fields, rows = grad.shape
    width = dec.shape[1]
    return pl.pallas_call(
        backward_body,
        grid=(members,),
        in_specs=[
            pl.BlockSpec((None, fields, rows), lambda m: (m, 0, 0)),
            pl.BlockSpec((fields, width), lambda m: (0, 0)),
            pl.BlockSpec((None, rows, width), lambda m: (m, 0, 0)),
            pl.BlockSpec((None, rows, 128), lambda m: (m, 0, 0)),
        ],
        out_specs=pl.BlockSpec((None, rows, width), lambda m: (m, 0, 0)),
        out_shape=jax.ShapeDtypeStruct((members, rows, width), BF16),
        compiler_params=pltpu.CompilerParams(vmem_limit_bytes=60 * MIB),
        cost_estimate=pl.CostEstimate(
            flops=5 * 10**8, bytes_accessed=5 * MIB, transcendentals=0
        ),
        name="backward",
    )(grad, dec, normalized, inverse)


def summed(pieces, loss_piece):
    axes = ("mem", "lat")
    parts = lax.all_to_all(pieces, axes, split_axis=0, concat_axis=0, tiled=True)
    mine = jnp.sum(parts.astype(F32), axis=0)
    loss = mine[0] + mine[1]
    rounded = lax.reduce_precision(loss, 8, 7)
    row = lax.broadcasted_iota(jnp.int32, mine.shape, 0)
    as_loss = jnp.where(row == 0, rounded, jnp.where(row == 1, loss - rounded, 0.0))
    mine = jnp.where(lax.axis_index(axes) == loss_piece, as_loss, mine).astype(BF16)
    spread = jnp.broadcast_to(mine[None], pieces.shape)
    return lax.all_to_all(spread, axes, split_axis=0, concat_axis=0, tiled=True)


def local(
    latent,
    member_noise,
    w_qkv,
    w_out,
    dec_weight,
    targets,
    area_weight,
    field_weight,
    band_count,
    band_window,
):
    members, rows, width = latent.shape
    bands = lax.axis_size("lat")
    fields = dec_weight.shape[0]
    up = [(i, i + 1) for i in range(bands - 1)]
    down = [(j, i) for i, j in up]
    before = lax.ppermute(latent[:, rows - HALO :], "lat", up)
    after = lax.ppermute(latent[:, :HALO], "lat", down)
    place = (lax.axis_index(("mem", "lat")).reshape(1), band_count, band_window)
    q, o, lse = near(place, latent, w_qkv)
    normalized, inverse, normed_out, predicted, dec = far(
        place, q, o, lse, before, after, w_qkv, member_noise, dec_weight, latent, w_out
    )
    preds = lax.all_gather(predicted, "mem", axis=0)
    peers = lax.axis_size("mem") * bands
    grad, pieces = crps(
        place, preds, targets, field_weight[None, :], area_weight[None, :], normed_out, peers
    )
    tiles = width // 128
    groups = preds.shape[2] // 8
    used = groups * tiles
    total = summed(pieces, used).astype(F32) / (rows * bands)
    grad_hidden = backward(grad, dec, normalized, inverse)
    weight_sum = total[:used].reshape(groups, tiles, 8, 128).transpose(0, 2, 1, 3)
    return (
        grad_hidden,
        weight_sum.reshape(groups * 8, width)[:fields],
        total[used, 0, 0] + total[used, 1, 0],
    )


def solution(mesh):
    return jax.shard_map(
        local,
        mesh=mesh,
        in_specs=(
            P("mem", "lat", None),
            P("mem", None),
            P(),
            P(),
            P(),
            P(None, "lat"),
            P("lat"),
            P(),
            P(),
            P("lat", None),
        ),
        out_specs=(P("mem", "lat", None), P(), P()),
        check_vma=False,
    )
```

```python
import jax
import jax.numpy as jnp
from jax import lax
from jax.experimental import pallas as pl
from jax.experimental.pallas import tpu as pltpu
from jax.sharding import PartitionSpec as P

HEAD_DIM = 64
HALO = 256
LOG2E = 1.4426950408889634

norm_eps = 1e-05
smooth_width = 0.25
F32 = jnp.float32
BF16 = jnp.bfloat16
MIB = 1024 * 1024


def normalize(x):
    mean = jnp.mean(x, axis=-1, keepdims=True)
    centred = x - mean
    var = jnp.mean(centred * centred, axis=-1, keepdims=True)
    inverse = lax.rsqrt(var + norm_eps)
    return centred * inverse, inverse


def nt_dot(a, b):
    return lax.dot_general(a, b, (((1,), (1,)), ((), ())), preferred_element_type=F32)


def tn_dot(a, b):
    return lax.dot_general(a, b, (((0,), (0,)), ((), ())), preferred_element_type=F32)


def nn_dot(a, b):
    return jnp.dot(a, b, preferred_element_type=F32)


QB = 256
STEP_COLS = 256
PAIR = 2 * HEAD_DIM
FIELD_TILE = 16
NEVER = -1e30


def bias_of(q_row, k_row, place_ref, count_ref, window_ref, rows):
    bands = count_ref.shape[0]
    band = lax.rem(place_ref[0], bands)
    offset = k_row - q_row
    in_window = (offset >= -window_ref[0, 0]) & (offset <= window_ref[0, 1])
    before = jnp.where(band > 0, count_ref[jnp.maximum(band - 1, 0)], 0)
    after = jnp.where(band < bands - 1, count_ref[jnp.minimum(band + 1, bands - 1)], 0)
    end = jnp.where(
        k_row < 0, before - rows, jnp.where(k_row < rows, count_ref[band], after + rows)
    )
    return jnp.where((in_window & (k_row < end)) | (offset == 0), 0.0, NEVER)


def iota(shape, axis):
    return lax.broadcasted_iota(jnp.int32, shape, axis)


def pair_scores(q, keys, bias, low):
    zero = jnp.zeros_like(q)
    both = jnp.concatenate([jnp.where(low, q, zero), jnp.where(low, zero, q)], axis=0)
    scores = nt_dot(both, keys)
    weights, tops = [], []
    for half in range(2):
        part = scores[half * q.shape[0] : (half + 1) * q.shape[0]] + bias
        top = jnp.max(part, axis=-1, keepdims=True)
        weights.append(jnp.exp2(part - top).astype(BF16))
        tops.append(top)
    return jnp.concatenate(weights, axis=1), jnp.where(low, tops[0], tops[1])


def set_ones(ref, low):
    half = ref.shape[-2] // 2
    one = jnp.ones((half, PAIR), BF16)
    for pair in range(ref.shape[0]):
        for group in range(ref.shape[1]):
            ref[pair, group, :half, PAIR:] = jnp.where(low, one, 0.0).astype(BF16)
            ref[pair, group, half:, PAIR:] = jnp.where(low, 0.0, one).astype(BF16)


def set_values(ref, group, at, value, low):
    half, count = ref.shape[-2] // 2, value.shape[0]
    for pair in range(ref.shape[0]):
        own = value[:, pair * PAIR : (pair + 1) * PAIR]
        zero = jnp.zeros_like(own)
        ref[pair, group, at : at + count, :PAIR] = jnp.where(low, own, zero)
        ref[pair, group, half + at : half + at + count, :PAIR] = jnp.where(low, zero, own)


def near_body(
    place_ref, count_ref, window_ref, latent_ref, wq_ref, wk_ref, wv_ref, q_ref, o_ref, lse_ref, normed_ref, bias_ref, k_ref, vx_ref
):
    step = pl.program_id(0)
    rows = bias_ref.shape[0]
    members = latent_ref.shape[0] // rows
    low = iota((1, PAIR), 1) < HEAD_DIM

    @pl.when(step == 0)
    def _():
        normed_ref[...] = normalize(latent_ref[...].astype(F32))[0].astype(BF16)
        shape = bias_ref.shape
        bias_ref[...] = bias_of(iota(shape, 0), iota(shape, 1), place_ref, count_ref, window_ref, rows)
        set_ones(vx_ref, low)


    def queries(at):
        span = slice(at, at + QB)
        q_ref[span] = (
            nn_dot(normed_ref[span], wq_ref[...]) * (HEAD_DIM ** (-0.5) * LOG2E)
        ).astype(BF16)

    def keys(at):
        span = slice(at, at + QB)
        k_ref[span] = nn_dot(normed_ref[span], wk_ref[...]).astype(BF16)

    def values(at):
        span = slice(at, at + QB)
        value = nn_dot(normed_ref[span], wv_ref[...]).astype(BF16)
        set_values(vx_ref, at // rows, at % rows, value, low)

    def attend(member, pair, block):
        cols = slice(pair * PAIR, (pair + 1) * PAIR)
        here = slice(block * QB, (block + 1) * QB)
        mine = slice(member * rows + block * QB, member * rows + (block + 1) * QB)
        reach = slice(member * rows, (member + 1) * rows)
        weight, top = pair_scores(q_ref[mine, cols], k_ref[reach, cols], bias_ref[here], low)
        total = nn_dot(weight, vx_ref[pair, member])
        summed_weight = total[:, PAIR:]
        o_ref[mine, cols] = (total[:, :PAIR] / summed_weight).astype(BF16)
        lse_ref[mine, cols] = top + jnp.log2(summed_weight)

    pairs, blocks = STEP_COLS // PAIR, rows // QB
    project = [
        [(f, member * rows + at) for f in (keys, values, queries) for at in range(0, rows, QB)]
        for member in range(members)
    ]
    for f, at in project[0]:
        f(at)
    for member in range(members):
        later = project[member + 1] if member + 1 < members else []
        tiles = [(pair, block) for pair in range(pairs) for block in range(blocks)]
        share = -(-len(later) // len(tiles))
        for i, (pair, block) in enumerate(tiles):
            for f, at in later[i * share : (i + 1) * share]:
                f(at)
            attend(member, pair, block)


def near(place, latent, w_qkv):
    members, rows, width = latent.shape
    tall = members * rows
    steps = width // STEP_COLS
    block = pl.BlockSpec((tall, STEP_COLS), lambda s: (0, s))
    return pl.pallas_call(
        near_body,
        grid=(steps,),
        in_specs=[
            *[pl.BlockSpec(memory_space=pltpu.SMEM)] * 3,
            pl.BlockSpec((tall, width), lambda s: (0, 0), pipeline_mode=pl.Buffered(1)),
            pl.BlockSpec((width, STEP_COLS), lambda s: (0, s)),
            pl.BlockSpec((width, STEP_COLS), lambda s: (0, steps + s)),
            pl.BlockSpec((width, STEP_COLS), lambda s: (0, 2 * steps + s)),
        ],
        out_specs=[block, block, block],
        out_shape=[
            jax.ShapeDtypeStruct((tall, width), BF16),
            jax.ShapeDtypeStruct((tall, width), BF16),
            jax.ShapeDtypeStruct((tall, width), F32),
        ],
        scratch_shapes=[
            pltpu.VMEM((tall, width), BF16),
            pltpu.VMEM((rows, rows), F32),
            pltpu.VMEM((tall, STEP_COLS), BF16),
            pltpu.VMEM((STEP_COLS // PAIR, members, 2 * rows, 2 * PAIR), BF16),
        ],
        compiler_params=pltpu.CompilerParams(vmem_limit_bytes=60 * MIB),
        cost_estimate=pl.CostEstimate(
            flops=20 * 10**9, bytes_accessed=16 * MIB, transcendentals=10**7
        ),
        name="near",
    )(*place, latent.reshape(tall, width), w_qkv, w_qkv, w_qkv)


def far_body(
    place_ref,
    count_ref,
    window_ref,
    q_ref,
    o_ref,
    lse_ref,
    before_ref,
    after_ref,
    wk_ref,
    wv_ref,
    noise_ref,
    dec_ref,
    latent_hbm,
    wout_hbm,
    normalized_hbm,
    inverse_ref,
    normed_out_hbm,
    predicted_ref,
    padded_ref,
    halo_ref,
    bias_ref,
    k_ref,
    vx_ref,
    att_ref,
    latent_ref,
    wout_ref,
    normalized_ref,
    normed_out_ref,
    sem,
    out_sem,
):
    step = pl.program_id(0)
    members, _, width = before_ref.shape
    tall = q_ref.shape[0]
    rows = tall // members
    low = iota((1, PAIR), 1) < HEAD_DIM
    late = [
        pltpu.make_async_copy(latent_hbm, latent_ref, sem.at[0]),
        pltpu.make_async_copy(wout_hbm, wout_ref, sem.at[1]),
    ]

    @pl.when(step == 0)
    def _():
        for copy in late:
            copy.start()
        padded_ref[...] = jnp.zeros_like(padded_ref)
        padded_ref[: dec_ref.shape[0]] = dec_ref[...]
        for member in range(members):
            for side, source in enumerate((before_ref, after_ref)):
                at = (2 * member + side) * HALO
                halo_ref[at : at + HALO] = normalize(source[member].astype(F32))[0].astype(BF16)
        shape = (HALO, HALO)
        bias_ref[0] = bias_of(iota(shape, 0), iota(shape, 1) - HALO, place_ref, count_ref, window_ref, rows)
        bias_ref[1] = bias_of(iota(shape, 0) + rows - HALO, iota(shape, 1) + rows, place_ref, count_ref, window_ref, rows)
        set_ones(vx_ref, low)

    def keys(at):
        span = slice(at, at + HALO)
        k_ref[span] = nn_dot(halo_ref[span], wk_ref[...]).astype(BF16)

    def values(at):
        span = slice(at, at + HALO)
        value = nn_dot(halo_ref[span], wv_ref[...]).astype(BF16)
        set_values(vx_ref, at // HALO, 0, value, low)

    def attend(member, pair, side):
        cols = slice(pair * PAIR, (pair + 1) * PAIR)
        out_cols = pl.ds(pl.multiple_of(step * STEP_COLS + pair * PAIR, PAIR), PAIR)
        at = member * rows + side * (rows - HALO)
        mine = slice(at, at + HALO)
        reach = slice((2 * member + side) * HALO, (2 * member + side + 1) * HALO)
        lse = lse_ref[mine, cols]
        weight, far_top = pair_scores(q_ref[mine, cols], k_ref[reach, cols], bias_ref[side], low)
        total = nn_dot(weight, vx_ref[pair, 2 * member + side])
        top = jnp.maximum(lse, far_top)
        near_share, far_share = jnp.exp2(lse - top), jnp.exp2(far_top - top)
        att_ref[mine, out_cols] = (
            (near_share * o_ref[mine, cols].astype(F32) + far_share * total[:, :PAIR])
            / (near_share + far_share * total[:, PAIR:])
        ).astype(BF16)

    groups = [(member, side) for member in range(members) for side in range(2)]

    def project(group):
        keys(group * HALO)
        values(group * HALO)

    project(0)
    for group, (member, side) in enumerate(groups):
        if group + 1 < len(groups):
            project(group + 1)
        for pair in range(STEP_COLS // PAIR):
            attend(member, pair, side)

    @pl.when(step == pl.num_programs(0) - 1)
    def _():
        for copy in late:
            copy.wait()
        copies = []
        chunks = [(member, at) for member in range(members) for at in range(0, rows, HALO)]

        def hidden_of(member, at):
            attended = att_ref[member * rows + at : member * rows + at + HALO]
            return latent_ref[member, at : at + HALO].astype(F32) + nn_dot(attended, wout_ref[...])

        hidden = hidden_of(*chunks[0])
        for index, (member, at) in enumerate(chunks):
            after = hidden_of(*chunks[index + 1]) if index + 1 < len(chunks) else None
            span = slice(at, at + HALO)
            normalized, inverse = normalize(hidden)
            normalized_ref[member, span] = normalized.astype(BF16)
            inverse_ref[member, span] = jnp.broadcast_to(inverse, (HALO, inverse_ref.shape[2]))
            normed_out = (normalized + noise_ref[member : member + 1].astype(F32)).astype(BF16)
            normed_out_ref[member, span] = normed_out
            predicted_ref[member, :, span] = nt_dot(padded_ref[...], normed_out).astype(BF16)
            for source, target in ((normalized_ref, normalized_hbm), (normed_out_ref, normed_out_hbm)):
                copy = pltpu.make_async_copy(
                    source.at[member, span], target.at[member, span], out_sem.at[len(copies)]
                )
                copy.start()
                copies.append(copy)
            hidden = after
        for copy in copies:
            copy.wait()


def far(place, q, o, lse, before, after, w_qkv, noise, dec, latent, w_out):
    members, rows, width = latent.shape
    tall = members * rows
    fields = dec.shape[0]
    padded = -(-fields // FIELD_TILE) * FIELD_TILE
    steps = width // STEP_COLS
    block = pl.BlockSpec((tall, STEP_COLS), lambda s: (0, s))
    whole2 = lambda s: (0, 0)
    whole3 = lambda s: (0, 0, 0)
    once = pl.Buffered(1)
    anywhere = pl.BlockSpec(memory_space=pl.ANY)
    return pl.pallas_call(
        far_body,
        grid=(steps,),
        in_specs=[
            *[pl.BlockSpec(memory_space=pltpu.SMEM)] * 3,
            block,
            block,
            block,
            pl.BlockSpec((members, HALO, width), whole3, pipeline_mode=once),
            pl.BlockSpec((members, HALO, width), whole3, pipeline_mode=once),
            pl.BlockSpec((width, STEP_COLS), lambda s: (0, steps + s)),
            pl.BlockSpec((width, STEP_COLS), lambda s: (0, 2 * steps + s)),
            pl.BlockSpec((members, width), whole2),
            pl.BlockSpec((fields, width), whole2),
            anywhere,
            anywhere,
        ],
        out_specs=[
            anywhere,
            pl.BlockSpec((members, rows, 128), whole3),
            anywhere,
            pl.BlockSpec((members, padded, rows), whole3),
            pl.BlockSpec((padded, width), whole2),
        ],
        out_shape=[
            jax.ShapeDtypeStruct((members, rows, width), BF16),
            jax.ShapeDtypeStruct((members, rows, 128), F32),
            jax.ShapeDtypeStruct((members, rows, width), BF16),
            jax.ShapeDtypeStruct((members, padded, rows), BF16),
            jax.ShapeDtypeStruct((padded, width), BF16),
        ],
        scratch_shapes=[
            pltpu.VMEM((members * 2 * HALO, width), BF16),
            pltpu.VMEM((2, HALO, HALO), F32),
            pltpu.VMEM((members * 2 * HALO, STEP_COLS), BF16),
            pltpu.VMEM((STEP_COLS // PAIR, members * 2, 2 * HALO, 2 * PAIR), BF16),
            pltpu.VMEM((tall, width), BF16),
            pltpu.VMEM((members, rows, width), BF16),
            pltpu.VMEM((width, width), BF16),
            pltpu.VMEM((members, rows, width), BF16),
            pltpu.VMEM((members, rows, width), BF16),
            pltpu.SemaphoreType.DMA((2,)),
            pltpu.SemaphoreType.DMA((2 * members * rows // HALO,)),
        ],
        compiler_params=pltpu.CompilerParams(vmem_limit_bytes=60 * MIB),
        cost_estimate=pl.CostEstimate(
            flops=15 * 10**9, bytes_accessed=22 * MIB, transcendentals=10**7
        ),
        name="far",
    )(*place, q, o, lse, before, after, w_qkv, w_qkv, noise, dec, latent, w_out)


def crps_body(
    place_ref, count_ref, pred_ref, target_ref, fw_ref, aw_ref, normed_hbm, grad_ref, pieces_ref, normed_ref, padded_ref, sem
):
    fetch = pltpu.make_async_copy(normed_hbm, normed_ref, sem)
    fetch.start()
    bands = count_ref.shape[0]
    first = lax.div(place_ref[0], bands)
    count = count_ref[lax.rem(place_ref[0], bands)]
    ensemble = pred_ref.shape[0] * pred_ref.shape[1]
    own_count = pred_ref.shape[1]
    lead = 1.0 / (ensemble - 1)
    fields, rows = padded_ref.shape
    real = target_ref.shape[0]
    padded_ref[...] = jnp.zeros_like(padded_ref)
    padded_ref[:real] = target_ref[...]
    width = normed_ref.shape[-1]
    target = padded_ref[...]
    used = lax.broadcasted_iota(jnp.int32, (1, rows), 1) < count
    shape = (fields, real)
    diagonal = iota(shape, 0) == iota(shape, 1)
    field_weight = jnp.sum(jnp.where(diagonal, fw_ref[...], 0.0), axis=1, keepdims=True)
    scale = field_weight * jnp.where(used, aw_ref[...], 0.0)

    def slope(gap):
        square = gap * gap + smooth_width * smooth_width
        root = lax.rsqrt(square)
        return gap * root, square * root

    loss = jnp.zeros((fields, rows), F32)
    grads = []
    for own in range(own_count):
        mine = pred_ref[first, own].astype(F32)
        pair_slope = jnp.zeros((fields, rows), F32)
        pair_abs = jnp.zeros((fields, rows), F32)
        for other in range(ensemble):
            s, a = slope(mine - pred_ref[other // own_count, other % own_count].astype(F32))
            pair_slope = pair_slope + s
            pair_abs = pair_abs + a
        s, a = slope(mine - target)
        grad = (scale * (s - pair_slope * lead)).astype(BF16)
        grad_ref[own] = grad
        loss = loss + scale * (a - pair_abs * (0.5 * lead))
        grads.append(grad)
    fetch.wait()
    weight = nn_dot(grads[0], normed_ref[0])
    for own in range(1, own_count):
        weight = weight + nn_dot(grads[own], normed_ref[own])
    tiles = width // 128
    for r in range(0, fields, 8):
        for c in range(tiles):
            piece = weight[r : r + 8, c * 128 : c * 128 + 128]
            pieces_ref[r // 8 * tiles + c] = piece.astype(BF16)
    used_pieces = fields // 8 * tiles
    whole = jnp.sum(jnp.sum(loss, axis=0, keepdims=True), axis=1, keepdims=True)
    high = whole.astype(BF16)
    rest = (whole - high.astype(F32)).astype(BF16)
    row = lax.broadcasted_iota(jnp.int32, (8, 128), 0)
    both = jnp.where(row == 0, high.astype(F32), jnp.where(row == 1, rest.astype(F32), 0.0))
    pieces_ref[used_pieces] = both.astype(BF16)
    pieces_ref[used_pieces + 1 :] = jnp.zeros_like(pieces_ref[used_pieces + 1 :])


def crps(place, preds, targets, field_weight, area_weight, normed_out, peers):
    _, own_count, fields, rows = preds.shape
    vmem = pl.BlockSpec(memory_space=pltpu.VMEM)
    return pl.pallas_call(
        crps_body,
        in_specs=[pl.BlockSpec(memory_space=pltpu.SMEM)] * 2
        + [vmem] * 4
        + [pl.BlockSpec(memory_space=pl.ANY)],
        out_specs=[vmem] * 2,
        out_shape=[
            jax.ShapeDtypeStruct((own_count, fields, rows), BF16),
            jax.ShapeDtypeStruct((peers, 8, 128), BF16),
        ],
        scratch_shapes=[
            pltpu.VMEM(normed_out.shape, BF16),
            pltpu.VMEM((fields, rows), F32),
            pltpu.SemaphoreType.DMA(()),
        ],
        compiler_params=pltpu.CompilerParams(vmem_limit_bytes=20 * MIB),
        cost_estimate=pl.CostEstimate(
            flops=4 * 10**8, bytes_accessed=4 * MIB, transcendentals=10**6
        ),
        name="crps",
    )(*place[:2], preds, targets, field_weight, area_weight, normed_out)


def backward_body(grad_ref, dec_ref, normalized_ref, inverse_ref, out_ref):
    grad_norm = tn_dot(grad_ref[...], dec_ref[...])
    normalized = normalized_ref[...].astype(F32)
    inverse = inverse_ref[...][:, :1]
    mean = jnp.mean(grad_norm, axis=-1, keepdims=True)
    dotted = jnp.mean(grad_norm * normalized, axis=-1, keepdims=True)
    out_ref[...] = (inverse * (grad_norm - mean - normalized * dotted)).astype(BF16)


def backward(grad, dec, normalized, inverse):
    members, fields, rows = grad.shape
    width = dec.shape[1]
    return pl.pallas_call(
        backward_body,
        grid=(members,),
        in_specs=[
            pl.BlockSpec((None, fields, rows), lambda m: (m, 0, 0)),
            pl.BlockSpec((fields, width), lambda m: (0, 0)),
            pl.BlockSpec((None, rows, width), lambda m: (m, 0, 0)),
            pl.BlockSpec((None, rows, 128), lambda m: (m, 0, 0)),
        ],
        out_specs=pl.BlockSpec((None, rows, width), lambda m: (m, 0, 0)),
        out_shape=jax.ShapeDtypeStruct((members, rows, width), BF16),
        compiler_params=pltpu.CompilerParams(vmem_limit_bytes=60 * MIB),
        cost_estimate=pl.CostEstimate(
            flops=5 * 10**8, bytes_accessed=5 * MIB, transcendentals=0
        ),
        name="backward",
    )(grad, dec, normalized, inverse)


def summed(pieces, loss_piece):
    axes = ("mem", "lat")
    parts = lax.all_to_all(pieces, axes, split_axis=0, concat_axis=0, tiled=True)
    mine = jnp.sum(parts.astype(F32), axis=0)
    loss = mine[0] + mine[1]
    rounded = lax.reduce_precision(loss, 8, 7)
    row = lax.broadcasted_iota(jnp.int32, mine.shape, 0)
    as_loss = jnp.where(row == 0, rounded, jnp.where(row == 1, loss - rounded, 0.0))
    mine = jnp.where(lax.axis_index(axes) == loss_piece, as_loss, mine).astype(BF16)
    spread = jnp.broadcast_to(mine[None], pieces.shape)
    return lax.all_to_all(spread, axes, split_axis=0, concat_axis=0, tiled=True)


def local(
    latent,
    member_noise,
    w_qkv,
    w_out,
    dec_weight,
    targets,
    area_weight,
    field_weight,
    band_count,
    band_window,
):
    members, rows, width = latent.shape
    bands = lax.axis_size("lat")
    fields = dec_weight.shape[0]
    up = [(i, i + 1) for i in range(bands - 1)]
    down = [(j, i) for i, j in up]
    before = lax.ppermute(latent[:, rows - HALO :], "lat", up)
    after = lax.ppermute(latent[:, :HALO], "lat", down)
    place = (lax.axis_index(("mem", "lat")).reshape(1), band_count, band_window)
    q, o, lse = near(place, latent, w_qkv)
    normalized, inverse, normed_out, predicted, dec = far(
        place, q, o, lse, before, after, w_qkv, member_noise, dec_weight, latent, w_out
    )
    preds = lax.all_gather(predicted, "mem", axis=0)
    peers = lax.axis_size("mem") * bands
    grad, pieces = crps(
        place, preds, targets, field_weight[None, :], area_weight[None, :], normed_out, peers
    )
    tiles = width // 128
    groups = preds.shape[2] // 8
    used = groups * tiles
    total = summed(pieces, used).astype(F32) / (rows * bands)
    grad_hidden = backward(grad, dec, normalized, inverse)
    weight_sum = total[:used].reshape(groups, tiles, 8, 128).transpose(0, 2, 1, 3)
    return (
        grad_hidden,
        weight_sum.reshape(groups * 8, width)[:fields],
        total[used, 0, 0] + total[used, 1, 0],
    )


def solution(mesh):
    return jax.shard_map(
        local,
        mesh=mesh,
        in_specs=(
            P("mem", "lat", None),
            P("mem", None),
            P(),
            P(),
            P(),
            P(None, "lat"),
            P("lat"),
            P(),
            P(),
            P("lat", None),
        ),
        out_specs=(P("mem", "lat", None), P(), P()),
        check_vma=False,
    )
```

```python
import jax
import jax.numpy as jnp
from jax import lax
from jax.experimental import pallas as pl
from jax.experimental.pallas import tpu as pltpu
from jax.sharding import PartitionSpec as P

HEAD_DIM = 64
HALO = 256
LOG2E = 1.4426950408889634

norm_eps = 1e-05
smooth_width = 0.25
F32 = jnp.float32
BF16 = jnp.bfloat16
MIB = 1024 * 1024


def normalize(x):
    mean = jnp.mean(x, axis=-1, keepdims=True)
    centred = x - mean
    var = jnp.mean(centred * centred, axis=-1, keepdims=True)
    inverse = lax.rsqrt(var + norm_eps)
    return centred * inverse, inverse


def nt_dot(a, b):
    return lax.dot_general(a, b, (((1,), (1,)), ((), ())), preferred_element_type=F32)


def tn_dot(a, b):
    return lax.dot_general(a, b, (((0,), (0,)), ((), ())), preferred_element_type=F32)


def nn_dot(a, b):
    return jnp.dot(a, b, preferred_element_type=F32)


QB = 256
STEP_COLS = 256
PAIR = 2 * HEAD_DIM
FIELD_TILE = 8
NEVER = -1e30


def bias_of(q_row, k_row, place_ref, count_ref, window_ref, rows):
    bands = count_ref.shape[0]
    band = lax.rem(place_ref[0], bands)
    offset = k_row - q_row
    in_window = (offset >= -window_ref[0, 0]) & (offset <= window_ref[0, 1])
    before = jnp.where(band > 0, count_ref[jnp.maximum(band - 1, 0)], 0)
    after = jnp.where(band < bands - 1, count_ref[jnp.minimum(band + 1, bands - 1)], 0)
    end = jnp.where(
        k_row < 0, before - rows, jnp.where(k_row < rows, count_ref[band], after + rows)
    )
    return jnp.where((in_window & (k_row < end)) | (offset == 0), 0.0, NEVER)


def iota(shape, axis):
    return lax.broadcasted_iota(jnp.int32, shape, axis)


def pair_scores(q, keys, bias, low):
    zero = jnp.zeros_like(q)
    both = jnp.concatenate([jnp.where(low, q, zero), jnp.where(low, zero, q)], axis=0)
    scores = nt_dot(both, keys)
    weights, tops = [], []
    for half in range(2):
        part = scores[half * q.shape[0] : (half + 1) * q.shape[0]] + bias
        top = jnp.max(part, axis=-1, keepdims=True)
        weights.append(jnp.exp2(part - top).astype(BF16))
        tops.append(top)
    return jnp.concatenate(weights, axis=1), jnp.where(low, tops[0], tops[1])


def set_ones(ref, low):
    half = ref.shape[-2] // 2
    one = jnp.ones((half, PAIR), BF16)
    for pair in range(ref.shape[0]):
        for group in range(ref.shape[1]):
            ref[pair, group, :half, PAIR:] = jnp.where(low, one, 0.0).astype(BF16)
            ref[pair, group, half:, PAIR:] = jnp.where(low, 0.0, one).astype(BF16)


def set_values(ref, group, at, value, low):
    half, count = ref.shape[-2] // 2, value.shape[0]
    for pair in range(ref.shape[0]):
        own = value[:, pair * PAIR : (pair + 1) * PAIR]
        zero = jnp.zeros_like(own)
        ref[pair, group, at : at + count, :PAIR] = jnp.where(low, own, zero)
        ref[pair, group, half + at : half + at + count, :PAIR] = jnp.where(low, zero, own)


def near_body(
    place_ref, count_ref, window_ref, latent_ref, wq_ref, wk_ref, wv_ref, q_ref, o_ref, lse_ref, normed_ref, bias_ref, k_ref, vx_ref
):
    step = pl.program_id(0)
    rows = bias_ref.shape[0]
    members = latent_ref.shape[0] // rows
    low = iota((1, PAIR), 1) < HEAD_DIM

    @pl.when(step == 0)
    def _():
        normed_ref[...] = normalize(latent_ref[...].astype(F32))[0].astype(BF16)
        shape = bias_ref.shape
        bias_ref[...] = bias_of(iota(shape, 0), iota(shape, 1), place_ref, count_ref, window_ref, rows)
        set_ones(vx_ref, low)


    def queries(at):
        span = slice(at, at + QB)
        q_ref[span] = (
            nn_dot(normed_ref[span], wq_ref[...]) * (HEAD_DIM ** (-0.5) * LOG2E)
        ).astype(BF16)

    def keys(at):
        span = slice(at, at + QB)
        k_ref[span] = nn_dot(normed_ref[span], wk_ref[...]).astype(BF16)

    def values(at):
        span = slice(at, at + QB)
        value = nn_dot(normed_ref[span], wv_ref[...]).astype(BF16)
        set_values(vx_ref, at // rows, at % rows, value, low)

    def attend(member, pair, block):
        cols = slice(pair * PAIR, (pair + 1) * PAIR)
        here = slice(block * QB, (block + 1) * QB)
        mine = slice(member * rows + block * QB, member * rows + (block + 1) * QB)
        reach = slice(member * rows, (member + 1) * rows)
        weight, top = pair_scores(q_ref[mine, cols], k_ref[reach, cols], bias_ref[here], low)
        total = nn_dot(weight, vx_ref[pair, member])
        summed_weight = total[:, PAIR:]
        o_ref[mine, cols] = (total[:, :PAIR] / summed_weight).astype(BF16)
        lse_ref[mine, cols] = top + jnp.log2(summed_weight)

    pairs, blocks = STEP_COLS // PAIR, rows // QB
    project = [
        [(f, member * rows + at) for f in (keys, values, queries) for at in range(0, rows, QB)]
        for member in range(members)
    ]
    for f, at in project[0]:
        f(at)
    for member in range(members):
        later = project[member + 1] if member + 1 < members else []
        tiles = [(pair, block) for pair in range(pairs) for block in range(blocks)]
        share = -(-len(later) // len(tiles))
        for i, (pair, block) in enumerate(tiles):
            for f, at in later[i * share : (i + 1) * share]:
                f(at)
            attend(member, pair, block)


def near(place, latent, w_qkv):
    members, rows, width = latent.shape
    tall = members * rows
    steps = width // STEP_COLS
    block = pl.BlockSpec((tall, STEP_COLS), lambda s: (0, s))
    return pl.pallas_call(
        near_body,
        grid=(steps,),
        in_specs=[
            *[pl.BlockSpec(memory_space=pltpu.SMEM)] * 3,
            pl.BlockSpec((tall, width), lambda s: (0, 0), pipeline_mode=pl.Buffered(1)),
            pl.BlockSpec((width, STEP_COLS), lambda s: (0, s)),
            pl.BlockSpec((width, STEP_COLS), lambda s: (0, steps + s)),
            pl.BlockSpec((width, STEP_COLS), lambda s: (0, 2 * steps + s)),
        ],
        out_specs=[block, block, block],
        out_shape=[
            jax.ShapeDtypeStruct((tall, width), BF16),
            jax.ShapeDtypeStruct((tall, width), BF16),
            jax.ShapeDtypeStruct((tall, width), F32),
        ],
        scratch_shapes=[
            pltpu.VMEM((tall, width), BF16),
            pltpu.VMEM((rows, rows), F32),
            pltpu.VMEM((tall, STEP_COLS), BF16),
            pltpu.VMEM((STEP_COLS // PAIR, members, 2 * rows, 2 * PAIR), BF16),
        ],
        compiler_params=pltpu.CompilerParams(vmem_limit_bytes=60 * MIB),
        cost_estimate=pl.CostEstimate(
            flops=20 * 10**9, bytes_accessed=16 * MIB, transcendentals=10**7
        ),
        name="near",
    )(*place, latent.reshape(tall, width), w_qkv, w_qkv, w_qkv)


def far_body(
    place_ref,
    count_ref,
    window_ref,
    q_ref,
    o_ref,
    lse_ref,
    before_ref,
    after_ref,
    wk_ref,
    wv_ref,
    noise_ref,
    dec_ref,
    latent_hbm,
    wout_hbm,
    normalized_hbm,
    inverse_ref,
    normed_out_hbm,
    predicted_ref,
    padded_ref,
    halo_ref,
    bias_ref,
    k_ref,
    vx_ref,
    att_ref,
    latent_ref,
    wout_ref,
    normalized_ref,
    normed_out_ref,
    sem,
    out_sem,
):
    step = pl.program_id(0)
    members, _, width = before_ref.shape
    tall = q_ref.shape[0]
    rows = tall // members
    low = iota((1, PAIR), 1) < HEAD_DIM
    late = [
        pltpu.make_async_copy(latent_hbm, latent_ref, sem.at[0]),
        pltpu.make_async_copy(wout_hbm, wout_ref, sem.at[1]),
    ]

    @pl.when(step == 0)
    def _():
        for copy in late:
            copy.start()
        padded_ref[...] = jnp.zeros_like(padded_ref)
        padded_ref[: dec_ref.shape[0]] = dec_ref[...]
        for member in range(members):
            for side, source in enumerate((before_ref, after_ref)):
                at = (2 * member + side) * HALO
                halo_ref[at : at + HALO] = normalize(source[member].astype(F32))[0].astype(BF16)
        shape = (HALO, HALO)
        bias_ref[0] = bias_of(iota(shape, 0), iota(shape, 1) - HALO, place_ref, count_ref, window_ref, rows)
        bias_ref[1] = bias_of(iota(shape, 0) + rows - HALO, iota(shape, 1) + rows, place_ref, count_ref, window_ref, rows)
        set_ones(vx_ref, low)

    def keys(at):
        span = slice(at, at + HALO)
        k_ref[span] = nn_dot(halo_ref[span], wk_ref[...]).astype(BF16)

    def values(at):
        span = slice(at, at + HALO)
        value = nn_dot(halo_ref[span], wv_ref[...]).astype(BF16)
        set_values(vx_ref, at // HALO, 0, value, low)

    def attend(member, pair, side):
        cols = slice(pair * PAIR, (pair + 1) * PAIR)
        out_cols = pl.ds(pl.multiple_of(step * STEP_COLS + pair * PAIR, PAIR), PAIR)
        at = member * rows + side * (rows - HALO)
        mine = slice(at, at + HALO)
        reach = slice((2 * member + side) * HALO, (2 * member + side + 1) * HALO)
        lse = lse_ref[mine, cols]
        weight, far_top = pair_scores(q_ref[mine, cols], k_ref[reach, cols], bias_ref[side], low)
        total = nn_dot(weight, vx_ref[pair, 2 * member + side])
        top = jnp.maximum(lse, far_top)
        near_share, far_share = jnp.exp2(lse - top), jnp.exp2(far_top - top)
        att_ref[mine, out_cols] = (
            (near_share * o_ref[mine, cols].astype(F32) + far_share * total[:, :PAIR])
            / (near_share + far_share * total[:, PAIR:])
        ).astype(BF16)

    groups = [(member, side) for member in range(members) for side in range(2)]

    def project(group):
        keys(group * HALO)
        values(group * HALO)

    project(0)
    for group, (member, side) in enumerate(groups):
        if group + 1 < len(groups):
            project(group + 1)
        for pair in range(STEP_COLS // PAIR):
            attend(member, pair, side)

    @pl.when(step == pl.num_programs(0) - 1)
    def _():
        for copy in late:
            copy.wait()
        copies = []
        chunks = [(member, at) for member in range(members) for at in range(0, rows, HALO)]

        def hidden_of(member, at):
            attended = att_ref[member * rows + at : member * rows + at + HALO]
            return latent_ref[member, at : at + HALO].astype(F32) + nn_dot(attended, wout_ref[...])

        hidden = hidden_of(*chunks[0])
        for index, (member, at) in enumerate(chunks):
            after = hidden_of(*chunks[index + 1]) if index + 1 < len(chunks) else None
            span = slice(at, at + HALO)
            normalized, inverse = normalize(hidden)
            normalized_ref[member, span] = normalized.astype(BF16)
            inverse_ref[member, span] = jnp.broadcast_to(inverse, (HALO, inverse_ref.shape[2]))
            normed_out = (normalized + noise_ref[member : member + 1].astype(F32)).astype(BF16)
            normed_out_ref[member, span] = normed_out
            predicted_ref[member, :, span] = nt_dot(padded_ref[...], normed_out).astype(BF16)
            for source, target in ((normalized_ref, normalized_hbm), (normed_out_ref, normed_out_hbm)):
                copy = pltpu.make_async_copy(
                    source.at[member, span], target.at[member, span], out_sem.at[len(copies)]
                )
                copy.start()
                copies.append(copy)
            hidden = after
        for copy in copies:
            copy.wait()


def far(place, q, o, lse, before, after, w_qkv, noise, dec, latent, w_out):
    members, rows, width = latent.shape
    tall = members * rows
    fields = dec.shape[0]
    padded = -(-fields // FIELD_TILE) * FIELD_TILE
    steps = width // STEP_COLS
    block = pl.BlockSpec((tall, STEP_COLS), lambda s: (0, s))
    whole2 = lambda s: (0, 0)
    whole3 = lambda s: (0, 0, 0)
    anywhere = pl.BlockSpec(memory_space=pltpu.HBM)
    return pl.pallas_call(
        far_body,
        grid=(steps,),
        in_specs=[
            *[pl.BlockSpec(memory_space=pltpu.SMEM)] * 3,
            block,
            block,
            block,
            pl.BlockSpec(memory_space=pltpu.VMEM),
            pl.BlockSpec(memory_space=pltpu.VMEM),
            pl.BlockSpec((width, STEP_COLS), lambda s: (0, steps + s)),
            pl.BlockSpec((width, STEP_COLS), lambda s: (0, 2 * steps + s)),
            pl.BlockSpec((members, width), whole2),
            pl.BlockSpec((fields, width), whole2),
            anywhere,
            anywhere,
        ],
        out_specs=[
            anywhere,
            pl.BlockSpec((members, rows, 128), whole3),
            anywhere,
            pl.BlockSpec((members, padded, rows), whole3),
            pl.BlockSpec((padded, width), whole2),
        ],
        out_shape=[
            jax.ShapeDtypeStruct((members, rows, width), BF16),
            jax.ShapeDtypeStruct((members, rows, 128), F32),
            jax.ShapeDtypeStruct((members, rows, width), BF16),
            jax.ShapeDtypeStruct((members, padded, rows), BF16),
            jax.ShapeDtypeStruct((padded, width), BF16),
        ],
        scratch_shapes=[
            pltpu.VMEM((members * 2 * HALO, width), BF16),
            pltpu.VMEM((2, HALO, HALO), F32),
            pltpu.VMEM((members * 2 * HALO, STEP_COLS), BF16),
            pltpu.VMEM((STEP_COLS // PAIR, members * 2, 2 * HALO, 2 * PAIR), BF16),
            pltpu.VMEM((tall, width), BF16),
            pltpu.VMEM((members, rows, width), BF16),
            pltpu.VMEM((width, width), BF16),
            pltpu.VMEM((members, rows, width), BF16),
            pltpu.VMEM((members, rows, width), BF16),
            pltpu.SemaphoreType.DMA((2,)),
            pltpu.SemaphoreType.DMA((2 * members * rows // HALO,)),
        ],
        compiler_params=pltpu.CompilerParams(vmem_limit_bytes=48 * MIB),
        cost_estimate=pl.CostEstimate(
            flops=15 * 10**9, bytes_accessed=22 * MIB, transcendentals=10**7
        ),
        name="far",
    )(*place, q, o, lse, before, after, w_qkv, w_qkv, noise, dec, latent, w_out)


def crps_body(
    place_ref, count_ref, pred_ref, target_ref, fw_ref, aw_ref, normed_hbm, grad_ref, pieces_ref, normed_ref, padded_ref, sem
):
    fetch = pltpu.make_async_copy(normed_hbm, normed_ref, sem)
    fetch.start()
    bands = count_ref.shape[0]
    first = lax.div(place_ref[0], bands)
    count = count_ref[lax.rem(place_ref[0], bands)]
    ensemble = pred_ref.shape[0] * pred_ref.shape[1]
    own_count = pred_ref.shape[1]
    lead = 1.0 / (ensemble - 1)
    fields, rows = padded_ref.shape
    real = target_ref.shape[0]
    padded_ref[...] = jnp.zeros_like(padded_ref)
    padded_ref[:real] = target_ref[...]
    width = normed_ref.shape[-1]
    target = padded_ref[...]
    used = lax.broadcasted_iota(jnp.int32, (1, rows), 1) < count
    shape = (fields, real)
    diagonal = iota(shape, 0) == iota(shape, 1)
    field_weight = jnp.sum(jnp.where(diagonal, fw_ref[...], 0.0), axis=1, keepdims=True)
    scale = field_weight * jnp.where(used, aw_ref[...], 0.0)

    def slope(gap):
        square = gap * gap + smooth_width * smooth_width
        root = lax.rsqrt(square)
        return gap * root, square * root

    loss = jnp.zeros((fields, rows), F32)
    grads = []
    for own in range(own_count):
        mine = pred_ref[first, own].astype(F32)
        pair_slope = jnp.zeros((fields, rows), F32)
        pair_abs = jnp.zeros((fields, rows), F32)
        for other in range(ensemble):
            s, a = slope(mine - pred_ref[other // own_count, other % own_count].astype(F32))
            pair_slope = pair_slope + s
            pair_abs = pair_abs + a
        s, a = slope(mine - target)
        grad = (scale * (s - pair_slope * lead)).astype(BF16)
        grad_ref[own] = grad
        loss = loss + scale * (a - pair_abs * (0.5 * lead))
        grads.append(grad)
    fetch.wait()
    weight = nn_dot(grads[0], normed_ref[0])
    for own in range(1, own_count):
        weight = weight + nn_dot(grads[own], normed_ref[own])
    tiles = width // 128
    for r in range(0, fields, 8):
        for c in range(tiles):
            piece = weight[r : r + 8, c * 128 : c * 128 + 128]
            pieces_ref[r // 8 * tiles + c] = piece.astype(BF16)
    used_pieces = fields // 8 * tiles
    whole = jnp.sum(jnp.sum(loss, axis=0, keepdims=True), axis=1, keepdims=True)
    high = whole.astype(BF16)
    rest = (whole - high.astype(F32)).astype(BF16)
    row = lax.broadcasted_iota(jnp.int32, (8, 128), 0)
    both = jnp.where(row == 0, high.astype(F32), jnp.where(row == 1, rest.astype(F32), 0.0))
    pieces_ref[used_pieces] = both.astype(BF16)
    pieces_ref[used_pieces + 1 :] = jnp.zeros_like(pieces_ref[used_pieces + 1 :])


def crps(place, preds, targets, field_weight, area_weight, normed_out, peers):
    _, own_count, fields, rows = preds.shape
    vmem = pl.BlockSpec(memory_space=pltpu.VMEM)
    return pl.pallas_call(
        crps_body,
        in_specs=[pl.BlockSpec(memory_space=pltpu.SMEM)] * 2
        + [vmem] * 4
        + [pl.BlockSpec(memory_space=pltpu.HBM)],
        out_specs=[vmem] * 2,
        out_shape=[
            jax.ShapeDtypeStruct((own_count, fields, rows), BF16),
            jax.ShapeDtypeStruct((peers, 8, 128), BF16),
        ],
        scratch_shapes=[
            pltpu.VMEM(normed_out.shape, BF16),
            pltpu.VMEM((fields, rows), F32),
            pltpu.SemaphoreType.DMA(()),
        ],
        compiler_params=pltpu.CompilerParams(vmem_limit_bytes=52 * MIB),
        cost_estimate=pl.CostEstimate(
            flops=4 * 10**8, bytes_accessed=4 * MIB, transcendentals=10**6
        ),
        name="crps",
    )(*place[:2], preds, targets, field_weight, area_weight, normed_out)


def backward_body(grad_ref, dec_ref, normalized_ref, inverse_ref, out_ref):
    grad_norm = tn_dot(grad_ref[...], dec_ref[...])
    normalized = normalized_ref[...].astype(F32)
    inverse = inverse_ref[...][:, :1]
    mean = jnp.mean(grad_norm, axis=-1, keepdims=True)
    dotted = jnp.mean(grad_norm * normalized, axis=-1, keepdims=True)
    out_ref[...] = (inverse * (grad_norm - mean - normalized * dotted)).astype(BF16)


def backward(grad, dec, normalized, inverse):
    members, fields, rows = grad.shape
    width = dec.shape[1]
    return pl.pallas_call(
        backward_body,
        grid=(members,),
        in_specs=[
            pl.BlockSpec((None, fields, rows), lambda m: (m, 0, 0)),
            pl.BlockSpec((fields, width), lambda m: (0, 0)),
            pl.BlockSpec((None, rows, width), lambda m: (m, 0, 0)),
            pl.BlockSpec((None, rows, 128), lambda m: (m, 0, 0)),
        ],
        out_specs=pl.BlockSpec((None, rows, width), lambda m: (m, 0, 0)),
        out_shape=jax.ShapeDtypeStruct((members, rows, width), BF16),
        compiler_params=pltpu.CompilerParams(vmem_limit_bytes=60 * MIB),
        cost_estimate=pl.CostEstimate(
            flops=5 * 10**8, bytes_accessed=5 * MIB, transcendentals=0
        ),
        name="backward",
    )(grad, dec, normalized, inverse)


def summed(pieces, loss_piece):
    axes = ("mem", "lat")
    parts = lax.all_to_all(pieces, axes, split_axis=0, concat_axis=0, tiled=True)
    mine = jnp.sum(parts.astype(F32), axis=0)
    loss = mine[0] + mine[1]
    rounded = lax.reduce_precision(loss, 8, 7)
    row = lax.broadcasted_iota(jnp.int32, mine.shape, 0)
    as_loss = jnp.where(row == 0, rounded, jnp.where(row == 1, loss - rounded, 0.0))
    mine = jnp.where(lax.axis_index(axes) == loss_piece, as_loss, mine).astype(BF16)
    spread = jnp.broadcast_to(mine[None], pieces.shape)
    return lax.all_to_all(spread, axes, split_axis=0, concat_axis=0, tiled=True)


def local(
    latent,
    member_noise,
    w_qkv,
    w_out,
    dec_weight,
    targets,
    area_weight,
    field_weight,
    band_count,
    band_window,
):
    members, rows, width = latent.shape
    bands = lax.axis_size("lat")
    fields = dec_weight.shape[0]
    up = [(i, i + 1) for i in range(bands - 1)]
    down = [(j, i) for i, j in up]
    before = lax.ppermute(latent[:, rows - HALO :], "lat", up)
    after = lax.ppermute(latent[:, :HALO], "lat", down)
    place = (lax.axis_index(("mem", "lat")).reshape(1), band_count, band_window)
    q, o, lse = near(place, latent, w_qkv)
    normalized, inverse, normed_out, predicted, dec = far(
        place, q, o, lse, before, after, w_qkv, member_noise, dec_weight, latent, w_out
    )
    preds = lax.all_gather(predicted, "mem", axis=0)
    peers = lax.axis_size("mem") * bands
    grad, pieces = crps(
        place, preds, targets, field_weight[None, :], area_weight[None, :], normed_out, peers
    )
    tiles = width // 128
    groups = preds.shape[2] // 8
    used = groups * tiles
    total = summed(pieces, used).astype(F32) / (rows * bands)
    grad_hidden = backward(grad, dec, normalized, inverse)
    weight_sum = total[:used].reshape(groups, tiles, 8, 128).transpose(0, 2, 1, 3)
    return (
        grad_hidden,
        weight_sum.reshape(groups * 8, width)[:fields],
        total[used, 0, 0] + total[used, 1, 0],
    )


def solution(mesh):
    return jax.shard_map(
        local,
        mesh=mesh,
        in_specs=(
            P("mem", "lat", None),
            P("mem", None),
            P(),
            P(),
            P(),
            P(None, "lat"),
            P("lat"),
            P(),
            P(),
            P("lat", None),
        ),
        out_specs=(P("mem", "lat", None), P(), P()),
        check_vma=False,
    )
```

```python
import functools

import jax
import jax.numpy as jnp
from jax import lax
from jax.experimental import pallas as pl
from jax.experimental.pallas import tpu as pltpu
from jax.sharding import PartitionSpec as P

HEAD_DIM = 64
HALO = 256
LOG2E = 1.4426950408889634

norm_eps = 1e-05
smooth_width = 0.25
F32 = jnp.float32
BF16 = jnp.bfloat16
MIB = 1024 * 1024


def normalize(x):
    mean = jnp.mean(x, axis=-1, keepdims=True)
    centred = x - mean
    var = jnp.mean(centred * centred, axis=-1, keepdims=True)
    inverse = lax.rsqrt(var + norm_eps)
    return centred * inverse, inverse


def nt_dot(a, b):
    return lax.dot_general(a, b, (((1,), (1,)), ((), ())), preferred_element_type=F32)


def tn_dot(a, b):
    return lax.dot_general(a, b, (((0,), (0,)), ((), ())), preferred_element_type=F32)


def nn_dot(a, b):
    return jnp.dot(a, b, preferred_element_type=F32)


QB = 256
STEP_COLS = 256
PAIR = 2 * HEAD_DIM
FIELD_TILE = 8
LOSS_PIECE = 104
NEVER = -1e30


def bias_of(q_row, k_row, place_ref, count_ref, window_ref, rows):
    bands = count_ref.shape[0]
    band = lax.rem(place_ref[0], bands)
    offset = k_row - q_row
    in_window = (offset >= -window_ref[0, 0]) & (offset <= window_ref[0, 1])
    before = jnp.where(band > 0, count_ref[jnp.maximum(band - 1, 0)], 0)
    after = jnp.where(band < bands - 1, count_ref[jnp.minimum(band + 1, bands - 1)], 0)
    end = jnp.where(
        k_row < 0, before - rows, jnp.where(k_row < rows, count_ref[band], after + rows)
    )
    return jnp.where((in_window & (k_row < end)) | (offset == 0), 0.0, NEVER)


def iota(shape, axis):
    return lax.broadcasted_iota(jnp.int32, shape, axis)


def pair_scores(q, keys, bias, low):
    zero = jnp.zeros_like(q)
    both = jnp.concatenate([jnp.where(low, q, zero), jnp.where(low, zero, q)], axis=0)
    scores = nt_dot(both, keys)
    weights, tops = [], []
    for half in range(2):
        part = scores[half * q.shape[0] : (half + 1) * q.shape[0]] + bias
        top = jnp.max(part, axis=-1, keepdims=True)
        weights.append(jnp.exp2(part - top).astype(BF16))
        tops.append(top)
    return jnp.concatenate(weights, axis=1), jnp.where(low, tops[0], tops[1])


def set_ones(ref, low):
    half = ref.shape[-2] // 2
    one = jnp.ones((half, PAIR), BF16)
    for pair in range(ref.shape[0]):
        for group in range(ref.shape[1]):
            ref[pair, group, :half, PAIR:] = jnp.where(low, one, 0.0).astype(BF16)
            ref[pair, group, half:, PAIR:] = jnp.where(low, 0.0, one).astype(BF16)


def set_values(ref, group, at, value, low):
    half, count = ref.shape[-2] // 2, value.shape[0]
    for pair in range(ref.shape[0]):
        own = value[:, pair * PAIR : (pair + 1) * PAIR]
        zero = jnp.zeros_like(own)
        ref[pair, group, at : at + count, :PAIR] = jnp.where(low, own, zero)
        ref[pair, group, half + at : half + at + count, :PAIR] = jnp.where(low, zero, own)


def near_body(
    place_ref, count_ref, window_ref, latent_ref, wq_ref, wk_ref, wv_ref, q_ref, o_ref, lse_ref, normed_ref, bias_ref, k_ref, vx_ref
):
    step = pl.program_id(0)
    rows = bias_ref.shape[0]
    members = latent_ref.shape[0] // rows
    low = iota((1, PAIR), 1) < HEAD_DIM

    @pl.when(step == 0)
    def _():
        normed_ref[...] = normalize(latent_ref[...].astype(F32))[0].astype(BF16)
        shape = bias_ref.shape
        bias_ref[...] = bias_of(iota(shape, 0), iota(shape, 1), place_ref, count_ref, window_ref, rows)
        set_ones(vx_ref, low)


    def queries(at):
        span = slice(at, at + QB)
        q_ref[span] = (
            nn_dot(normed_ref[span], wq_ref[...]) * (HEAD_DIM ** (-0.5) * LOG2E)
        ).astype(BF16)

    def keys(at):
        span = slice(at, at + QB)
        k_ref[span] = nn_dot(normed_ref[span], wk_ref[...]).astype(BF16)

    def values(at):
        span = slice(at, at + QB)
        value = nn_dot(normed_ref[span], wv_ref[...]).astype(BF16)
        set_values(vx_ref, at // rows, at % rows, value, low)

    def attend(member, pair, block):
        cols = slice(pair * PAIR, (pair + 1) * PAIR)
        here = slice(block * QB, (block + 1) * QB)
        mine = slice(member * rows + block * QB, member * rows + (block + 1) * QB)
        reach = slice(member * rows, (member + 1) * rows)
        weight, top = pair_scores(q_ref[mine, cols], k_ref[reach, cols], bias_ref[here], low)
        total = nn_dot(weight, vx_ref[pair, member])
        summed_weight = total[:, PAIR:]
        o_ref[mine, cols] = (total[:, :PAIR] / summed_weight).astype(BF16)
        lse_ref[mine, cols] = top + jnp.log2(summed_weight)

    pairs, blocks = STEP_COLS // PAIR, rows // QB
    project = [
        [(f, member * rows + at) for f in (keys, values, queries) for at in range(0, rows, QB)]
        for member in range(members)
    ]
    for f, at in project[0]:
        f(at)
    for member in range(members):
        later = project[member + 1] if member + 1 < members else []
        tiles = [(pair, block) for pair in range(pairs) for block in range(blocks)]
        share = -(-len(later) // len(tiles))
        for i, (pair, block) in enumerate(tiles):
            for f, at in later[i * share : (i + 1) * share]:
                f(at)
            attend(member, pair, block)


def near(place, latent, w_qkv):
    members, rows, width = latent.shape
    tall = members * rows
    steps = width // STEP_COLS
    block = pl.BlockSpec((tall, STEP_COLS), lambda s: (0, s))
    return pl.pallas_call(
        near_body,
        grid=(steps,),
        in_specs=[
            *[pl.BlockSpec(memory_space=pltpu.SMEM)] * 3,
            pl.BlockSpec((tall, width), lambda s: (0, 0), pipeline_mode=pl.Buffered(1)),
            pl.BlockSpec((width, STEP_COLS), lambda s: (0, s)),
            pl.BlockSpec((width, STEP_COLS), lambda s: (0, steps + s)),
            pl.BlockSpec((width, STEP_COLS), lambda s: (0, 2 * steps + s)),
        ],
        out_specs=[block, block, block],
        out_shape=[
            jax.ShapeDtypeStruct((tall, width), BF16),
            jax.ShapeDtypeStruct((tall, width), BF16),
            jax.ShapeDtypeStruct((tall, width), F32),
        ],
        scratch_shapes=[
            pltpu.VMEM((tall, width), BF16),
            pltpu.VMEM((rows, rows), F32),
            pltpu.VMEM((tall, STEP_COLS), BF16),
            pltpu.VMEM((STEP_COLS // PAIR, members, 2 * rows, 2 * PAIR), BF16),
        ],
        compiler_params=pltpu.CompilerParams(vmem_limit_bytes=60 * MIB),
        cost_estimate=pl.CostEstimate(
            flops=20 * 10**9, bytes_accessed=16 * MIB, transcendentals=10**7
        ),
        name="near",
    )(*place, latent.reshape(tall, width), w_qkv, w_qkv, w_qkv)


def far_body(
    place_ref,
    count_ref,
    window_ref,
    q_ref,
    o_ref,
    lse_ref,
    before_ref,
    after_ref,
    wk_ref,
    wv_ref,
    noise_ref,
    dec_ref,
    latent_hbm,
    wout_hbm,
    normalized_hbm,
    inverse_ref,
    normed_out_hbm,
    predicted_ref,
    padded_ref,
    halo_ref,
    bias_ref,
    k_ref,
    vx_ref,
    att_ref,
    latent_ref,
    wout_ref,
    normalized_ref,
    normed_out_ref,
    sem,
    out_sem,
):
    step = pl.program_id(0)
    members, _, width = before_ref.shape
    tall = q_ref.shape[0]
    rows = tall // members
    low = iota((1, PAIR), 1) < HEAD_DIM
    late = [
        pltpu.make_async_copy(latent_hbm, latent_ref, sem.at[0]),
        pltpu.make_async_copy(wout_hbm, wout_ref, sem.at[1]),
    ]

    @pl.when(step == 0)
    def _():
        for copy in late:
            copy.start()
        padded_ref[...] = jnp.zeros_like(padded_ref)
        padded_ref[: dec_ref.shape[0]] = dec_ref[...]
        for member in range(members):
            for side, source in enumerate((before_ref, after_ref)):
                at = (2 * member + side) * HALO
                halo_ref[at : at + HALO] = normalize(source[member].astype(F32))[0].astype(BF16)
        shape = (HALO, HALO)
        bias_ref[0] = bias_of(iota(shape, 0), iota(shape, 1) - HALO, place_ref, count_ref, window_ref, rows)
        bias_ref[1] = bias_of(iota(shape, 0) + rows - HALO, iota(shape, 1) + rows, place_ref, count_ref, window_ref, rows)
        set_ones(vx_ref, low)

    def keys(at):
        span = slice(at, at + HALO)
        k_ref[span] = nn_dot(halo_ref[span], wk_ref[...]).astype(BF16)

    def values(at):
        span = slice(at, at + HALO)
        value = nn_dot(halo_ref[span], wv_ref[...]).astype(BF16)
        set_values(vx_ref, at // HALO, 0, value, low)

    def attend(member, pair, side):
        cols = slice(pair * PAIR, (pair + 1) * PAIR)
        out_cols = pl.ds(pl.multiple_of(step * STEP_COLS + pair * PAIR, PAIR), PAIR)
        at = member * rows + side * (rows - HALO)
        mine = slice(at, at + HALO)
        reach = slice((2 * member + side) * HALO, (2 * member + side + 1) * HALO)
        lse = lse_ref[mine, cols]
        weight, far_top = pair_scores(q_ref[mine, cols], k_ref[reach, cols], bias_ref[side], low)
        total = nn_dot(weight, vx_ref[pair, 2 * member + side])
        top = jnp.maximum(lse, far_top)
        near_share, far_share = jnp.exp2(lse - top), jnp.exp2(far_top - top)
        att_ref[mine, out_cols] = (
            (near_share * o_ref[mine, cols].astype(F32) + far_share * total[:, :PAIR])
            / (near_share + far_share * total[:, PAIR:])
        ).astype(BF16)

    groups = [(member, side) for member in range(members) for side in range(2)]

    def project(group):
        keys(group * HALO)
        values(group * HALO)

    project(0)
    for group, (member, side) in enumerate(groups):
        if group + 1 < len(groups):
            project(group + 1)
        for pair in range(STEP_COLS // PAIR):
            attend(member, pair, side)

    @pl.when(step == pl.num_programs(0) - 1)
    def _():
        for copy in late:
            copy.wait()
        copies = []
        chunks = [(member, at) for member in range(members) for at in range(0, rows, HALO)]

        def hidden_of(member, at):
            attended = att_ref[member * rows + at : member * rows + at + HALO]
            return latent_ref[member, at : at + HALO].astype(F32) + nn_dot(attended, wout_ref[...])

        hidden = hidden_of(*chunks[0])
        for index, (member, at) in enumerate(chunks):
            after = hidden_of(*chunks[index + 1]) if index + 1 < len(chunks) else None
            span = slice(at, at + HALO)
            normalized, inverse = normalize(hidden)
            normalized_ref[member, span] = normalized.astype(BF16)
            inverse_ref[member, span] = jnp.broadcast_to(inverse, (HALO, inverse_ref.shape[2]))
            normed_out = (normalized + noise_ref[member : member + 1].astype(F32)).astype(BF16)
            normed_out_ref[member, span] = normed_out
            predicted_ref[member, :, span] = nt_dot(padded_ref[...], normed_out).astype(BF16)
            for source, target in ((normalized_ref, normalized_hbm), (normed_out_ref, normed_out_hbm)):
                copy = pltpu.make_async_copy(
                    source.at[member, span], target.at[member, span], out_sem.at[len(copies)]
                )
                copy.start()
                copies.append(copy)
            hidden = after
        for copy in copies:
            copy.wait()


def far(place, q, o, lse, before, after, w_qkv, noise, dec, latent, w_out):
    members, rows, width = latent.shape
    tall = members * rows
    fields = dec.shape[0]
    padded = -(-fields // FIELD_TILE) * FIELD_TILE
    steps = width // STEP_COLS
    block = pl.BlockSpec((tall, STEP_COLS), lambda s: (0, s))
    whole2 = lambda s: (0, 0)
    whole3 = lambda s: (0, 0, 0)
    anywhere = pl.BlockSpec(memory_space=pltpu.HBM)
    return pl.pallas_call(
        far_body,
        grid=(steps,),
        in_specs=[
            *[pl.BlockSpec(memory_space=pltpu.SMEM)] * 3,
            block,
            block,
            block,
            pl.BlockSpec(memory_space=pltpu.VMEM),
            pl.BlockSpec(memory_space=pltpu.VMEM),
            pl.BlockSpec((width, STEP_COLS), lambda s: (0, steps + s)),
            pl.BlockSpec((width, STEP_COLS), lambda s: (0, 2 * steps + s)),
            pl.BlockSpec((members, width), whole2),
            pl.BlockSpec((fields, width), whole2),
            anywhere,
            anywhere,
        ],
        out_specs=[
            anywhere,
            pl.BlockSpec((members, rows, 128), whole3),
            anywhere,
            pl.BlockSpec((members, padded, rows), whole3),
            pl.BlockSpec((padded, width), whole2),
        ],
        out_shape=[
            jax.ShapeDtypeStruct((members, rows, width), BF16),
            jax.ShapeDtypeStruct((members, rows, 128), F32),
            jax.ShapeDtypeStruct((members, rows, width), BF16),
            jax.ShapeDtypeStruct((members, padded, rows), BF16),
            jax.ShapeDtypeStruct((padded, width), BF16),
        ],
        scratch_shapes=[
            pltpu.VMEM((members * 2 * HALO, width), BF16),
            pltpu.VMEM((2, HALO, HALO), F32),
            pltpu.VMEM((members * 2 * HALO, STEP_COLS), BF16),
            pltpu.VMEM((STEP_COLS // PAIR, members * 2, 2 * HALO, 2 * PAIR), BF16),
            pltpu.VMEM((tall, width), BF16),
            pltpu.VMEM((members, rows, width), BF16),
            pltpu.VMEM((width, width), BF16),
            pltpu.VMEM((members, rows, width), BF16),
            pltpu.VMEM((members, rows, width), BF16),
            pltpu.SemaphoreType.DMA((2,)),
            pltpu.SemaphoreType.DMA((2 * members * rows // HALO,)),
        ],
        compiler_params=pltpu.CompilerParams(vmem_limit_bytes=48 * MIB),
        cost_estimate=pl.CostEstimate(
            flops=15 * 10**9, bytes_accessed=22 * MIB, transcendentals=10**7
        ),
        name="far",
    )(*place, q, o, lse, before, after, w_qkv, w_qkv, noise, dec, latent, w_out)


def crps_body(
    place_ref, count_ref, pred_ref, target_ref, fw_ref, aw_ref, normed_hbm, grad_ref, pieces_ref, normed_ref, padded_ref, sem
):
    fetch = pltpu.make_async_copy(normed_hbm, normed_ref, sem)
    fetch.start()
    bands = count_ref.shape[0]
    first = lax.div(place_ref[0], bands)
    count = count_ref[lax.rem(place_ref[0], bands)]
    ensemble = pred_ref.shape[0] * pred_ref.shape[1]
    own_count = pred_ref.shape[1]
    lead = 1.0 / (ensemble - 1)
    fields, rows = padded_ref.shape
    real = target_ref.shape[0]
    padded_ref[...] = jnp.zeros_like(padded_ref)
    padded_ref[:real] = target_ref[...]
    width = normed_ref.shape[-1]
    target = padded_ref[...]
    used = lax.broadcasted_iota(jnp.int32, (1, rows), 1) < count
    shape = (fields, real)
    diagonal = iota(shape, 0) == iota(shape, 1)
    field_weight = jnp.sum(jnp.where(diagonal, fw_ref[...], 0.0), axis=1, keepdims=True)
    scale = field_weight * jnp.where(used, aw_ref[...], 0.0)

    def slope(gap):
        square = gap * gap + smooth_width * smooth_width
        root = lax.rsqrt(square)
        return gap * root, square * root

    loss = jnp.zeros((fields, rows), F32)
    grads = []
    for own in range(own_count):
        mine = pred_ref[first, own].astype(F32)
        pair_slope = jnp.zeros((fields, rows), F32)
        pair_abs = jnp.zeros((fields, rows), F32)
        for other in range(ensemble):
            s, a = slope(mine - pred_ref[other // own_count, other % own_count].astype(F32))
            pair_slope = pair_slope + s
            pair_abs = pair_abs + a
        s, a = slope(mine - target)
        grad = (scale * (s - pair_slope * lead)).astype(BF16)
        grad_ref[own] = grad
        loss = loss + scale * (a - pair_abs * (0.5 * lead))
        grads.append(grad)
    fetch.wait()
    weight = nn_dot(grads[0], normed_ref[0])
    for own in range(1, own_count):
        weight = weight + nn_dot(grads[own], normed_ref[own])
    tiles = width // 128
    for r in range(0, fields, 8):
        for c in range(tiles):
            piece = weight[r : r + 8, c * 128 : c * 128 + 128]
            pieces_ref[r // 8 * tiles + c] = piece.astype(BF16)
    used_pieces = LOSS_PIECE
    whole = jnp.sum(jnp.sum(loss, axis=0, keepdims=True), axis=1, keepdims=True)
    high = whole.astype(BF16)
    rest = (whole - high.astype(F32)).astype(BF16)
    row = lax.broadcasted_iota(jnp.int32, (8, 128), 0)
    both = jnp.where(row == 0, high.astype(F32), jnp.where(row == 1, rest.astype(F32), 0.0))
    pieces_ref[used_pieces] = both.astype(BF16)
    pieces_ref[used_pieces + 1 :] = jnp.zeros_like(pieces_ref[used_pieces + 1 :])


def crps(place, preds, targets, field_weight, area_weight, normed_out, peers):
    _, own_count, fields, rows = preds.shape
    vmem = pl.BlockSpec(memory_space=pltpu.VMEM)
    return pl.pallas_call(
        crps_body,
        in_specs=[pl.BlockSpec(memory_space=pltpu.SMEM)] * 2
        + [vmem] * 4
        + [pl.BlockSpec(memory_space=pltpu.HBM)],
        out_specs=[vmem] * 2,
        out_shape=[
            jax.ShapeDtypeStruct((own_count, fields, rows), BF16),
            jax.ShapeDtypeStruct((peers, 8, 128), BF16),
        ],
        scratch_shapes=[
            pltpu.VMEM(normed_out.shape, BF16),
            pltpu.VMEM((fields, rows), F32),
            pltpu.SemaphoreType.DMA(()),
        ],
        compiler_params=pltpu.CompilerParams(vmem_limit_bytes=52 * MIB),
        cost_estimate=pl.CostEstimate(
            flops=4 * 10**8, bytes_accessed=4 * MIB, transcendentals=10**6
        ),
        name="crps",
    )(*place[:2], preds, targets, field_weight, area_weight, normed_out)


def backward_body(grad_ref, dec_ref, normalized_ref, inverse_ref, out_ref):
    grad_norm = tn_dot(grad_ref[...], dec_ref[...])
    normalized = normalized_ref[...].astype(F32)
    inverse = inverse_ref[...][:, :1]
    mean = jnp.mean(grad_norm, axis=-1, keepdims=True)
    dotted = jnp.mean(grad_norm * normalized, axis=-1, keepdims=True)
    out_ref[...] = (inverse * (grad_norm - mean - normalized * dotted)).astype(BF16)


def backward(grad, dec, normalized, inverse):
    members, fields, rows = grad.shape
    width = dec.shape[1]
    return pl.pallas_call(
        backward_body,
        grid=(members,),
        in_specs=[
            pl.BlockSpec((None, fields, rows), lambda m: (m, 0, 0)),
            pl.BlockSpec((fields, width), lambda m: (0, 0)),
            pl.BlockSpec((None, rows, width), lambda m: (m, 0, 0)),
            pl.BlockSpec((None, rows, 128), lambda m: (m, 0, 0)),
        ],
        out_specs=pl.BlockSpec((None, rows, width), lambda m: (m, 0, 0)),
        out_shape=jax.ShapeDtypeStruct((members, rows, width), BF16),
        compiler_params=pltpu.CompilerParams(vmem_limit_bytes=32 * MIB),
        cost_estimate=pl.CostEstimate(
            flops=5 * 10**8, bytes_accessed=5 * MIB, transcendentals=0
        ),
        name="backward",
    )(grad, dec, normalized, inverse)


def share_body(rank_ref, parts_ref, spread_ref):
    peers = parts_ref.shape[0]
    mine = jnp.sum(parts_ref[...].astype(F32), axis=0)
    row = iota(mine.shape, 0)
    loss = jnp.sum(jnp.where(row < 2, mine, 0.0), axis=0, keepdims=True)
    rounded = loss.astype(BF16).astype(F32)
    as_loss = jnp.where(row == 0, rounded, jnp.where(row == 1, loss - rounded, 0.0))
    mine = jnp.where(rank_ref[0] == LOSS_PIECE, as_loss, mine).astype(BF16)
    spread_ref[...] = jnp.broadcast_to(mine[None], spread_ref.shape)


def finish_body(pieces_ref, weight_ref, loss_ref, *, tokens):
    fields, width = weight_ref.shape
    tiles = width // 128
    for r in range(0, fields, 8):
        count = min(8, fields - r)
        for c in range(tiles):
            piece = pieces_ref[r // 8 * tiles + c].astype(F32) * (1.0 / tokens)
            weight_ref[r : r + count, c * 128 : c * 128 + 128] = piece[:count]
    loss = jnp.sum(pieces_ref[LOSS_PIECE].astype(F32), axis=0, keepdims=True) * (1.0 / tokens)
    loss_ref[0, 0] = jnp.max(loss)


def summed(place, pieces, fields, width, tokens):
    axes = ("mem", "lat")
    vmem = pl.BlockSpec(memory_space=pltpu.VMEM)
    smem = pl.BlockSpec(memory_space=pltpu.SMEM)
    params = pltpu.CompilerParams(vmem_limit_bytes=16 * MIB)
    parts = lax.all_to_all(pieces, axes, split_axis=0, concat_axis=0, tiled=True)
    spread = pl.pallas_call(
        share_body,
        in_specs=[smem, vmem],
        out_specs=vmem,
        out_shape=jax.ShapeDtypeStruct(pieces.shape, BF16),
        compiler_params=params,
        name="share",
    )(place[0], parts)
    whole = lax.all_to_all(spread, axes, split_axis=0, concat_axis=0, tiled=True)
    return pl.pallas_call(
        functools.partial(finish_body, tokens=tokens),
        in_specs=[vmem],
        out_specs=[vmem, smem],
        out_shape=[
            jax.ShapeDtypeStruct((fields, width), F32),
            jax.ShapeDtypeStruct((1, 1), F32),
        ],
        compiler_params=params,
        name="finish",
    )(whole)


def local(
    latent,
    member_noise,
    w_qkv,
    w_out,
    dec_weight,
    targets,
    area_weight,
    field_weight,
    band_count,
    band_window,
):
    members, rows, width = latent.shape
    bands = lax.axis_size("lat")
    fields = dec_weight.shape[0]
    up = [(i, i + 1) for i in range(bands - 1)]
    down = [(j, i) for i, j in up]
    before = lax.ppermute(latent[:, rows - HALO :], "lat", up)
    after = lax.ppermute(latent[:, :HALO], "lat", down)
    place = (lax.axis_index(("mem", "lat")).reshape(1), band_count, band_window)
    q, o, lse = near(place, latent, w_qkv)
    normalized, inverse, normed_out, predicted, dec = far(
        place, q, o, lse, before, after, w_qkv, member_noise, dec_weight, latent, w_out
    )
    preds = lax.all_gather(predicted, "mem", axis=0)
    peers = lax.axis_size("mem") * bands
    grad, pieces = crps(
        place, preds, targets, field_weight[None, :], area_weight[None, :], normed_out, peers
    )
    weight, loss = summed(place, pieces, fields, width, rows * bands)
    grad_hidden = backward(grad, dec, normalized, inverse)
    return grad_hidden, weight, loss.reshape(())


def solution(mesh):
    return jax.shard_map(
        local,
        mesh=mesh,
        in_specs=(
            P("mem", "lat", None),
            P("mem", None),
            P(),
            P(),
            P(),
            P(None, "lat"),
            P("lat"),
            P(),
            P(),
            P("lat", None),
        ),
        out_specs=(P("mem", "lat", None), P(), P()),
        check_vma=False,
    )
```

```python
import functools

import jax
import jax.numpy as jnp
from jax import lax
from jax.experimental import pallas as pl
from jax.experimental.pallas import tpu as pltpu
from jax.sharding import PartitionSpec as P

HEAD_DIM = 64
HALO = 256
LOG2E = 1.4426950408889634

norm_eps = 1e-05
smooth_width = 0.25
F32 = jnp.float32
BF16 = jnp.bfloat16
MIB = 1024 * 1024


def normalize(x):
    mean = jnp.mean(x, axis=-1, keepdims=True)
    centred = x - mean
    var = jnp.mean(centred * centred, axis=-1, keepdims=True)
    inverse = lax.rsqrt(var + norm_eps)
    return centred * inverse, inverse


def nt_dot(a, b):
    return lax.dot_general(a, b, (((1,), (1,)), ((), ())), preferred_element_type=F32)


def tn_dot(a, b):
    return lax.dot_general(a, b, (((0,), (0,)), ((), ())), preferred_element_type=F32)


def nn_dot(a, b):
    return jnp.dot(a, b, preferred_element_type=F32)


QB = 256
STEP_COLS = 256
PAIR = 2 * HEAD_DIM
FIELD_TILE = 8
LOSS_PIECE = 104
NEVER = -1e30


def bias_of(q_row, k_row, place_ref, count_ref, window_ref, rows):
    bands = count_ref.shape[0]
    band = lax.rem(place_ref[0], bands)
    offset = k_row - q_row
    in_window = (offset >= -window_ref[0, 0]) & (offset <= window_ref[0, 1])
    before = jnp.where(band > 0, count_ref[jnp.maximum(band - 1, 0)], 0)
    after = jnp.where(band < bands - 1, count_ref[jnp.minimum(band + 1, bands - 1)], 0)
    end = jnp.where(
        k_row < 0, before - rows, jnp.where(k_row < rows, count_ref[band], after + rows)
    )
    return jnp.where((in_window & (k_row < end)) | (offset == 0), 0.0, NEVER)


def iota(shape, axis):
    return lax.broadcasted_iota(jnp.int32, shape, axis)


def pair_scores(q, keys, bias, low):
    zero = jnp.zeros_like(q)
    both = jnp.concatenate([jnp.where(low, q, zero), jnp.where(low, zero, q)], axis=0)
    scores = nt_dot(both, keys)
    weights, tops = [], []
    for half in range(2):
        part = scores[half * q.shape[0] : (half + 1) * q.shape[0]] + bias
        top = jnp.max(part, axis=-1, keepdims=True)
        weights.append(jnp.exp2(part - top).astype(BF16))
        tops.append(top)
    return jnp.concatenate(weights, axis=1), jnp.where(low, tops[0], tops[1])


def set_ones(ref, low):
    half = ref.shape[-2] // 2
    one = jnp.ones((half, PAIR), BF16)
    for pair in range(ref.shape[0]):
        for group in range(ref.shape[1]):
            ref[pair, group, :half, PAIR:] = jnp.where(low, one, 0.0).astype(BF16)
            ref[pair, group, half:, PAIR:] = jnp.where(low, 0.0, one).astype(BF16)


def set_values(ref, group, at, value, low):
    half, count = ref.shape[-2] // 2, value.shape[0]
    for pair in range(ref.shape[0]):
        own = value[:, pair * PAIR : (pair + 1) * PAIR]
        zero = jnp.zeros_like(own)
        ref[pair, group, at : at + count, :PAIR] = jnp.where(low, own, zero)
        ref[pair, group, half + at : half + at + count, :PAIR] = jnp.where(low, zero, own)


def near_body(
    place_ref, count_ref, window_ref, latent_ref, wq_ref, wk_ref, wv_ref, q_ref, o_ref, lse_ref, normed_ref, bias_ref, k_ref, vx_ref
):
    step = pl.program_id(0)
    rows = bias_ref.shape[0]
    members = latent_ref.shape[0] // rows
    low = iota((1, PAIR), 1) < HEAD_DIM

    @pl.when(step == 0)
    def _():
        normed_ref[...] = normalize(latent_ref[...].astype(F32))[0].astype(BF16)
        shape = bias_ref.shape
        bias_ref[...] = bias_of(iota(shape, 0), iota(shape, 1), place_ref, count_ref, window_ref, rows)
        set_ones(vx_ref, low)


    def queries(at):
        span = slice(at, at + QB)
        q_ref[span] = (
            nn_dot(normed_ref[span], wq_ref[...]) * (HEAD_DIM ** (-0.5) * LOG2E)
        ).astype(BF16)

    def keys(at):
        span = slice(at, at + QB)
        k_ref[span] = nn_dot(normed_ref[span], wk_ref[...]).astype(BF16)

    def values(at):
        span = slice(at, at + QB)
        value = nn_dot(normed_ref[span], wv_ref[...]).astype(BF16)
        set_values(vx_ref, at // rows, at % rows, value, low)

    def attend(member, pair, block):
        cols = slice(pair * PAIR, (pair + 1) * PAIR)
        here = slice(block * QB, (block + 1) * QB)
        mine = slice(member * rows + block * QB, member * rows + (block + 1) * QB)
        reach = slice(member * rows, (member + 1) * rows)
        weight, top = pair_scores(q_ref[mine, cols], k_ref[reach, cols], bias_ref[here], low)
        total = nn_dot(weight, vx_ref[pair, member])
        summed_weight = total[:, PAIR:]
        o_ref[mine, cols] = (total[:, :PAIR] / summed_weight).astype(BF16)
        lse_ref[mine, cols] = top + jnp.log2(summed_weight)

    pairs, blocks = STEP_COLS // PAIR, rows // QB
    project = [
        [(f, member * rows + at) for f in (keys, values, queries) for at in range(0, rows, QB)]
        for member in range(members)
    ]
    for f, at in project[0]:
        f(at)
    for member in range(members):
        later = project[member + 1] if member + 1 < members else []
        tiles = [(pair, block) for pair in range(pairs) for block in range(blocks)]
        share = -(-len(later) // len(tiles))
        for i, (pair, block) in enumerate(tiles):
            for f, at in later[i * share : (i + 1) * share]:
                f(at)
            attend(member, pair, block)


def near(place, latent, w_qkv):
    members, rows, width = latent.shape
    tall = members * rows
    steps = width // STEP_COLS
    block = pl.BlockSpec((tall, STEP_COLS), lambda s: (0, s))
    return pl.pallas_call(
        near_body,
        grid=(steps,),
        in_specs=[
            *[pl.BlockSpec(memory_space=pltpu.SMEM)] * 3,
            pl.BlockSpec((tall, width), lambda s: (0, 0), pipeline_mode=pl.Buffered(1)),
            pl.BlockSpec((width, STEP_COLS), lambda s: (0, s)),
            pl.BlockSpec((width, STEP_COLS), lambda s: (0, steps + s)),
            pl.BlockSpec((width, STEP_COLS), lambda s: (0, 2 * steps + s)),
        ],
        out_specs=[block, block, block],
        out_shape=[
            jax.ShapeDtypeStruct((tall, width), BF16),
            jax.ShapeDtypeStruct((tall, width), BF16),
            jax.ShapeDtypeStruct((tall, width), F32),
        ],
        scratch_shapes=[
            pltpu.VMEM((tall, width), BF16),
            pltpu.VMEM((rows, rows), F32),
            pltpu.VMEM((tall, STEP_COLS), BF16),
            pltpu.VMEM((STEP_COLS // PAIR, members, 2 * rows, 2 * PAIR), BF16),
        ],
        compiler_params=pltpu.CompilerParams(vmem_limit_bytes=60 * MIB),
        cost_estimate=pl.CostEstimate(
            flops=20 * 10**9, bytes_accessed=16 * MIB, transcendentals=10**7
        ),
        name="near",
    )(*place, latent.reshape(tall, width), w_qkv, w_qkv, w_qkv)


def far_body(
    place_ref,
    count_ref,
    window_ref,
    q_ref,
    o_ref,
    lse_ref,
    before_ref,
    after_ref,
    wk_ref,
    wv_ref,
    noise_ref,
    dec_ref,
    latent_hbm,
    wout_hbm,
    normalized_hbm,
    inverse_ref,
    normed_out_hbm,
    predicted_ref,
    padded_ref,
    halo_ref,
    bias_ref,
    k_ref,
    vx_ref,
    att_ref,
    latent_ref,
    wout_ref,
    normalized_ref,
    normed_out_ref,
    sem,
    out_sem,
):
    step = pl.program_id(0)
    members, _, width = before_ref.shape
    tall = q_ref.shape[0]
    rows = tall // members
    low = iota((1, PAIR), 1) < HEAD_DIM
    late = [
        pltpu.make_async_copy(latent_hbm, latent_ref, sem.at[0]),
        pltpu.make_async_copy(wout_hbm, wout_ref, sem.at[1]),
    ]

    @pl.when(step == 0)
    def _():
        for copy in late:
            copy.start()
        padded_ref[...] = jnp.zeros_like(padded_ref)
        padded_ref[: dec_ref.shape[0]] = dec_ref[...]
        for member in range(members):
            for side, source in enumerate((before_ref, after_ref)):
                at = (2 * member + side) * HALO
                halo_ref[at : at + HALO] = normalize(source[member].astype(F32))[0].astype(BF16)
        shape = (HALO, HALO)
        bias_ref[0] = bias_of(iota(shape, 0), iota(shape, 1) - HALO, place_ref, count_ref, window_ref, rows)
        bias_ref[1] = bias_of(iota(shape, 0) + rows - HALO, iota(shape, 1) + rows, place_ref, count_ref, window_ref, rows)
        set_ones(vx_ref, low)

    def keys(at):
        span = slice(at, at + HALO)
        k_ref[span] = nn_dot(halo_ref[span], wk_ref[...]).astype(BF16)

    def values(at):
        span = slice(at, at + HALO)
        value = nn_dot(halo_ref[span], wv_ref[...]).astype(BF16)
        set_values(vx_ref, at // HALO, 0, value, low)

    def attend(member, pair, side):
        cols = slice(pair * PAIR, (pair + 1) * PAIR)
        out_cols = pl.ds(pl.multiple_of(step * STEP_COLS + pair * PAIR, PAIR), PAIR)
        at = member * rows + side * (rows - HALO)
        mine = slice(at, at + HALO)
        reach = slice((2 * member + side) * HALO, (2 * member + side + 1) * HALO)
        lse = lse_ref[mine, cols]
        weight, far_top = pair_scores(q_ref[mine, cols], k_ref[reach, cols], bias_ref[side], low)
        total = nn_dot(weight, vx_ref[pair, 2 * member + side])
        top = jnp.maximum(lse, far_top)
        near_share, far_share = jnp.exp2(lse - top), jnp.exp2(far_top - top)
        att_ref[mine, out_cols] = (
            (near_share * o_ref[mine, cols].astype(F32) + far_share * total[:, :PAIR])
            / (near_share + far_share * total[:, PAIR:])
        ).astype(BF16)

    groups = [(member, side) for member in range(members) for side in range(2)]

    def project(group):
        keys(group * HALO)
        values(group * HALO)

    project(0)
    for group, (member, side) in enumerate(groups):
        if group + 1 < len(groups):
            project(group + 1)
        for pair in range(STEP_COLS // PAIR):
            attend(member, pair, side)

    @pl.when(step == pl.num_programs(0) - 1)
    def _():
        for copy in late:
            copy.wait()
        copies = []
        chunks = [(member, at) for member in range(members) for at in range(0, rows, HALO)]

        def hidden_of(member, at):
            attended = att_ref[member * rows + at : member * rows + at + HALO]
            return latent_ref[member, at : at + HALO].astype(F32) + nn_dot(attended, wout_ref[...])

        hidden = hidden_of(*chunks[0])
        for index, (member, at) in enumerate(chunks):
            after = hidden_of(*chunks[index + 1]) if index + 1 < len(chunks) else None
            span = slice(at, at + HALO)
            normalized, inverse = normalize(hidden)
            normalized_ref[member, span] = normalized.astype(BF16)
            inverse_ref[member, span] = jnp.broadcast_to(inverse, (HALO, inverse_ref.shape[2]))
            normed_out = (normalized + noise_ref[member : member + 1].astype(F32)).astype(BF16)
            normed_out_ref[member, span] = normed_out
            predicted_ref[member, :, span] = nt_dot(padded_ref[...], normed_out).astype(BF16)
            for source, target in ((normalized_ref, normalized_hbm), (normed_out_ref, normed_out_hbm)):
                copy = pltpu.make_async_copy(
                    source.at[member, span], target.at[member, span], out_sem.at[len(copies)]
                )
                copy.start()
                copies.append(copy)
            hidden = after
        for copy in copies:
            copy.wait()


def far(place, q, o, lse, before, after, w_qkv, noise, dec, latent, w_out):
    members, rows, width = latent.shape
    tall = members * rows
    fields = dec.shape[0]
    padded = -(-fields // FIELD_TILE) * FIELD_TILE
    steps = width // STEP_COLS
    block = pl.BlockSpec((tall, STEP_COLS), lambda s: (0, s))
    whole2 = lambda s: (0, 0)
    whole3 = lambda s: (0, 0, 0)
    anywhere = pl.BlockSpec(memory_space=pltpu.HBM)
    return pl.pallas_call(
        far_body,
        grid=(steps,),
        in_specs=[
            *[pl.BlockSpec(memory_space=pltpu.SMEM)] * 3,
            block,
            block,
            block,
            pl.BlockSpec(memory_space=pltpu.VMEM),
            pl.BlockSpec(memory_space=pltpu.VMEM),
            pl.BlockSpec((width, STEP_COLS), lambda s: (0, steps + s)),
            pl.BlockSpec((width, STEP_COLS), lambda s: (0, 2 * steps + s)),
            pl.BlockSpec((members, width), whole2),
            pl.BlockSpec((fields, width), whole2),
            anywhere,
            anywhere,
        ],
        out_specs=[
            anywhere,
            pl.BlockSpec((members, rows, 128), whole3),
            anywhere,
            pl.BlockSpec((members, padded, rows), whole3),
            pl.BlockSpec((padded, width), whole2),
        ],
        out_shape=[
            jax.ShapeDtypeStruct((members, rows, width), BF16),
            jax.ShapeDtypeStruct((members, rows, 128), F32),
            jax.ShapeDtypeStruct((members, rows, width), BF16),
            jax.ShapeDtypeStruct((members, padded, rows), BF16),
            jax.ShapeDtypeStruct((padded, width), BF16),
        ],
        scratch_shapes=[
            pltpu.VMEM((members * 2 * HALO, width), BF16),
            pltpu.VMEM((2, HALO, HALO), F32),
            pltpu.VMEM((members * 2 * HALO, STEP_COLS), BF16),
            pltpu.VMEM((STEP_COLS // PAIR, members * 2, 2 * HALO, 2 * PAIR), BF16),
            pltpu.VMEM((tall, width), BF16),
            pltpu.VMEM((members, rows, width), BF16),
            pltpu.VMEM((width, width), BF16),
            pltpu.VMEM((members, rows, width), BF16),
            pltpu.VMEM((members, rows, width), BF16),
            pltpu.SemaphoreType.DMA((2,)),
            pltpu.SemaphoreType.DMA((2 * members * rows // HALO,)),
        ],
        compiler_params=pltpu.CompilerParams(vmem_limit_bytes=60 * MIB),
        cost_estimate=pl.CostEstimate(
            flops=15 * 10**9, bytes_accessed=22 * MIB, transcendentals=10**7
        ),
        name="far",
    )(*place, q, o, lse, before, after, w_qkv, w_qkv, noise, dec, latent, w_out)


def crps_body(
    place_ref, count_ref, pred_ref, target_ref, fw_ref, aw_ref, normed_hbm, grad_ref, pieces_ref, normed_ref, padded_ref, sem
):
    fetch = pltpu.make_async_copy(normed_hbm, normed_ref, sem)
    fetch.start()
    bands = count_ref.shape[0]
    first = lax.div(place_ref[0], bands)
    count = count_ref[lax.rem(place_ref[0], bands)]
    ensemble = pred_ref.shape[0] * pred_ref.shape[1]
    own_count = pred_ref.shape[1]
    lead = 1.0 / (ensemble - 1)
    fields, rows = padded_ref.shape
    real = target_ref.shape[0]
    padded_ref[...] = jnp.zeros_like(padded_ref)
    padded_ref[:real] = target_ref[...]
    width = normed_ref.shape[-1]
    target = padded_ref[...]
    used = lax.broadcasted_iota(jnp.int32, (1, rows), 1) < count
    shape = (fields, real)
    diagonal = iota(shape, 0) == iota(shape, 1)
    field_weight = jnp.sum(jnp.where(diagonal, fw_ref[...], 0.0), axis=1, keepdims=True)
    scale = field_weight * jnp.where(used, aw_ref[...], 0.0)

    def slope(gap):
        square = gap * gap + smooth_width * smooth_width
        root = lax.rsqrt(square)
        return gap * root, square * root

    loss = jnp.zeros((fields, rows), F32)
    grads = []
    for own in range(own_count):
        mine = pred_ref[first, own].astype(F32)
        pair_slope = jnp.zeros((fields, rows), F32)
        pair_abs = jnp.zeros((fields, rows), F32)
        for other in range(ensemble):
            s, a = slope(mine - pred_ref[other // own_count, other % own_count].astype(F32))
            pair_slope = pair_slope + s
            pair_abs = pair_abs + a
        s, a = slope(mine - target)
        grad = (scale * (s - pair_slope * lead)).astype(BF16)
        grad_ref[own] = grad
        loss = loss + scale * (a - pair_abs * (0.5 * lead))
        grads.append(grad)
    fetch.wait()
    weight = nn_dot(grads[0], normed_ref[0])
    for own in range(1, own_count):
        weight = weight + nn_dot(grads[own], normed_ref[own])
    tiles = width // 128
    for r in range(0, fields, 8):
        for c in range(tiles):
            piece = weight[r : r + 8, c * 128 : c * 128 + 128]
            pieces_ref[r // 8 * tiles + c] = piece.astype(BF16)
    used_pieces = LOSS_PIECE
    whole = jnp.sum(jnp.sum(loss, axis=0, keepdims=True), axis=1, keepdims=True)
    high = whole.astype(BF16)
    rest = (whole - high.astype(F32)).astype(BF16)
    row = lax.broadcasted_iota(jnp.int32, (8, 128), 0)
    both = jnp.where(row == 0, high.astype(F32), jnp.where(row == 1, rest.astype(F32), 0.0))
    pieces_ref[used_pieces] = both.astype(BF16)
    pieces_ref[used_pieces + 1 :] = jnp.zeros_like(pieces_ref[used_pieces + 1 :])


def crps(place, preds, targets, field_weight, area_weight, normed_out, peers):
    _, own_count, fields, rows = preds.shape
    vmem = pl.BlockSpec(memory_space=pltpu.VMEM)
    return pl.pallas_call(
        crps_body,
        in_specs=[pl.BlockSpec(memory_space=pltpu.SMEM)] * 2
        + [vmem] * 4
        + [pl.BlockSpec(memory_space=pltpu.HBM)],
        out_specs=[vmem] * 2,
        out_shape=[
            jax.ShapeDtypeStruct((own_count, fields, rows), BF16),
            jax.ShapeDtypeStruct((peers, 8, 128), BF16),
        ],
        scratch_shapes=[
            pltpu.VMEM(normed_out.shape, BF16),
            pltpu.VMEM((fields, rows), F32),
            pltpu.SemaphoreType.DMA(()),
        ],
        compiler_params=pltpu.CompilerParams(vmem_limit_bytes=52 * MIB),
        cost_estimate=pl.CostEstimate(
            flops=4 * 10**8, bytes_accessed=4 * MIB, transcendentals=10**6
        ),
        name="crps",
    )(*place[:2], preds, targets, field_weight, area_weight, normed_out)


def backward_body(grad_ref, dec_ref, normalized_ref, inverse_ref, out_ref):
    grad_norm = tn_dot(grad_ref[...], dec_ref[...])
    normalized = normalized_ref[...].astype(F32)
    inverse = inverse_ref[...][:, :1]
    mean = jnp.mean(grad_norm, axis=-1, keepdims=True)
    dotted = jnp.mean(grad_norm * normalized, axis=-1, keepdims=True)
    out_ref[...] = (inverse * (grad_norm - mean - normalized * dotted)).astype(BF16)


def backward(grad, dec, normalized, inverse):
    members, fields, rows = grad.shape
    width = dec.shape[1]
    return pl.pallas_call(
        backward_body,
        grid=(members,),
        in_specs=[
            pl.BlockSpec((None, fields, rows), lambda m: (m, 0, 0)),
            pl.BlockSpec((fields, width), lambda m: (0, 0)),
            pl.BlockSpec((None, rows, width), lambda m: (m, 0, 0)),
            pl.BlockSpec((None, rows, 128), lambda m: (m, 0, 0)),
        ],
        out_specs=pl.BlockSpec((None, rows, width), lambda m: (m, 0, 0)),
        out_shape=jax.ShapeDtypeStruct((members, rows, width), BF16),
        compiler_params=pltpu.CompilerParams(vmem_limit_bytes=32 * MIB),
        cost_estimate=pl.CostEstimate(
            flops=5 * 10**8, bytes_accessed=5 * MIB, transcendentals=0
        ),
        name="backward",
    )(grad, dec, normalized, inverse)


def share_body(rank_ref, parts_ref, spread_ref):
    peers = parts_ref.shape[0]
    mine = jnp.sum(parts_ref[...].astype(F32), axis=0)
    row = iota(mine.shape, 0)
    loss = jnp.sum(jnp.where(row < 2, mine, 0.0), axis=0, keepdims=True)
    rounded = loss.astype(BF16).astype(F32)
    as_loss = jnp.where(row == 0, rounded, jnp.where(row == 1, loss - rounded, 0.0))
    mine = jnp.where(rank_ref[0] == LOSS_PIECE, as_loss, mine).astype(BF16)
    spread_ref[...] = jnp.broadcast_to(mine[None], spread_ref.shape)


def finish_body(pieces_ref, weight_ref, loss_ref, *, tokens):
    fields, width = weight_ref.shape
    tiles = width // 128
    for r in range(0, fields, 8):
        count = min(8, fields - r)
        for c in range(tiles):
            piece = pieces_ref[r // 8 * tiles + c].astype(F32) * (1.0 / tokens)
            weight_ref[r : r + count, c * 128 : c * 128 + 128] = piece[:count]
    loss = jnp.sum(pieces_ref[LOSS_PIECE].astype(F32), axis=0, keepdims=True) * (1.0 / tokens)
    loss_ref[0, 0] = jnp.max(loss)


def summed(place, pieces, fields, width, tokens):
    axes = ("mem", "lat")
    vmem = pl.BlockSpec(memory_space=pltpu.VMEM)
    smem = pl.BlockSpec(memory_space=pltpu.SMEM)
    params = pltpu.CompilerParams(vmem_limit_bytes=16 * MIB)
    parts = lax.all_to_all(pieces, axes, split_axis=0, concat_axis=0, tiled=True)
    spread = pl.pallas_call(
        share_body,
        in_specs=[smem, vmem],
        out_specs=vmem,
        out_shape=jax.ShapeDtypeStruct(pieces.shape, BF16),
        compiler_params=params,
        name="share",
    )(place[0], parts)
    whole = lax.all_to_all(spread, axes, split_axis=0, concat_axis=0, tiled=True)
    return pl.pallas_call(
        functools.partial(finish_body, tokens=tokens),
        in_specs=[vmem],
        out_specs=[vmem, smem],
        out_shape=[
            jax.ShapeDtypeStruct((fields, width), F32),
            jax.ShapeDtypeStruct((1, 1), F32),
        ],
        compiler_params=params,
        name="finish",
    )(whole)


def local(
    latent,
    member_noise,
    w_qkv,
    w_out,
    dec_weight,
    targets,
    area_weight,
    field_weight,
    band_count,
    band_window,
):
    members, rows, width = latent.shape
    bands = lax.axis_size("lat")
    fields = dec_weight.shape[0]
    up = [(i, i + 1) for i in range(bands - 1)]
    down = [(j, i) for i, j in up]
    before = lax.ppermute(latent[:, rows - HALO :], "lat", up)
    after = lax.ppermute(latent[:, :HALO], "lat", down)
    place = (lax.axis_index(("mem", "lat")).reshape(1), band_count, band_window)
    q, o, lse = near(place, latent, w_qkv)
    normalized, inverse, normed_out, predicted, dec = far(
        place, q, o, lse, before, after, w_qkv, member_noise, dec_weight, latent, w_out
    )
    preds = lax.all_gather(predicted, "mem", axis=0)
    peers = lax.axis_size("mem") * bands
    grad, pieces = crps(
        place, preds, targets, field_weight[None, :], area_weight[None, :], normed_out, peers
    )
    weight, loss = summed(place, pieces, fields, width, rows * bands)
    grad_hidden = backward(grad, dec, normalized, inverse)
    return grad_hidden, weight, loss.reshape(())


def solution(mesh):
    return jax.shard_map(
        local,
        mesh=mesh,
        in_specs=(
            P("mem", "lat", None),
            P("mem", None),
            P(),
            P(),
            P(),
            P(None, "lat"),
            P("lat"),
            P(),
            P(),
            P("lat", None),
        ),
        out_specs=(P("mem", "lat", None), P(), P()),
        check_vma=False,
    )
```

```python
import functools

import jax
import jax.numpy as jnp
from jax import lax
from jax.experimental import pallas as pl
from jax.experimental.pallas import tpu as pltpu
from jax.sharding import PartitionSpec as P

HEAD_DIM = 64
HALO = 256
LOG2E = 1.4426950408889634

norm_eps = 1e-05
smooth_width = 0.25
F32 = jnp.float32
BF16 = jnp.bfloat16
MIB = 1024 * 1024


def normalize(x):
    mean = jnp.mean(x, axis=-1, keepdims=True)
    centred = x - mean
    var = jnp.mean(centred * centred, axis=-1, keepdims=True)
    inverse = lax.rsqrt(var + norm_eps)
    return centred * inverse, inverse


def nt_dot(a, b):
    return lax.dot_general(a, b, (((1,), (1,)), ((), ())), preferred_element_type=F32)


def tn_dot(a, b):
    return lax.dot_general(a, b, (((0,), (0,)), ((), ())), preferred_element_type=F32)


def nn_dot(a, b):
    return jnp.dot(a, b, preferred_element_type=F32)


QB = 256
STEP_COLS = 256
PAIR = 2 * HEAD_DIM
FIELD_TILE = 8
LOSS_PIECE = 104
NEVER = -1e30


def bias_of(q_row, k_row, place_ref, count_ref, window_ref, rows):
    bands = count_ref.shape[0]
    band = lax.rem(place_ref[0], bands)
    offset = k_row - q_row
    in_window = (offset >= -window_ref[0, 0]) & (offset <= window_ref[0, 1])
    before = jnp.where(band > 0, count_ref[jnp.maximum(band - 1, 0)], 0)
    after = jnp.where(band < bands - 1, count_ref[jnp.minimum(band + 1, bands - 1)], 0)
    end = jnp.where(
        k_row < 0, before - rows, jnp.where(k_row < rows, count_ref[band], after + rows)
    )
    return jnp.where((in_window & (k_row < end)) | (offset == 0), 0.0, NEVER)


def iota(shape, axis):
    return lax.broadcasted_iota(jnp.int32, shape, axis)


def pair_scores(q, keys, bias, low):
    zero = jnp.zeros_like(q)
    both = jnp.concatenate([jnp.where(low, q, zero), jnp.where(low, zero, q)], axis=0)
    scores = nt_dot(both, keys)
    weights, tops = [], []
    for half in range(2):
        part = scores[half * q.shape[0] : (half + 1) * q.shape[0]] + bias
        top = jnp.max(part, axis=-1, keepdims=True)
        weights.append(jnp.exp2(part - top).astype(BF16))
        tops.append(top)
    return jnp.concatenate(weights, axis=1), jnp.where(low, tops[0], tops[1])


def set_ones(ref, low):
    half = ref.shape[-2] // 2
    one = jnp.ones((half, PAIR), BF16)
    for pair in range(ref.shape[0]):
        for group in range(ref.shape[1]):
            ref[pair, group, :half, PAIR:] = jnp.where(low, one, 0.0).astype(BF16)
            ref[pair, group, half:, PAIR:] = jnp.where(low, 0.0, one).astype(BF16)


def set_values(ref, group, at, value, low):
    half, count = ref.shape[-2] // 2, value.shape[0]
    for pair in range(ref.shape[0]):
        own = value[:, pair * PAIR : (pair + 1) * PAIR]
        zero = jnp.zeros_like(own)
        ref[pair, group, at : at + count, :PAIR] = jnp.where(low, own, zero)
        ref[pair, group, half + at : half + at + count, :PAIR] = jnp.where(low, zero, own)


def near_body(
    place_ref, count_ref, window_ref, latent_ref, wq_ref, wk_ref, wv_ref, q_ref, o_ref, lse_ref, normed_ref, bias_ref, k_ref, vx_ref
):
    step = pl.program_id(0)
    rows = bias_ref.shape[0]
    members = latent_ref.shape[0] // rows
    low = iota((1, PAIR), 1) < HEAD_DIM

    @pl.when(step == 0)
    def _():
        normed_ref[...] = normalize(latent_ref[...].astype(F32))[0].astype(BF16)
        shape = bias_ref.shape
        bias_ref[...] = bias_of(iota(shape, 0), iota(shape, 1), place_ref, count_ref, window_ref, rows)
        set_ones(vx_ref, low)


    def queries(at):
        span = slice(at, at + QB)
        q_ref[span] = (
            nn_dot(normed_ref[span], wq_ref[...]) * (HEAD_DIM ** (-0.5) * LOG2E)
        ).astype(BF16)

    def keys(at):
        span = slice(at, at + QB)
        k_ref[span] = nn_dot(normed_ref[span], wk_ref[...]).astype(BF16)

    def values(at):
        span = slice(at, at + QB)
        value = nn_dot(normed_ref[span], wv_ref[...]).astype(BF16)
        set_values(vx_ref, at // rows, at % rows, value, low)

    def attend(member, pair, block):
        cols = slice(pair * PAIR, (pair + 1) * PAIR)
        here = slice(block * QB, (block + 1) * QB)
        mine = slice(member * rows + block * QB, member * rows + (block + 1) * QB)
        reach = slice(member * rows, (member + 1) * rows)
        weight, top = pair_scores(q_ref[mine, cols], k_ref[reach, cols], bias_ref[here], low)
        total = nn_dot(weight, vx_ref[pair, member])
        summed_weight = total[:, PAIR:]
        o_ref[mine, cols] = (total[:, :PAIR] / summed_weight).astype(BF16)
        lse_ref[mine, cols] = top + jnp.log2(summed_weight)

    pairs, blocks = STEP_COLS // PAIR, rows // QB
    project = [
        [(f, member * rows + at) for f in (keys, values, queries) for at in range(0, rows, QB)]
        for member in range(members)
    ]
    for f, at in project[0]:
        f(at)
    for member in range(members):
        later = project[member + 1] if member + 1 < members else []
        tiles = [(pair, block) for pair in range(pairs) for block in range(blocks)]
        share = -(-len(later) // len(tiles))
        for i, (pair, block) in enumerate(tiles):
            for f, at in later[i * share : (i + 1) * share]:
                f(at)
            attend(member, pair, block)


def near(place, latent, w_qkv):
    members, rows, width = latent.shape
    tall = members * rows
    steps = width // STEP_COLS
    block = pl.BlockSpec((tall, STEP_COLS), lambda s: (0, s))
    return pl.pallas_call(
        near_body,
        grid=(steps,),
        in_specs=[
            *[pl.BlockSpec(memory_space=pltpu.SMEM)] * 3,
            pl.BlockSpec((tall, width), lambda s: (0, 0), pipeline_mode=pl.Buffered(1)),
            pl.BlockSpec((width, STEP_COLS), lambda s: (0, s)),
            pl.BlockSpec((width, STEP_COLS), lambda s: (0, steps + s)),
            pl.BlockSpec((width, STEP_COLS), lambda s: (0, 2 * steps + s)),
        ],
        out_specs=[block, block, block],
        out_shape=[
            jax.ShapeDtypeStruct((tall, width), BF16),
            jax.ShapeDtypeStruct((tall, width), BF16),
            jax.ShapeDtypeStruct((tall, width), F32),
        ],
        scratch_shapes=[
            pltpu.VMEM((tall, width), BF16),
            pltpu.VMEM((rows, rows), F32),
            pltpu.VMEM((tall, STEP_COLS), BF16),
            pltpu.VMEM((STEP_COLS // PAIR, members, 2 * rows, 2 * PAIR), BF16),
        ],
        compiler_params=pltpu.CompilerParams(vmem_limit_bytes=60 * MIB),
        cost_estimate=pl.CostEstimate(
            flops=20 * 10**9, bytes_accessed=16 * MIB, transcendentals=10**7
        ),
        name="near",
    )(*place, latent.reshape(tall, width), w_qkv, w_qkv, w_qkv)


def far_body(
    place_ref,
    count_ref,
    window_ref,
    q_ref,
    o_ref,
    lse_ref,
    after_ref,
    before_ref,
    wk_ref,
    wv_ref,
    noise_ref,
    dec_ref,
    latent_hbm,
    wout_hbm,
    normalized_hbm,
    inverse_ref,
    normed_out_hbm,
    predicted_ref,
    padded_ref,
    halo_ref,
    bias_ref,
    k_ref,
    vx_ref,
    att_ref,
    latent_ref,
    wout_ref,
    normalized_ref,
    normed_out_ref,
    sem,
    out_sem,
):
    step = pl.program_id(0)
    members, _, width = before_ref.shape
    tall = q_ref.shape[0]
    rows = tall // members
    low = iota((1, PAIR), 1) < HEAD_DIM
    late = [
        pltpu.make_async_copy(latent_hbm, latent_ref, sem.at[0]),
        pltpu.make_async_copy(wout_hbm, wout_ref, sem.at[1]),
    ]

    @pl.when(step == 0)
    def _():
        for copy in late:
            copy.start()
        padded_ref[...] = jnp.zeros_like(padded_ref)
        padded_ref[: dec_ref.shape[0]] = dec_ref[...]
        for member in range(members):
            for side, source in enumerate((before_ref, after_ref)):
                at = (2 * member + side) * HALO
                halo_ref[at : at + HALO] = normalize(source[member].astype(F32))[0].astype(BF16)
        shape = (HALO, HALO)
        bias_ref[0] = bias_of(iota(shape, 0), iota(shape, 1) - HALO, place_ref, count_ref, window_ref, rows)
        bias_ref[1] = bias_of(iota(shape, 0) + rows - HALO, iota(shape, 1) + rows, place_ref, count_ref, window_ref, rows)
        set_ones(vx_ref, low)

    def keys(at):
        span = slice(at, at + HALO)
        k_ref[span] = nn_dot(halo_ref[span], wk_ref[...]).astype(BF16)

    def values(at):
        span = slice(at, at + HALO)
        value = nn_dot(halo_ref[span], wv_ref[...]).astype(BF16)
        set_values(vx_ref, at // HALO, 0, value, low)

    def attend(member, pair, side):
        cols = slice(pair * PAIR, (pair + 1) * PAIR)
        out_cols = pl.ds(pl.multiple_of(step * STEP_COLS + pair * PAIR, PAIR), PAIR)
        at = member * rows + side * (rows - HALO)
        mine = slice(at, at + HALO)
        reach = slice((2 * member + side) * HALO, (2 * member + side + 1) * HALO)
        lse = lse_ref[mine, cols]
        weight, far_top = pair_scores(q_ref[mine, cols], k_ref[reach, cols], bias_ref[side], low)
        total = nn_dot(weight, vx_ref[pair, 2 * member + side])
        top = jnp.maximum(lse, far_top)
        near_share, far_share = jnp.exp2(lse - top), jnp.exp2(far_top - top)
        att_ref[mine, out_cols] = (
            (near_share * o_ref[mine, cols].astype(F32) + far_share * total[:, :PAIR])
            / (near_share + far_share * total[:, PAIR:])
        ).astype(BF16)

    groups = [(member, side) for member in range(members) for side in range(2)]

    def project(group):
        keys(group * HALO)
        values(group * HALO)

    project(0)
    for group, (member, side) in enumerate(groups):
        if group + 1 < len(groups):
            project(group + 1)
        for pair in range(STEP_COLS // PAIR):
            attend(member, pair, side)

    @pl.when(step == pl.num_programs(0) - 1)
    def _():
        for copy in late:
            copy.wait()
        copies = []
        chunks = [(member, at) for member in range(members) for at in range(0, rows, HALO)]

        def hidden_of(member, at):
            attended = att_ref[member * rows + at : member * rows + at + HALO]
            return latent_ref[member, at : at + HALO].astype(F32) + nn_dot(attended, wout_ref[...])

        hidden = hidden_of(*chunks[0])
        for index, (member, at) in enumerate(chunks):
            after = hidden_of(*chunks[index + 1]) if index + 1 < len(chunks) else None
            span = slice(at, at + HALO)
            normalized, inverse = normalize(hidden)
            normalized_ref[member, span] = normalized.astype(BF16)
            inverse_ref[member, span] = jnp.broadcast_to(inverse, (HALO, inverse_ref.shape[2]))
            normed_out = (normalized + noise_ref[member : member + 1].astype(F32)).astype(BF16)
            normed_out_ref[member, span] = normed_out
            predicted_ref[member, :, span] = nt_dot(padded_ref[...], normed_out).astype(BF16)
            for source, target in ((normalized_ref, normalized_hbm), (normed_out_ref, normed_out_hbm)):
                copy = pltpu.make_async_copy(
                    source.at[member, span], target.at[member, span], out_sem.at[len(copies)]
                )
                copy.start()
                copies.append(copy)
            hidden = after
        for copy in copies:
            copy.wait()


def far(place, q, o, lse, after, before, w_qkv, noise, dec, latent, w_out):
    members, rows, width = latent.shape
    tall = members * rows
    fields = dec.shape[0]
    padded = -(-fields // FIELD_TILE) * FIELD_TILE
    steps = width // STEP_COLS
    block = pl.BlockSpec((tall, STEP_COLS), lambda s: (0, s))
    whole2 = lambda s: (0, 0)
    whole3 = lambda s: (0, 0, 0)
    anywhere = pl.BlockSpec(memory_space=pltpu.HBM)
    return pl.pallas_call(
        far_body,
        grid=(steps,),
        in_specs=[
            *[pl.BlockSpec(memory_space=pltpu.SMEM)] * 3,
            block,
            block,
            block,
            pl.BlockSpec(memory_space=pltpu.VMEM),
            pl.BlockSpec(memory_space=pltpu.VMEM),
            pl.BlockSpec((width, STEP_COLS), lambda s: (0, steps + s)),
            pl.BlockSpec((width, STEP_COLS), lambda s: (0, 2 * steps + s)),
            pl.BlockSpec((members, width), whole2),
            pl.BlockSpec((fields, width), whole2),
            anywhere,
            anywhere,
        ],
        out_specs=[
            anywhere,
            pl.BlockSpec((members, rows, 128), whole3),
            anywhere,
            pl.BlockSpec((members, padded, rows), whole3),
            pl.BlockSpec((padded, width), whole2),
        ],
        out_shape=[
            jax.ShapeDtypeStruct((members, rows, width), BF16),
            jax.ShapeDtypeStruct((members, rows, 128), F32),
            jax.ShapeDtypeStruct((members, rows, width), BF16),
            jax.ShapeDtypeStruct((members, padded, rows), BF16),
            jax.ShapeDtypeStruct((padded, width), BF16),
        ],
        scratch_shapes=[
            pltpu.VMEM((members * 2 * HALO, width), BF16),
            pltpu.VMEM((2, HALO, HALO), F32),
            pltpu.VMEM((members * 2 * HALO, STEP_COLS), BF16),
            pltpu.VMEM((STEP_COLS // PAIR, members * 2, 2 * HALO, 2 * PAIR), BF16),
            pltpu.VMEM((tall, width), BF16),
            pltpu.VMEM((members, rows, width), BF16),
            pltpu.VMEM((width, width), BF16),
            pltpu.VMEM((members, rows, width), BF16),
            pltpu.VMEM((members, rows, width), BF16),
            pltpu.SemaphoreType.DMA((2,)),
            pltpu.SemaphoreType.DMA((2 * members * rows // HALO,)),
        ],
        compiler_params=pltpu.CompilerParams(vmem_limit_bytes=60 * MIB),
        cost_estimate=pl.CostEstimate(
            flops=15 * 10**9, bytes_accessed=22 * MIB, transcendentals=10**7
        ),
        name="far",
    )(*place, q, o, lse, after, before, w_qkv, w_qkv, noise, dec, latent, w_out)


def crps_body(
    place_ref, count_ref, pred_ref, target_ref, fw_ref, aw_ref, normed_hbm, grad_ref, pieces_ref, normed_ref, padded_ref, sem
):
    fetch = pltpu.make_async_copy(normed_hbm, normed_ref, sem)
    fetch.start()
    bands = count_ref.shape[0]
    first = lax.div(place_ref[0], bands)
    count = count_ref[lax.rem(place_ref[0], bands)]
    ensemble = pred_ref.shape[0] * pred_ref.shape[1]
    own_count = pred_ref.shape[1]
    lead = 1.0 / (ensemble - 1)
    fields, rows = padded_ref.shape
    real = target_ref.shape[0]
    padded_ref[...] = jnp.zeros_like(padded_ref)
    padded_ref[:real] = target_ref[...]
    width = normed_ref.shape[-1]
    target = padded_ref[...]
    used = lax.broadcasted_iota(jnp.int32, (1, rows), 1) < count
    shape = (fields, real)
    diagonal = iota(shape, 0) == iota(shape, 1)
    field_weight = jnp.sum(jnp.where(diagonal, fw_ref[...], 0.0), axis=1, keepdims=True)
    scale = field_weight * jnp.where(used, aw_ref[...], 0.0)

    def slope(gap):
        square = gap * gap + smooth_width * smooth_width
        root = lax.rsqrt(square)
        return gap * root, square * root

    loss = jnp.zeros((fields, rows), F32)
    grads = []
    for own in range(own_count):
        mine = pred_ref[first, own].astype(F32)
        pair_slope = jnp.zeros((fields, rows), F32)
        pair_abs = jnp.zeros((fields, rows), F32)
        for other in range(ensemble):
            s, a = slope(mine - pred_ref[other // own_count, other % own_count].astype(F32))
            pair_slope = pair_slope + s
            pair_abs = pair_abs + a
        s, a = slope(mine - target)
        grad = (scale * (s - pair_slope * lead)).astype(BF16)
        grad_ref[own] = grad
        loss = loss + scale * (a - pair_abs * (0.5 * lead))
        grads.append(grad)
    fetch.wait()
    weight = nn_dot(grads[0], normed_ref[0])
    for own in range(1, own_count):
        weight = weight + nn_dot(grads[own], normed_ref[own])
    tiles = width // 128
    for r in range(0, fields, 8):
        for c in range(tiles):
            piece = weight[r : r + 8, c * 128 : c * 128 + 128]
            pieces_ref[r // 8 * tiles + c] = piece.astype(BF16)
    used_pieces = LOSS_PIECE
    whole = jnp.sum(jnp.sum(loss, axis=0, keepdims=True), axis=1, keepdims=True)
    high = whole.astype(BF16)
    rest = (whole - high.astype(F32)).astype(BF16)
    row = lax.broadcasted_iota(jnp.int32, (8, 128), 0)
    both = jnp.where(row == 0, high.astype(F32), jnp.where(row == 1, rest.astype(F32), 0.0))
    pieces_ref[used_pieces] = both.astype(BF16)
    pieces_ref[used_pieces + 1 :] = jnp.zeros_like(pieces_ref[used_pieces + 1 :])


def crps(place, preds, targets, field_weight, area_weight, normed_out, peers):
    _, own_count, fields, rows = preds.shape
    vmem = pl.BlockSpec(memory_space=pltpu.VMEM)
    return pl.pallas_call(
        crps_body,
        in_specs=[pl.BlockSpec(memory_space=pltpu.SMEM)] * 2
        + [vmem] * 4
        + [pl.BlockSpec(memory_space=pltpu.HBM)],
        out_specs=[vmem] * 2,
        out_shape=[
            jax.ShapeDtypeStruct((own_count, fields, rows), BF16),
            jax.ShapeDtypeStruct((peers, 8, 128), BF16),
        ],
        scratch_shapes=[
            pltpu.VMEM(normed_out.shape, BF16),
            pltpu.VMEM((fields, rows), F32),
            pltpu.SemaphoreType.DMA(()),
        ],
        compiler_params=pltpu.CompilerParams(vmem_limit_bytes=52 * MIB),
        cost_estimate=pl.CostEstimate(
            flops=4 * 10**8, bytes_accessed=4 * MIB, transcendentals=10**6
        ),
        name="crps",
    )(*place[:2], preds, targets, field_weight, area_weight, normed_out)


def backward_body(grad_ref, dec_ref, normalized_ref, inverse_ref, out_ref):
    grad_norm = tn_dot(grad_ref[...], dec_ref[...])
    normalized = normalized_ref[...].astype(F32)
    inverse = inverse_ref[...][:, :1]
    mean = jnp.mean(grad_norm, axis=-1, keepdims=True)
    dotted = jnp.mean(grad_norm * normalized, axis=-1, keepdims=True)
    out_ref[...] = (inverse * (grad_norm - mean - normalized * dotted)).astype(BF16)


def backward(grad, dec, normalized, inverse):
    members, fields, rows = grad.shape
    width = dec.shape[1]
    return pl.pallas_call(
        backward_body,
        grid=(members,),
        in_specs=[
            pl.BlockSpec((None, fields, rows), lambda m: (m, 0, 0)),
            pl.BlockSpec((fields, width), lambda m: (0, 0)),
            pl.BlockSpec((None, rows, width), lambda m: (m, 0, 0)),
            pl.BlockSpec((None, rows, 128), lambda m: (m, 0, 0)),
        ],
        out_specs=pl.BlockSpec((None, rows, width), lambda m: (m, 0, 0)),
        out_shape=jax.ShapeDtypeStruct((members, rows, width), BF16),
        compiler_params=pltpu.CompilerParams(vmem_limit_bytes=32 * MIB),
        cost_estimate=pl.CostEstimate(
            flops=5 * 10**8, bytes_accessed=5 * MIB, transcendentals=0
        ),
        name="backward",
    )(grad, dec, normalized, inverse)


def share_body(rank_ref, parts_ref, spread_ref):
    peers = parts_ref.shape[0]
    mine = jnp.sum(parts_ref[...].astype(F32), axis=0)
    row = iota(mine.shape, 0)
    loss = jnp.sum(jnp.where(row < 2, mine, 0.0), axis=0, keepdims=True)
    rounded = loss.astype(BF16).astype(F32)
    as_loss = jnp.where(row == 0, rounded, jnp.where(row == 1, loss - rounded, 0.0))
    mine = jnp.where(rank_ref[0] == LOSS_PIECE, as_loss, mine).astype(BF16)
    spread_ref[...] = jnp.broadcast_to(mine[None], spread_ref.shape)


def finish_body(pieces_ref, weight_ref, loss_ref, *, tokens):
    fields, width = weight_ref.shape
    tiles = width // 128
    for r in range(0, fields, 8):
        count = min(8, fields - r)
        for c in range(tiles):
            piece = pieces_ref[r // 8 * tiles + c].astype(F32) * (1.0 / tokens)
            weight_ref[r : r + count, c * 128 : c * 128 + 128] = piece[:count]
    loss = jnp.sum(pieces_ref[LOSS_PIECE].astype(F32), axis=0, keepdims=True) * (1.0 / tokens)
    loss_ref[0, 0] = jnp.max(loss)


def summed(place, pieces, fields, width, tokens):
    axes = ("mem", "lat")
    vmem = pl.BlockSpec(memory_space=pltpu.VMEM)
    smem = pl.BlockSpec(memory_space=pltpu.SMEM)
    params = pltpu.CompilerParams(vmem_limit_bytes=16 * MIB)
    parts = lax.all_to_all(pieces, axes, split_axis=0, concat_axis=0, tiled=True)
    spread = pl.pallas_call(
        share_body,
        in_specs=[smem, vmem],
        out_specs=vmem,
        out_shape=jax.ShapeDtypeStruct(pieces.shape, BF16),
        compiler_params=params,
        name="share",
    )(place[0], parts)
    whole = lax.all_to_all(spread, axes, split_axis=0, concat_axis=0, tiled=True)
    return pl.pallas_call(
        functools.partial(finish_body, tokens=tokens),
        in_specs=[vmem],
        out_specs=[vmem, smem],
        out_shape=[
            jax.ShapeDtypeStruct((fields, width), F32),
            jax.ShapeDtypeStruct((1, 1), F32),
        ],
        compiler_params=params,
        name="finish",
    )(whole)


def local(
    latent,
    member_noise,
    w_qkv,
    w_out,
    dec_weight,
    targets,
    area_weight,
    field_weight,
    band_count,
    band_window,
):
    members, rows, width = latent.shape
    bands = lax.axis_size("lat")
    fields = dec_weight.shape[0]
    up = [(i, i + 1) for i in range(bands - 1)]
    down = [(j, i) for i, j in up]
    before = lax.ppermute(latent[:, rows - HALO :], "lat", up)
    after = lax.ppermute(latent[:, :HALO], "lat", down)
    place = (lax.axis_index(("mem", "lat")).reshape(1), band_count, band_window)
    q, o, lse = near(place, latent, w_qkv)
    normalized, inverse, normed_out, predicted, dec = far(
        place, q, o, lse, after, before, w_qkv, member_noise, dec_weight, latent, w_out
    )
    preds = lax.all_gather(predicted, "mem", axis=0)
    peers = lax.axis_size("mem") * bands
    grad, pieces = crps(
        place, preds, targets, field_weight[None, :], area_weight[None, :], normed_out, peers
    )
    weight, loss = summed(place, pieces, fields, width, rows * bands)
    grad_hidden = backward(grad, dec, normalized, inverse)
    return grad_hidden, weight, loss.reshape(())


def solution(mesh):
    return jax.shard_map(
        local,
        mesh=mesh,
        in_specs=(
            P("mem", "lat", None),
            P("mem", None),
            P(),
            P(),
            P(),
            P(None, "lat"),
            P("lat"),
            P(),
            P(),
            P("lat", None),
        ),
        out_specs=(P("mem", "lat", None), P(), P()),
        check_vma=False,
    )
```

```python
import functools

import jax
import jax.numpy as jnp
from jax import lax
from jax.experimental import pallas as pl
from jax.experimental.pallas import tpu as pltpu
from jax.sharding import PartitionSpec as P

HEAD_DIM = 64
HALO = 256
LOG2E = 1.4426950408889634

norm_eps = 1e-05
smooth_width = 0.25
F32 = jnp.float32
BF16 = jnp.bfloat16
MIB = 1024 * 1024


def normalize(x):
    mean = jnp.mean(x, axis=-1, keepdims=True)
    centred = x - mean
    var = jnp.mean(centred * centred, axis=-1, keepdims=True)
    inverse = lax.rsqrt(var + norm_eps)
    return centred * inverse, inverse


def nt_dot(a, b):
    return lax.dot_general(a, b, (((1,), (1,)), ((), ())), preferred_element_type=F32)


def tn_dot(a, b):
    return lax.dot_general(a, b, (((0,), (0,)), ((), ())), preferred_element_type=F32)


def nn_dot(a, b):
    return jnp.dot(a, b, preferred_element_type=F32)


QB = 256
STEP_COLS = 256
PAIR = 2 * HEAD_DIM
FIELD_TILE = 8
LOSS_PIECE = 104
NEVER = -1e30


def bias_of(q_row, k_row, place_ref, count_ref, window_ref, rows):
    bands = count_ref.shape[0]
    band = lax.rem(place_ref[0], bands)
    offset = k_row - q_row
    in_window = (offset >= -window_ref[0, 0]) & (offset <= window_ref[0, 1])
    before = jnp.where(band > 0, count_ref[jnp.maximum(band - 1, 0)], 0)
    after = jnp.where(band < bands - 1, count_ref[jnp.minimum(band + 1, bands - 1)], 0)
    end = jnp.where(
        k_row < 0, before - rows, jnp.where(k_row < rows, count_ref[band], after + rows)
    )
    return jnp.where((in_window & (k_row < end)) | (offset == 0), 0.0, NEVER)


def iota(shape, axis):
    return lax.broadcasted_iota(jnp.int32, shape, axis)


def pair_scores(q, keys, bias, low):
    zero = jnp.zeros_like(q)
    both = jnp.concatenate([jnp.where(low, q, zero), jnp.where(low, zero, q)], axis=0)
    scores = nt_dot(both, keys)
    weights, tops = [], []
    for half in range(2):
        part = scores[half * q.shape[0] : (half + 1) * q.shape[0]] + bias
        top = jnp.max(part, axis=-1, keepdims=True)
        weights.append(jnp.exp2(part - top).astype(BF16))
        tops.append(top)
    return jnp.concatenate(weights, axis=1), jnp.where(low, tops[0], tops[1])


def set_ones(ref, low):
    half = ref.shape[-2] // 2
    one = jnp.ones((half, PAIR), BF16)
    for pair in range(ref.shape[0]):
        for group in range(ref.shape[1]):
            ref[pair, group, :half, PAIR:] = jnp.where(low, one, 0.0).astype(BF16)
            ref[pair, group, half:, PAIR:] = jnp.where(low, 0.0, one).astype(BF16)


def set_values(ref, group, at, value, low):
    half, count = ref.shape[-2] // 2, value.shape[0]
    for pair in range(ref.shape[0]):
        own = value[:, pair * PAIR : (pair + 1) * PAIR]
        zero = jnp.zeros_like(own)
        ref[pair, group, at : at + count, :PAIR] = jnp.where(low, own, zero)
        ref[pair, group, half + at : half + at + count, :PAIR] = jnp.where(low, zero, own)


def near_body(
    place_ref, count_ref, window_ref, latent_ref, wq_ref, wk_ref, wv_ref, q_ref, o_ref, lse_ref, normed_ref, bias_ref, k_ref, vx_ref
):
    step = pl.program_id(0)
    rows = bias_ref.shape[0]
    members = latent_ref.shape[0] // rows
    low = iota((1, PAIR), 1) < HEAD_DIM

    @pl.when(step == 0)
    def _():
        normed_ref[...] = normalize(latent_ref[...].astype(F32))[0].astype(BF16)
        shape = bias_ref.shape
        bias_ref[...] = bias_of(iota(shape, 0), iota(shape, 1), place_ref, count_ref, window_ref, rows)
        set_ones(vx_ref, low)


    def queries(at):
        span = slice(at, at + QB)
        q_ref[span] = (
            nn_dot(normed_ref[span], wq_ref[...]) * (HEAD_DIM ** (-0.5) * LOG2E)
        ).astype(BF16)

    def keys(at):
        span = slice(at, at + QB)
        k_ref[span] = nn_dot(normed_ref[span], wk_ref[...]).astype(BF16)

    def values(at):
        span = slice(at, at + QB)
        value = nn_dot(normed_ref[span], wv_ref[...]).astype(BF16)
        set_values(vx_ref, at // rows, at % rows, value, low)

    def attend(member, pair, block):
        cols = slice(pair * PAIR, (pair + 1) * PAIR)
        here = slice(block * QB, (block + 1) * QB)
        mine = slice(member * rows + block * QB, member * rows + (block + 1) * QB)
        reach = slice(member * rows, (member + 1) * rows)
        weight, top = pair_scores(q_ref[mine, cols], k_ref[reach, cols], bias_ref[here], low)
        total = nn_dot(weight, vx_ref[pair, member])
        summed_weight = total[:, PAIR:]
        o_ref[mine, cols] = (total[:, :PAIR] / summed_weight).astype(BF16)
        lse_ref[mine, cols] = top + jnp.log2(summed_weight)

    pairs, blocks = STEP_COLS // PAIR, rows // QB
    project = [
        [(f, member * rows + at) for f in (keys, values, queries) for at in range(0, rows, QB)]
        for member in range(members)
    ]
    for f, at in project[0]:
        f(at)
    for member in range(members):
        later = project[member + 1] if member + 1 < members else []
        tiles = [(pair, block) for pair in range(pairs) for block in range(blocks)]
        share = -(-len(later) // len(tiles))
        for i, (pair, block) in enumerate(tiles):
            for f, at in later[i * share : (i + 1) * share]:
                f(at)
            attend(member, pair, block)


def near(place, latent, w_qkv):
    members, rows, width = latent.shape
    tall = members * rows
    steps = width // STEP_COLS
    block = pl.BlockSpec((tall, STEP_COLS), lambda s: (0, s))
    return pl.pallas_call(
        near_body,
        grid=(steps,),
        in_specs=[
            *[pl.BlockSpec(memory_space=pltpu.SMEM)] * 3,
            pl.BlockSpec((tall, width), lambda s: (0, 0), pipeline_mode=pl.Buffered(1)),
            pl.BlockSpec((width, STEP_COLS), lambda s: (0, s)),
            pl.BlockSpec((width, STEP_COLS), lambda s: (0, steps + s)),
            pl.BlockSpec((width, STEP_COLS), lambda s: (0, 2 * steps + s)),
        ],
        out_specs=[block, block, block],
        out_shape=[
            jax.ShapeDtypeStruct((tall, width), BF16),
            jax.ShapeDtypeStruct((tall, width), BF16),
            jax.ShapeDtypeStruct((tall, width), F32),
        ],
        scratch_shapes=[
            pltpu.VMEM((tall, width), BF16),
            pltpu.VMEM((rows, rows), F32),
            pltpu.VMEM((tall, STEP_COLS), BF16),
            pltpu.VMEM((STEP_COLS // PAIR, members, 2 * rows, 2 * PAIR), BF16),
        ],
        compiler_params=pltpu.CompilerParams(vmem_limit_bytes=60 * MIB),
        cost_estimate=pl.CostEstimate(
            flops=20 * 10**9, bytes_accessed=16 * MIB, transcendentals=10**7
        ),
        name="near",
    )(*place, latent.reshape(tall, width), w_qkv, w_qkv, w_qkv)


def far_body(
    place_ref,
    count_ref,
    window_ref,
    q_ref,
    o_ref,
    lse_ref,
    after_ref,
    before_ref,
    wk_ref,
    wv_ref,
    noise_ref,
    dec_ref,
    latent_hbm,
    wout_hbm,
    normalized_hbm,
    inverse_ref,
    normed_out_hbm,
    predicted_ref,
    padded_ref,
    halo_ref,
    bias_ref,
    k_ref,
    vx_ref,
    att_ref,
    latent_ref,
    wout_ref,
    normalized_ref,
    normed_out_ref,
    sem,
    out_sem,
):
    step = pl.program_id(0)
    members, _, width = before_ref.shape
    tall = q_ref.shape[0]
    rows = tall // members
    low = iota((1, PAIR), 1) < HEAD_DIM
    late = [
        pltpu.make_async_copy(latent_hbm, latent_ref, sem.at[0]),
        pltpu.make_async_copy(wout_hbm, wout_ref, sem.at[1]),
    ]

    @pl.when(step == 0)
    def _():
        for copy in late:
            copy.start()
        padded_ref[...] = jnp.zeros_like(padded_ref)
        padded_ref[: dec_ref.shape[0]] = dec_ref[...]
        for member in range(members):
            for side, source in enumerate((before_ref, after_ref)):
                at = (2 * member + side) * HALO
                halo_ref[at : at + HALO] = normalize(source[member].astype(F32))[0].astype(BF16)
        shape = (HALO, HALO)
        bias_ref[0] = bias_of(iota(shape, 0), iota(shape, 1) - HALO, place_ref, count_ref, window_ref, rows)
        bias_ref[1] = bias_of(iota(shape, 0) + rows - HALO, iota(shape, 1) + rows, place_ref, count_ref, window_ref, rows)
        set_ones(vx_ref, low)

    def keys(at):
        span = slice(at, at + HALO)
        k_ref[span] = nn_dot(halo_ref[span], wk_ref[...]).astype(BF16)

    def values(at):
        span = slice(at, at + HALO)
        value = nn_dot(halo_ref[span], wv_ref[...]).astype(BF16)
        set_values(vx_ref, at // HALO, 0, value, low)

    def attend(member, pair, side):
        cols = slice(pair * PAIR, (pair + 1) * PAIR)
        out_cols = pl.ds(pl.multiple_of(step * STEP_COLS + pair * PAIR, PAIR), PAIR)
        at = member * rows + side * (rows - HALO)
        mine = slice(at, at + HALO)
        reach = slice((2 * member + side) * HALO, (2 * member + side + 1) * HALO)
        lse = lse_ref[mine, cols]
        weight, far_top = pair_scores(q_ref[mine, cols], k_ref[reach, cols], bias_ref[side], low)
        total = nn_dot(weight, vx_ref[pair, 2 * member + side])
        top = jnp.maximum(lse, far_top)
        near_share, far_share = jnp.exp2(lse - top), jnp.exp2(far_top - top)
        att_ref[mine, out_cols] = (
            (near_share * o_ref[mine, cols].astype(F32) + far_share * total[:, :PAIR])
            / (near_share + far_share * total[:, PAIR:])
        ).astype(BF16)

    groups = [(member, side) for member in range(members) for side in range(2)]

    def project(group):
        keys(group * HALO)
        values(group * HALO)

    project(0)
    for group, (member, side) in enumerate(groups):
        if group + 1 < len(groups):
            project(group + 1)
        for pair in range(STEP_COLS // PAIR):
            attend(member, pair, side)

    @pl.when(step == pl.num_programs(0) - 1)
    def _():
        for copy in late:
            copy.wait()
        copies = []
        chunks = [(member, at) for member in range(members) for at in range(0, rows, HALO)]

        def hidden_of(member, at):
            attended = att_ref[member * rows + at : member * rows + at + HALO]
            return latent_ref[member, at : at + HALO].astype(F32) + nn_dot(attended, wout_ref[...])

        hidden = hidden_of(*chunks[0])
        for index, (member, at) in enumerate(chunks):
            after = hidden_of(*chunks[index + 1]) if index + 1 < len(chunks) else None
            span = slice(at, at + HALO)
            normalized, inverse = normalize(hidden)
            normalized_ref[member, span] = normalized.astype(BF16)
            inverse_ref[member, span] = jnp.broadcast_to(inverse, (HALO, inverse_ref.shape[2]))
            normed_out = (normalized + noise_ref[member : member + 1].astype(F32)).astype(BF16)
            normed_out_ref[member, span] = normed_out
            predicted_ref[member, :, span] = nt_dot(padded_ref[...], normed_out).astype(BF16)
            for source, target in ((normalized_ref, normalized_hbm), (normed_out_ref, normed_out_hbm)):
                copy = pltpu.make_async_copy(
                    source.at[member, span], target.at[member, span], out_sem.at[len(copies)]
                )
                copy.start()
                copies.append(copy)
            hidden = after
        for copy in copies:
            copy.wait()


def far(place, q, o, lse, after, before, w_qkv, noise, dec, latent, w_out):
    members, rows, width = latent.shape
    tall = members * rows
    fields = dec.shape[0]
    padded = -(-fields // FIELD_TILE) * FIELD_TILE
    steps = width // STEP_COLS
    block = pl.BlockSpec((tall, STEP_COLS), lambda s: (0, s))
    whole2 = lambda s: (0, 0)
    whole3 = lambda s: (0, 0, 0)
    anywhere = pl.BlockSpec(memory_space=pltpu.HBM)
    return pl.pallas_call(
        far_body,
        grid=(steps,),
        in_specs=[
            *[pl.BlockSpec(memory_space=pltpu.SMEM)] * 3,
            block,
            block,
            block,
            pl.BlockSpec(memory_space=pltpu.VMEM),
            pl.BlockSpec(memory_space=pltpu.VMEM),
            pl.BlockSpec((width, STEP_COLS), lambda s: (0, steps + s)),
            pl.BlockSpec((width, STEP_COLS), lambda s: (0, 2 * steps + s)),
            pl.BlockSpec((members, width), whole2),
            pl.BlockSpec((fields, width), whole2),
            anywhere,
            anywhere,
        ],
        out_specs=[
            anywhere,
            pl.BlockSpec((members, rows, 128), whole3),
            anywhere,
            pl.BlockSpec((members, padded, rows), whole3),
            pl.BlockSpec((padded, width), whole2),
        ],
        out_shape=[
            jax.ShapeDtypeStruct((members, rows, width), BF16),
            jax.ShapeDtypeStruct((members, rows, 128), F32),
            jax.ShapeDtypeStruct((members, rows, width), BF16),
            jax.ShapeDtypeStruct((members, padded, rows), BF16),
            jax.ShapeDtypeStruct((padded, width), BF16),
        ],
        scratch_shapes=[
            pltpu.VMEM((members * 2 * HALO, width), BF16),
            pltpu.VMEM((2, HALO, HALO), F32),
            pltpu.VMEM((members * 2 * HALO, STEP_COLS), BF16),
            pltpu.VMEM((STEP_COLS // PAIR, members * 2, 2 * HALO, 2 * PAIR), BF16),
            pltpu.VMEM((tall, width), BF16),
            pltpu.VMEM((members, rows, width), BF16),
            pltpu.VMEM((width, width), BF16),
            pltpu.VMEM((members, rows, width), BF16),
            pltpu.VMEM((members, rows, width), BF16),
            pltpu.SemaphoreType.DMA((2,)),
            pltpu.SemaphoreType.DMA((2 * members * rows // HALO,)),
        ],
        compiler_params=pltpu.CompilerParams(vmem_limit_bytes=51 * MIB),
        cost_estimate=pl.CostEstimate(
            flops=15 * 10**9, bytes_accessed=22 * MIB, transcendentals=10**7
        ),
        name="far",
    )(*place, q, o, lse, after, before, w_qkv, w_qkv, noise, dec, latent, w_out)


def crps_body(
    place_ref, count_ref, pred_ref, target_ref, fw_ref, aw_ref, normed_hbm, grad_ref, pieces_ref, normed_ref, padded_ref, sem
):
    fetch = pltpu.make_async_copy(normed_hbm, normed_ref, sem)
    fetch.start()
    bands = count_ref.shape[0]
    first = lax.div(place_ref[0], bands)
    count = count_ref[lax.rem(place_ref[0], bands)]
    ensemble = pred_ref.shape[0] * pred_ref.shape[1]
    own_count = pred_ref.shape[1]
    lead = 1.0 / (ensemble - 1)
    fields, rows = padded_ref.shape
    real = target_ref.shape[0]
    padded_ref[...] = jnp.zeros_like(padded_ref)
    padded_ref[:real] = target_ref[...]
    width = normed_ref.shape[-1]
    target = padded_ref[...]
    used = lax.broadcasted_iota(jnp.int32, (1, rows), 1) < count
    shape = (fields, real)
    diagonal = iota(shape, 0) == iota(shape, 1)
    field_weight = jnp.sum(jnp.where(diagonal, fw_ref[...], 0.0), axis=1, keepdims=True)
    scale = field_weight * jnp.where(used, aw_ref[...], 0.0)

    def slope(gap):
        square = gap * gap + smooth_width * smooth_width
        root = lax.rsqrt(square)
        return gap * root, square * root

    loss = jnp.zeros((fields, rows), F32)
    grads = []
    for own in range(own_count):
        mine = pred_ref[first, own].astype(F32)
        pair_slope = jnp.zeros((fields, rows), F32)
        pair_abs = jnp.zeros((fields, rows), F32)
        for other in range(ensemble):
            s, a = slope(mine - pred_ref[other // own_count, other % own_count].astype(F32))
            pair_slope = pair_slope + s
            pair_abs = pair_abs + a
        s, a = slope(mine - target)
        grad = (scale * (s - pair_slope * lead)).astype(BF16)
        grad_ref[own] = grad
        loss = loss + scale * (a - pair_abs * (0.5 * lead))
        grads.append(grad)
    fetch.wait()
    weight = nn_dot(grads[0], normed_ref[0])
    for own in range(1, own_count):
        weight = weight + nn_dot(grads[own], normed_ref[own])
    tiles = width // 128
    for r in range(0, fields, 8):
        for c in range(tiles):
            piece = weight[r : r + 8, c * 128 : c * 128 + 128]
            pieces_ref[r // 8 * tiles + c] = piece.astype(BF16)
    used_pieces = LOSS_PIECE
    whole = jnp.sum(jnp.sum(loss, axis=0, keepdims=True), axis=1, keepdims=True)
    high = whole.astype(BF16)
    rest = (whole - high.astype(F32)).astype(BF16)
    row = lax.broadcasted_iota(jnp.int32, (8, 128), 0)
    both = jnp.where(row == 0, high.astype(F32), jnp.where(row == 1, rest.astype(F32), 0.0))
    pieces_ref[used_pieces] = both.astype(BF16)
    pieces_ref[used_pieces + 1 :] = jnp.zeros_like(pieces_ref[used_pieces + 1 :])


def crps(place, preds, targets, field_weight, area_weight, normed_out, peers):
    _, own_count, fields, rows = preds.shape
    vmem = pl.BlockSpec(memory_space=pltpu.VMEM)
    return pl.pallas_call(
        crps_body,
        in_specs=[pl.BlockSpec(memory_space=pltpu.SMEM)] * 2
        + [vmem] * 4
        + [pl.BlockSpec(memory_space=pltpu.HBM)],
        out_specs=[vmem] * 2,
        out_shape=[
            jax.ShapeDtypeStruct((own_count, fields, rows), BF16),
            jax.ShapeDtypeStruct((peers, 8, 128), BF16),
        ],
        scratch_shapes=[
            pltpu.VMEM(normed_out.shape, BF16),
            pltpu.VMEM((fields, rows), F32),
            pltpu.SemaphoreType.DMA(()),
        ],
        compiler_params=pltpu.CompilerParams(vmem_limit_bytes=52 * MIB),
        cost_estimate=pl.CostEstimate(
            flops=4 * 10**8, bytes_accessed=4 * MIB, transcendentals=10**6
        ),
        name="crps",
    )(*place[:2], preds, targets, field_weight, area_weight, normed_out)


def backward_body(grad_ref, dec_ref, normalized_ref, inverse_ref, out_ref):
    grad_norm = tn_dot(grad_ref[...], dec_ref[...])
    normalized = normalized_ref[...].astype(F32)
    inverse = inverse_ref[...][:, :1]
    mean = jnp.mean(grad_norm, axis=-1, keepdims=True)
    dotted = jnp.mean(grad_norm * normalized, axis=-1, keepdims=True)
    out_ref[...] = (inverse * (grad_norm - mean - normalized * dotted)).astype(BF16)


def backward(grad, dec, normalized, inverse):
    members, fields, rows = grad.shape
    width = dec.shape[1]
    return pl.pallas_call(
        backward_body,
        grid=(members,),
        in_specs=[
            pl.BlockSpec((None, fields, rows), lambda m: (m, 0, 0)),
            pl.BlockSpec((fields, width), lambda m: (0, 0)),
            pl.BlockSpec((None, rows, width), lambda m: (m, 0, 0)),
            pl.BlockSpec((None, rows, 128), lambda m: (m, 0, 0)),
        ],
        out_specs=pl.BlockSpec((None, rows, width), lambda m: (m, 0, 0)),
        out_shape=jax.ShapeDtypeStruct((members, rows, width), BF16),
        compiler_params=pltpu.CompilerParams(vmem_limit_bytes=32 * MIB),
        cost_estimate=pl.CostEstimate(
            flops=5 * 10**8, bytes_accessed=5 * MIB, transcendentals=0
        ),
        name="backward",
    )(grad, dec, normalized, inverse)


def share_body(rank_ref, parts_ref, spread_ref):
    peers = parts_ref.shape[0]
    mine = jnp.sum(parts_ref[...].astype(F32), axis=0)
    row = iota(mine.shape, 0)
    loss = jnp.sum(jnp.where(row < 2, mine, 0.0), axis=0, keepdims=True)
    rounded = loss.astype(BF16).astype(F32)
    as_loss = jnp.where(row == 0, rounded, jnp.where(row == 1, loss - rounded, 0.0))
    mine = jnp.where(rank_ref[0] == LOSS_PIECE, as_loss, mine).astype(BF16)
    spread_ref[...] = jnp.broadcast_to(mine[None], spread_ref.shape)


def finish_body(pieces_ref, weight_ref, loss_ref, *, tokens):
    fields, width = weight_ref.shape
    tiles = width // 128
    for r in range(0, fields, 8):
        count = min(8, fields - r)
        for c in range(tiles):
            piece = pieces_ref[r // 8 * tiles + c].astype(F32) * (1.0 / tokens)
            weight_ref[r : r + count, c * 128 : c * 128 + 128] = piece[:count]
    loss = jnp.sum(pieces_ref[LOSS_PIECE].astype(F32), axis=0, keepdims=True) * (1.0 / tokens)
    loss_ref[0, 0] = jnp.max(loss)


def summed(place, pieces, fields, width, tokens):
    axes = ("mem", "lat")
    vmem = pl.BlockSpec(memory_space=pltpu.VMEM)
    smem = pl.BlockSpec(memory_space=pltpu.SMEM)
    params = pltpu.CompilerParams(vmem_limit_bytes=16 * MIB)
    parts = lax.all_to_all(pieces, axes, split_axis=0, concat_axis=0, tiled=True)
    spread = pl.pallas_call(
        share_body,
        in_specs=[smem, vmem],
        out_specs=vmem,
        out_shape=jax.ShapeDtypeStruct(pieces.shape, BF16),
        compiler_params=params,
        name="share",
    )(place[0], parts)
    whole = lax.all_to_all(spread, axes, split_axis=0, concat_axis=0, tiled=True)
    return pl.pallas_call(
        functools.partial(finish_body, tokens=tokens),
        in_specs=[vmem],
        out_specs=[vmem, smem],
        out_shape=[
            jax.ShapeDtypeStruct((fields, width), F32),
            jax.ShapeDtypeStruct((1, 1), F32),
        ],
        compiler_params=params,
        name="finish",
    )(whole)


def local(
    latent,
    member_noise,
    w_qkv,
    w_out,
    dec_weight,
    targets,
    area_weight,
    field_weight,
    band_count,
    band_window,
):
    members, rows, width = latent.shape
    bands = lax.axis_size("lat")
    fields = dec_weight.shape[0]
    up = [(i, i + 1) for i in range(bands - 1)]
    down = [(j, i) for i, j in up]
    before = lax.ppermute(latent[:, rows - HALO :], "lat", up)
    after = lax.ppermute(latent[:, :HALO], "lat", down)
    place = (lax.axis_index(("mem", "lat")).reshape(1), band_count, band_window)
    q, o, lse = near(place, latent, w_qkv)
    normalized, inverse, normed_out, predicted, dec = far(
        place, q, o, lse, after, before, w_qkv, member_noise, dec_weight, latent, w_out
    )
    preds = lax.all_gather(predicted, "mem", axis=0)
    peers = lax.axis_size("mem") * bands
    grad, pieces = crps(
        place, preds, targets, field_weight[None, :], area_weight[None, :], normed_out, peers
    )
    weight, loss = summed(place, pieces, fields, width, rows * bands)
    grad_hidden = backward(grad, dec, normalized, inverse)
    return grad_hidden, weight, loss.reshape(())


def solution(mesh):
    return jax.shard_map(
        local,
        mesh=mesh,
        in_specs=(
            P("mem", "lat", None),
            P("mem", None),
            P(),
            P(),
            P(),
            P(None, "lat"),
            P("lat"),
            P(),
            P(),
            P("lat", None),
        ),
        out_specs=(P("mem", "lat", None), P(), P()),
        check_vma=False,
    )
```

```python
import functools

import jax
import jax.numpy as jnp
from jax import lax
from jax.experimental import pallas as pl
from jax.experimental.pallas import tpu as pltpu
from jax.sharding import PartitionSpec as P

HEAD_DIM = 64
HALO = 256
LOG2E = 1.4426950408889634

norm_eps = 1e-05
smooth_width = 0.25
F32 = jnp.float32
BF16 = jnp.bfloat16
MIB = 1024 * 1024


def normalize(x):
    mean = jnp.mean(x, axis=-1, keepdims=True)
    centred = x - mean
    var = jnp.mean(centred * centred, axis=-1, keepdims=True)
    inverse = lax.rsqrt(var + norm_eps)
    return centred * inverse, inverse


def nt_dot(a, b):
    return lax.dot_general(a, b, (((1,), (1,)), ((), ())), preferred_element_type=F32)


def tn_dot(a, b):
    return lax.dot_general(a, b, (((0,), (0,)), ((), ())), preferred_element_type=F32)


def nn_dot(a, b):
    return jnp.dot(a, b, preferred_element_type=F32)


QB = 256
STEP_COLS = 256
PAIR = 2 * HEAD_DIM
FIELD_TILE = 8
LOSS_PIECE = 104
NEVER = -1e30


def bias_of(q_row, k_row, place_ref, count_ref, window_ref, rows):
    bands = count_ref.shape[0]
    band = lax.rem(place_ref[0], bands)
    offset = k_row - q_row
    in_window = (offset >= -window_ref[0, 0]) & (offset <= window_ref[0, 1])
    before = jnp.where(band > 0, count_ref[jnp.maximum(band - 1, 0)], 0)
    after = jnp.where(band < bands - 1, count_ref[jnp.minimum(band + 1, bands - 1)], 0)
    end = jnp.where(
        k_row < 0, before - rows, jnp.where(k_row < rows, count_ref[band], after + rows)
    )
    return jnp.where((in_window & (k_row < end)) | (offset == 0), 0.0, NEVER)


def iota(shape, axis):
    return lax.broadcasted_iota(jnp.int32, shape, axis)


def pair_scores(q, keys, bias, low):
    zero = jnp.zeros_like(q)
    both = jnp.concatenate([jnp.where(low, q, zero), jnp.where(low, zero, q)], axis=0)
    scores = nt_dot(both, keys)
    weights, tops = [], []
    for half in range(2):
        part = scores[half * q.shape[0] : (half + 1) * q.shape[0]] + bias
        top = jnp.max(part, axis=-1, keepdims=True)
        weights.append(jnp.exp2(part - top).astype(BF16))
        tops.append(top)
    return jnp.concatenate(weights, axis=1), jnp.where(low, tops[0], tops[1])


def set_ones(ref, low):
    half = ref.shape[-2] // 2
    one = jnp.ones((half, PAIR), BF16)
    for pair in range(ref.shape[0]):
        for group in range(ref.shape[1]):
            ref[pair, group, :half, PAIR:] = jnp.where(low, one, 0.0).astype(BF16)
            ref[pair, group, half:, PAIR:] = jnp.where(low, 0.0, one).astype(BF16)


def set_values(ref, group, at, value, low):
    half, count = ref.shape[-2] // 2, value.shape[0]
    for pair in range(ref.shape[0]):
        own = value[:, pair * PAIR : (pair + 1) * PAIR]
        zero = jnp.zeros_like(own)
        ref[pair, group, at : at + count, :PAIR] = jnp.where(low, own, zero)
        ref[pair, group, half + at : half + at + count, :PAIR] = jnp.where(low, zero, own)


def near_body(
    place_ref, count_ref, window_ref, latent_ref, wq_ref, wk_ref, wv_ref, q_ref, o_ref, lse_ref, normed_ref, bias_ref, k_ref, vx_ref
):
    step = pl.program_id(0)
    rows = bias_ref.shape[0]
    members = latent_ref.shape[0] // rows
    low = iota((1, PAIR), 1) < HEAD_DIM

    @pl.when(step == 0)
    def _():
        normed_ref[...] = normalize(latent_ref[...].astype(F32))[0].astype(BF16)
        shape = bias_ref.shape
        bias_ref[...] = bias_of(iota(shape, 0), iota(shape, 1), place_ref, count_ref, window_ref, rows)
        set_ones(vx_ref, low)


    def queries(at):
        span = slice(at, at + QB)
        q_ref[span] = (
            nn_dot(normed_ref[span], wq_ref[...]) * (HEAD_DIM ** (-0.5) * LOG2E)
        ).astype(BF16)

    def keys(at):
        span = slice(at, at + QB)
        k_ref[span] = nn_dot(normed_ref[span], wk_ref[...]).astype(BF16)

    def values(at):
        span = slice(at, at + QB)
        value = nn_dot(normed_ref[span], wv_ref[...]).astype(BF16)
        set_values(vx_ref, at // rows, at % rows, value, low)

    def attend(member, pair, block):
        cols = slice(pair * PAIR, (pair + 1) * PAIR)
        here = slice(block * QB, (block + 1) * QB)
        mine = slice(member * rows + block * QB, member * rows + (block + 1) * QB)
        reach = slice(member * rows, (member + 1) * rows)
        weight, top = pair_scores(q_ref[mine, cols], k_ref[reach, cols], bias_ref[here], low)
        total = nn_dot(weight, vx_ref[pair, member])
        summed_weight = total[:, PAIR:]
        o_ref[mine, cols] = (total[:, :PAIR] / summed_weight).astype(BF16)
        lse_ref[mine, cols] = top + jnp.log2(summed_weight)

    pairs, blocks = STEP_COLS // PAIR, rows // QB
    project = [
        [(f, member * rows + at) for f in (keys, values, queries) for at in range(0, rows, QB)]
        for member in range(members)
    ]
    for f, at in project[0]:
        f(at)
    for member in range(members):
        later = project[member + 1] if member + 1 < members else []
        tiles = [(pair, block) for pair in range(pairs) for block in range(blocks)]
        share = -(-len(later) // len(tiles))
        for i, (pair, block) in enumerate(tiles):
            for f, at in later[i * share : (i + 1) * share]:
                f(at)
            attend(member, pair, block)


def near(place, latent, w_qkv):
    members, rows, width = latent.shape
    tall = members * rows
    steps = width // STEP_COLS
    block = pl.BlockSpec((tall, STEP_COLS), lambda s: (0, s))
    return pl.pallas_call(
        near_body,
        grid=(steps,),
        in_specs=[
            *[pl.BlockSpec(memory_space=pltpu.SMEM)] * 3,
            pl.BlockSpec((tall, width), lambda s: (0, 0), pipeline_mode=pl.Buffered(1)),
            pl.BlockSpec((width, STEP_COLS), lambda s: (0, s)),
            pl.BlockSpec((width, STEP_COLS), lambda s: (0, steps + s)),
            pl.BlockSpec((width, STEP_COLS), lambda s: (0, 2 * steps + s)),
        ],
        out_specs=[block, block, block],
        out_shape=[
            jax.ShapeDtypeStruct((tall, width), BF16),
            jax.ShapeDtypeStruct((tall, width), BF16),
            jax.ShapeDtypeStruct((tall, width), F32),
        ],
        scratch_shapes=[
            pltpu.VMEM((tall, width), BF16),
            pltpu.VMEM((rows, rows), F32),
            pltpu.VMEM((tall, STEP_COLS), BF16),
            pltpu.VMEM((STEP_COLS // PAIR, members, 2 * rows, 2 * PAIR), BF16),
        ],
        compiler_params=pltpu.CompilerParams(vmem_limit_bytes=57 * MIB),
        cost_estimate=pl.CostEstimate(
            flops=20 * 10**9, bytes_accessed=16 * MIB, transcendentals=10**7
        ),
        name="near",
    )(*place, latent.reshape(tall, width), w_qkv, w_qkv, w_qkv)


def far_body(
    place_ref,
    count_ref,
    window_ref,
    q_ref,
    o_ref,
    lse_ref,
    after_ref,
    before_ref,
    wk_ref,
    wv_ref,
    noise_ref,
    dec_ref,
    latent_hbm,
    wout_hbm,
    normalized_hbm,
    inverse_ref,
    normed_out_hbm,
    predicted_ref,
    padded_ref,
    halo_ref,
    bias_ref,
    k_ref,
    vx_ref,
    att_ref,
    latent_ref,
    wout_ref,
    normalized_ref,
    normed_out_ref,
    sem,
    out_sem,
):
    step = pl.program_id(0)
    members, _, width = before_ref.shape
    tall = q_ref.shape[0]
    rows = tall // members
    low = iota((1, PAIR), 1) < HEAD_DIM
    late = [
        pltpu.make_async_copy(latent_hbm, latent_ref, sem.at[0]),
        pltpu.make_async_copy(wout_hbm, wout_ref, sem.at[1]),
    ]

    @pl.when(step == 0)
    def _():
        for copy in late:
            copy.start()
        padded_ref[...] = jnp.zeros_like(padded_ref)
        padded_ref[: dec_ref.shape[0]] = dec_ref[...]
        for member in range(members):
            for side, source in enumerate((before_ref, after_ref)):
                at = (2 * member + side) * HALO
                halo_ref[at : at + HALO] = normalize(source[member].astype(F32))[0].astype(BF16)
        shape = (HALO, HALO)
        bias_ref[0] = bias_of(iota(shape, 0), iota(shape, 1) - HALO, place_ref, count_ref, window_ref, rows)
        bias_ref[1] = bias_of(iota(shape, 0) + rows - HALO, iota(shape, 1) + rows, place_ref, count_ref, window_ref, rows)
        set_ones(vx_ref, low)

    def keys(at):
        span = slice(at, at + HALO)
        k_ref[span] = nn_dot(halo_ref[span], wk_ref[...]).astype(BF16)

    def values(at):
        span = slice(at, at + HALO)
        value = nn_dot(halo_ref[span], wv_ref[...]).astype(BF16)
        set_values(vx_ref, at // HALO, 0, value, low)

    def attend(member, pair, side):
        cols = slice(pair * PAIR, (pair + 1) * PAIR)
        out_cols = pl.ds(pl.multiple_of(step * STEP_COLS + pair * PAIR, PAIR), PAIR)
        at = member * rows + side * (rows - HALO)
        mine = slice(at, at + HALO)
        reach = slice((2 * member + side) * HALO, (2 * member + side + 1) * HALO)
        lse = lse_ref[mine, cols]
        weight, far_top = pair_scores(q_ref[mine, cols], k_ref[reach, cols], bias_ref[side], low)
        total = nn_dot(weight, vx_ref[pair, 2 * member + side])
        top = jnp.maximum(lse, far_top)
        near_share, far_share = jnp.exp2(lse - top), jnp.exp2(far_top - top)
        att_ref[mine, out_cols] = (
            (near_share * o_ref[mine, cols].astype(F32) + far_share * total[:, :PAIR])
            / (near_share + far_share * total[:, PAIR:])
        ).astype(BF16)

    groups = [(member, side) for member in range(members) for side in range(2)]

    def project(group):
        keys(group * HALO)
        values(group * HALO)

    project(0)
    for group, (member, side) in enumerate(groups):
        if group + 1 < len(groups):
            project(group + 1)
        for pair in range(STEP_COLS // PAIR):
            attend(member, pair, side)

    @pl.when(step == pl.num_programs(0) - 1)
    def _():
        for copy in late:
            copy.wait()
        copies = []
        chunks = [(member, at) for member in range(members) for at in range(0, rows, HALO)]

        def hidden_of(member, at):
            attended = att_ref[member * rows + at : member * rows + at + HALO]
            return latent_ref[member, at : at + HALO].astype(F32) + nn_dot(attended, wout_ref[...])

        hidden = hidden_of(*chunks[0])
        for index, (member, at) in enumerate(chunks):
            after = hidden_of(*chunks[index + 1]) if index + 1 < len(chunks) else None
            span = slice(at, at + HALO)
            normalized, inverse = normalize(hidden)
            normalized_ref[member, span] = normalized.astype(BF16)
            inverse_ref[member, span] = jnp.broadcast_to(inverse, (HALO, inverse_ref.shape[2]))
            normed_out = (normalized + noise_ref[member : member + 1].astype(F32)).astype(BF16)
            normed_out_ref[member, span] = normed_out
            predicted_ref[member, :, span] = nt_dot(padded_ref[...], normed_out).astype(BF16)
            for source, target in ((normalized_ref, normalized_hbm), (normed_out_ref, normed_out_hbm)):
                copy = pltpu.make_async_copy(
                    source.at[member, span], target.at[member, span], out_sem.at[len(copies)]
                )
                copy.start()
                copies.append(copy)
            hidden = after
        for copy in copies:
            copy.wait()


def far(place, q, o, lse, after, before, w_qkv, noise, dec, latent, w_out):
    members, rows, width = latent.shape
    tall = members * rows
    fields = dec.shape[0]
    padded = -(-fields // FIELD_TILE) * FIELD_TILE
    steps = width // STEP_COLS
    block = pl.BlockSpec((tall, STEP_COLS), lambda s: (0, s))
    whole2 = lambda s: (0, 0)
    whole3 = lambda s: (0, 0, 0)
    anywhere = pl.BlockSpec(memory_space=pltpu.HBM)
    return pl.pallas_call(
        far_body,
        grid=(steps,),
        in_specs=[
            *[pl.BlockSpec(memory_space=pltpu.SMEM)] * 3,
            block,
            block,
            block,
            pl.BlockSpec(memory_space=pltpu.VMEM),
            pl.BlockSpec(memory_space=pltpu.VMEM),
            pl.BlockSpec((width, STEP_COLS), lambda s: (0, steps + s)),
            pl.BlockSpec((width, STEP_COLS), lambda s: (0, 2 * steps + s)),
            pl.BlockSpec((members, width), whole2),
            pl.BlockSpec((fields, width), whole2),
            anywhere,
            anywhere,
        ],
        out_specs=[
            anywhere,
            pl.BlockSpec((members, rows, 128), whole3),
            anywhere,
            pl.BlockSpec((members, padded, rows), whole3),
            pl.BlockSpec((padded, width), whole2),
        ],
        out_shape=[
            jax.ShapeDtypeStruct((members, rows, width), BF16),
            jax.ShapeDtypeStruct((members, rows, 128), F32),
            jax.ShapeDtypeStruct((members, rows, width), BF16),
            jax.ShapeDtypeStruct((members, padded, rows), BF16),
            jax.ShapeDtypeStruct((padded, width), BF16),
        ],
        scratch_shapes=[
            pltpu.VMEM((members * 2 * HALO, width), BF16),
            pltpu.VMEM((2, HALO, HALO), F32),
            pltpu.VMEM((members * 2 * HALO, STEP_COLS), BF16),
            pltpu.VMEM((STEP_COLS // PAIR, members * 2, 2 * HALO, 2 * PAIR), BF16),
            pltpu.VMEM((tall, width), BF16),
            pltpu.VMEM((members, rows, width), BF16),
            pltpu.VMEM((width, width), BF16),
            pltpu.VMEM((members, rows, width), BF16),
            pltpu.VMEM((members, rows, width), BF16),
            pltpu.SemaphoreType.DMA((2,)),
            pltpu.SemaphoreType.DMA((2 * members * rows // HALO,)),
        ],
        compiler_params=pltpu.CompilerParams(vmem_limit_bytes=51 * MIB),
        cost_estimate=pl.CostEstimate(
            flops=15 * 10**9, bytes_accessed=22 * MIB, transcendentals=10**7
        ),
        name="far",
    )(*place, q, o, lse, after, before, w_qkv, w_qkv, noise, dec, latent, w_out)


def crps_body(
    place_ref, count_ref, pred_ref, target_ref, fw_ref, aw_ref, normed_hbm, grad_ref, pieces_ref, normed_ref, padded_ref, sem
):
    fetch = pltpu.make_async_copy(normed_hbm, normed_ref, sem)
    fetch.start()
    bands = count_ref.shape[0]
    first = lax.div(place_ref[0], bands)
    count = count_ref[lax.rem(place_ref[0], bands)]
    ensemble = pred_ref.shape[0] * pred_ref.shape[1]
    own_count = pred_ref.shape[1]
    lead = 1.0 / (ensemble - 1)
    fields, rows = padded_ref.shape
    real = target_ref.shape[0]
    padded_ref[...] = jnp.zeros_like(padded_ref)
    padded_ref[:real] = target_ref[...]
    width = normed_ref.shape[-1]
    target = padded_ref[...]
    used = lax.broadcasted_iota(jnp.int32, (1, rows), 1) < count
    shape = (fields, real)
    diagonal = iota(shape, 0) == iota(shape, 1)
    field_weight = jnp.sum(jnp.where(diagonal, fw_ref[...], 0.0), axis=1, keepdims=True)
    scale = field_weight * jnp.where(used, aw_ref[...], 0.0)

    def slope(gap):
        square = gap * gap + smooth_width * smooth_width
        root = lax.rsqrt(square)
        return gap * root, square * root

    loss = jnp.zeros((fields, rows), F32)
    grads = []
    for own in range(own_count):
        mine = pred_ref[first, own].astype(F32)
        pair_slope = jnp.zeros((fields, rows), F32)
        pair_abs = jnp.zeros((fields, rows), F32)
        for other in range(ensemble):
            s, a = slope(mine - pred_ref[other // own_count, other % own_count].astype(F32))
            pair_slope = pair_slope + s
            pair_abs = pair_abs + a
        s, a = slope(mine - target)
        grad = (scale * (s - pair_slope * lead)).astype(BF16)
        grad_ref[own] = grad
        loss = loss + scale * (a - pair_abs * (0.5 * lead))
        grads.append(grad)
    fetch.wait()
    weight = nn_dot(grads[0], normed_ref[0])
    for own in range(1, own_count):
        weight = weight + nn_dot(grads[own], normed_ref[own])
    tiles = width // 128
    for r in range(0, fields, 8):
        for c in range(tiles):
            piece = weight[r : r + 8, c * 128 : c * 128 + 128]
            pieces_ref[r // 8 * tiles + c] = piece.astype(BF16)
    used_pieces = LOSS_PIECE
    whole = jnp.sum(jnp.sum(loss, axis=0, keepdims=True), axis=1, keepdims=True)
    high = whole.astype(BF16)
    rest = (whole - high.astype(F32)).astype(BF16)
    row = lax.broadcasted_iota(jnp.int32, (8, 128), 0)
    both = jnp.where(row == 0, high.astype(F32), jnp.where(row == 1, rest.astype(F32), 0.0))
    pieces_ref[used_pieces] = both.astype(BF16)
    pieces_ref[used_pieces + 1 :] = jnp.zeros_like(pieces_ref[used_pieces + 1 :])


def crps(place, preds, targets, field_weight, area_weight, normed_out, peers):
    _, own_count, fields, rows = preds.shape
    vmem = pl.BlockSpec(memory_space=pltpu.VMEM)
    return pl.pallas_call(
        crps_body,
        in_specs=[pl.BlockSpec(memory_space=pltpu.SMEM)] * 2
        + [vmem] * 4
        + [pl.BlockSpec(memory_space=pltpu.HBM)],
        out_specs=[vmem] * 2,
        out_shape=[
            jax.ShapeDtypeStruct((own_count, fields, rows), BF16),
            jax.ShapeDtypeStruct((peers, 8, 128), BF16),
        ],
        scratch_shapes=[
            pltpu.VMEM(normed_out.shape, BF16),
            pltpu.VMEM((fields, rows), F32),
            pltpu.SemaphoreType.DMA(()),
        ],
        compiler_params=pltpu.CompilerParams(vmem_limit_bytes=52 * MIB),
        cost_estimate=pl.CostEstimate(
            flops=4 * 10**8, bytes_accessed=4 * MIB, transcendentals=10**6
        ),
        name="crps",
    )(*place[:2], preds, targets, field_weight, area_weight, normed_out)


def backward_body(grad_ref, dec_ref, normalized_ref, inverse_ref, out_ref):
    grad_norm = tn_dot(grad_ref[...], dec_ref[...])
    normalized = normalized_ref[...].astype(F32)
    inverse = inverse_ref[...][:, :1]
    mean = jnp.mean(grad_norm, axis=-1, keepdims=True)
    dotted = jnp.mean(grad_norm * normalized, axis=-1, keepdims=True)
    out_ref[...] = (inverse * (grad_norm - mean - normalized * dotted)).astype(BF16)


def backward(grad, dec, normalized, inverse):
    members, fields, rows = grad.shape
    width = dec.shape[1]
    return pl.pallas_call(
        backward_body,
        grid=(members,),
        in_specs=[
            pl.BlockSpec((None, fields, rows), lambda m: (m, 0, 0)),
            pl.BlockSpec((fields, width), lambda m: (0, 0)),
            pl.BlockSpec((None, rows, width), lambda m: (m, 0, 0)),
            pl.BlockSpec((None, rows, 128), lambda m: (m, 0, 0)),
        ],
        out_specs=pl.BlockSpec((None, rows, width), lambda m: (m, 0, 0)),
        out_shape=jax.ShapeDtypeStruct((members, rows, width), BF16),
        compiler_params=pltpu.CompilerParams(vmem_limit_bytes=32 * MIB),
        cost_estimate=pl.CostEstimate(
            flops=5 * 10**8, bytes_accessed=5 * MIB, transcendentals=0
        ),
        name="backward",
    )(grad, dec, normalized, inverse)


def share_body(rank_ref, parts_ref, spread_ref):
    peers = parts_ref.shape[0]
    mine = jnp.sum(parts_ref[...].astype(F32), axis=0)
    row = iota(mine.shape, 0)
    loss = jnp.sum(jnp.where(row < 2, mine, 0.0), axis=0, keepdims=True)
    rounded = loss.astype(BF16).astype(F32)
    as_loss = jnp.where(row == 0, rounded, jnp.where(row == 1, loss - rounded, 0.0))
    mine = jnp.where(rank_ref[0] == LOSS_PIECE, as_loss, mine).astype(BF16)
    spread_ref[...] = jnp.broadcast_to(mine[None], spread_ref.shape)


def finish_body(pieces_ref, weight_ref, loss_ref, *, tokens):
    fields, width = weight_ref.shape
    tiles = width // 128
    for r in range(0, fields, 8):
        count = min(8, fields - r)
        for c in range(tiles):
            piece = pieces_ref[r // 8 * tiles + c].astype(F32) * (1.0 / tokens)
            weight_ref[r : r + count, c * 128 : c * 128 + 128] = piece[:count]
    loss = jnp.sum(pieces_ref[LOSS_PIECE].astype(F32), axis=0, keepdims=True) * (1.0 / tokens)
    loss_ref[0, 0] = jnp.max(loss)


def summed(place, pieces, fields, width, tokens):
    axes = ("mem", "lat")
    vmem = pl.BlockSpec(memory_space=pltpu.VMEM)
    smem = pl.BlockSpec(memory_space=pltpu.SMEM)
    params = pltpu.CompilerParams(vmem_limit_bytes=16 * MIB)
    parts = lax.all_to_all(pieces, axes, split_axis=0, concat_axis=0, tiled=True)
    spread = pl.pallas_call(
        share_body,
        in_specs=[smem, vmem],
        out_specs=vmem,
        out_shape=jax.ShapeDtypeStruct(pieces.shape, BF16),
        compiler_params=params,
        name="share",
    )(place[0], parts)
    whole = lax.all_to_all(spread, axes, split_axis=0, concat_axis=0, tiled=True)
    return pl.pallas_call(
        functools.partial(finish_body, tokens=tokens),
        in_specs=[vmem],
        out_specs=[vmem, smem],
        out_shape=[
            jax.ShapeDtypeStruct((fields, width), F32),
            jax.ShapeDtypeStruct((1, 1), F32),
        ],
        compiler_params=params,
        name="finish",
    )(whole)


def local(
    latent,
    member_noise,
    w_qkv,
    w_out,
    dec_weight,
    targets,
    area_weight,
    field_weight,
    band_count,
    band_window,
):
    members, rows, width = latent.shape
    bands = lax.axis_size("lat")
    fields = dec_weight.shape[0]
    up = [(i, i + 1) for i in range(bands - 1)]
    down = [(j, i) for i, j in up]
    before = lax.ppermute(latent[:, rows - HALO :], "lat", up)
    after = lax.ppermute(latent[:, :HALO], "lat", down)
    place = (lax.axis_index(("mem", "lat")).reshape(1), band_count, band_window)
    q, o, lse = near(place, latent, w_qkv)
    normalized, inverse, normed_out, predicted, dec = far(
        place, q, o, lse, after, before, w_qkv, member_noise, dec_weight, latent, w_out
    )
    preds = lax.all_gather(predicted, "mem", axis=0)
    peers = lax.axis_size("mem") * bands
    grad, pieces = crps(
        place, preds, targets, field_weight[None, :], area_weight[None, :], normed_out, peers
    )
    weight, loss = summed(place, pieces, fields, width, rows * bands)
    grad_hidden = backward(grad, dec, normalized, inverse)
    return grad_hidden, weight, loss.reshape(())


def solution(mesh):
    return jax.shard_map(
        local,
        mesh=mesh,
        in_specs=(
            P("mem", "lat", None),
            P("mem", None),
            P(),
            P(),
            P(),
            P(None, "lat"),
            P("lat"),
            P(),
            P(),
            P("lat", None),
        ),
        out_specs=(P("mem", "lat", None), P(), P()),
        check_vma=False,
    )
```
